128 devices in a mesh: ha: 16 (over x_hi, z, core), wa: 8 (over y, x_lo).
Axes of the slice: x: 4 (x_hi: 2, x_lo: 2; x = x_hi * 2 + x_lo), y: 4, z: 4, core: 2. Of those that a mesh axis runs over, the one named last changes fastest.
Arguments:
- queries: bfloat16 [4, 192, 64, 1536], P(None, 'ha', 'wa'), may hold values from -5 to 5
- key_heads: bfloat16 [4, 192, 64, 1536], P(None, 'ha', 'wa'), may hold values from -5 to 5
- value_heads: bfloat16 [4, 192, 64, 1536], P(None, 'ha', 'wa'), may hold values from -6 to 6
- out_grad: bfloat16 [4, 192, 64, 1536], P(None, 'ha', 'wa'), may hold values from -6 to 6
- reach_tiles: int32 [48, 16, 4], P('ha', 'wa'), may hold values from 0 to 1
Outputs:
- attended: bfloat16 [4, 192, 64, 1536], P(None, 'ha', 'wa')
- query_grad: bfloat16 [4, 192, 64, 1536], P(None, 'ha', 'wa')
- key_grad: bfloat16 [4, 192, 64, 1536], P(None, 'ha', 'wa')
- value_grad: bfloat16 [4, 192, 64, 1536], P(None, 'ha', 'wa')
The draws below stay inside these ranges and needn't reach their ends.
All inputs are finite; a program needn't handle non-finite values.
Results may differ from the reference program's by a relative error of at most 0.03.
Values may be sent and summed in bfloat16 or wider, within the bound.
A program may use at most 192 MiB of HBM per device.

```python
import jax
import jax.numpy as jnp
from jax import lax

HEADS = 12
TS = 4
FR = 4
E = 1536
NH = 192
NW = 64
GTR = 48
GTC = 16


def draw_queries(key, part):
    key = jax.random.fold_in(key, 1)
    values = jnp.clip(jax.random.normal(key, (FR, NH, NW, E), jnp.float32), -4.8, 4.8)
    return values.astype(jnp.bfloat16)


def draw_key_heads(key, part):
    key = jax.random.fold_in(key, 2)
    values = jnp.clip(jax.random.normal(key, (FR, NH, NW, E), jnp.float32), -4.8, 4.8)
    return values.astype(jnp.bfloat16)


def set_ends(array, rng, smallest, largest):
    spot = [jax.random.randint(jax.random.fold_in(rng, axis), (), 0, length) for axis, length in enumerate(array.shape)]
    main_axis = array.shape.index(max(array.shape))
    beside = spot[:main_axis] + [(spot[main_axis] + 1) % array.shape[main_axis]] + spot[main_axis + 1:]
    return array.at[tuple(spot)].set(smallest).at[tuple(beside)].set(largest)


def shard_levels(own_key, shape, shards, least, top_value):
    def one(dim, shards_of):
        steps = jax.random.uniform(jax.random.fold_in(jax.random.fold_in(own_key, 6), dim), (shards_of,), jnp.float32, least / len(shards), top_value / len(shards))
        return jnp.repeat(jnp.exp(steps), shape[dim] // shards_of).reshape((-1,) + (1,) * (len(shape) - dim - 1))

    loudness = one(*shards[0])
    for cut in shards[1:]:
        loudness = loudness * one(*cut)
    return loudness


def gaussian(own_key, dims, scale, reach, cuts=(), kind=jnp.bfloat16):
    result = jax.random.normal(own_key, dims, jnp.float32) * scale
    if len(cuts) > 0:
        result = shard_levels(own_key, dims, cuts, -0.22, 0.18) * result
    return jnp.clip(result, min=-reach, max=reach).astype(kind)


def setup_inputs(seed: int = 0) -> dict:
    key_of = jax.random.split(jax.random.key(seed), 6)
    return {
        "queries": draw_queries(jax.random.fold_in(key_of[5], 71), 0),
        "key_heads": draw_key_heads(jax.random.fold_in(key_of[5], 71), 0),
        "value_heads": gaussian(key_of[2], (FR, NH, NW, E), 1.0, 6.0, ((1, 16), (2, 8))),
        "out_grad": gaussian(key_of[3], (FR, NH, NW, E), 1.0, 6.0, ((1, 16), (2, 8))),
        "reach_tiles": set_ends(jax.random.randint(key_of[4], (GTR, GTC, 4), 0, 2), jax.random.fold_in(key_of[4], 1), 0, 1).astype(jnp.int32),
    }


NEGATIVE = -1.0e30


def to_tiles(layout, tile_side):
    frame_count, _, grid_cols, channels = layout.shape
    blocks = layout.reshape(frame_count, tile_side, grid_cols // tile_side, tile_side, channels)
    blocks = blocks.transpose(2, 0, 1, 3, 4)
    return blocks.reshape(grid_cols // tile_side, frame_count * tile_side * tile_side, channels)


def from_tiles(blocks, frame_count, tile_side):
    tile_count, _, channels = blocks.shape
    layout = blocks.reshape(tile_count, frame_count, tile_side, tile_side, channels).transpose(1, 2, 0, 3, 4)
    return layout.reshape(frame_count, tile_side, tile_count * tile_side, channels)


def window(padded, tile_row, tile_side):
    grid_cols = padded.shape[2] - 2 * tile_side
    sections = []
    for shift_row in range(3):
        band_rows = lax.dynamic_slice_in_dim(padded, (tile_row + shift_row) * tile_side, tile_side, 1)
        for shift_col in range(3):
            sections.append(to_tiles(band_rows[:, :, shift_col * tile_side:shift_col * tile_side + grid_cols, :], tile_side))
    return jnp.concatenate(sections, axis=1)


def add_window(summed, blocks, tile_row, tile_side):
    frame_count = summed.shape[0]
    grid_cols = summed.shape[2] - 2 * tile_side
    per_tile = blocks.shape[1] // 9
    for shift_row in range(3):
        start_row = (tile_row + shift_row) * tile_side
        band_rows = lax.dynamic_slice_in_dim(summed, start_row, tile_side, 1)
        for shift_col in range(3):
            offset = shift_row * 3 + shift_col
            section = from_tiles(blocks[:, offset * per_tile:(offset + 1) * per_tile, :], frame_count, tile_side)
            band_rows = band_rows.at[:, :, shift_col * tile_side:shift_col * tile_side + grid_cols, :].add(section)
        summed = lax.dynamic_update_slice_in_dim(summed, band_rows, start_row, 1)
    return summed


def query_mask(reach_row, tile_row, col_start, row_total, col_total, per_tile):
    tile_count = reach_row.shape[0]
    offsets = jnp.arange(9, dtype=jnp.int32)
    down_step = offsets // 3 - 1
    side_step = offsets % 3 - 1
    col_ids = col_start + jnp.arange(tile_count, dtype=jnp.int32)
    target_row = tile_row + down_step
    target_col = col_ids[:, None] + side_step[None, :]
    allowed = (down_step[None, :] >= -reach_row[:, 0:1]) & (down_step[None, :] <= reach_row[:, 1:2])
    allowed = allowed & (side_step[None, :] >= -reach_row[:, 2:3]) & (side_step[None, :] <= reach_row[:, 3:4])
    allowed = allowed & (target_row[None, :] >= 0) & (target_row[None, :] < row_total)
    allowed = allowed & (target_col >= 0) & (target_col < col_total)
    return jnp.repeat(allowed, per_tile, axis=1)


def assemble(stacked):
    row_count, frame_count, tile_side, grid_cols, channels = stacked.shape
    return stacked.transpose(1, 0, 2, 3, 4).reshape(frame_count, row_count * tile_side, grid_cols, channels)


def reference(queries, key_heads, value_heads, out_grad, reach_tiles):
    frame_count, grid_rows, grid_cols, channels = queries.shape
    tile_side = TS
    head_count = HEADS
    head_size = channels // head_count
    score_scale = head_size ** -0.5
    per_tile = frame_count * tile_side * tile_side
    row_total = grid_rows // tile_side
    col_total = grid_cols // tile_side
    padding = ((0, 0), (tile_side, tile_side), (tile_side, tile_side), (0, 0))
    key_pad = jnp.pad(key_heads, padding)
    value_pad = jnp.pad(value_heads, padding)
    empty = jnp.zeros(key_pad.shape, jnp.float32)

    def row_step(state_pair, tile_row):
        key_sum, value_sum = state_pair
        query_rows = to_tiles(lax.dynamic_slice_in_dim(queries, tile_row * tile_side, tile_side, 1), tile_side)
        grad_rows = to_tiles(lax.dynamic_slice_in_dim(out_grad, tile_row * tile_side, tile_side, 1), tile_side)
        key_window = window(key_pad, tile_row, tile_side)
        value_window = window(value_pad, tile_row, tile_side)
        reach_row = lax.dynamic_index_in_dim(reach_tiles, tile_row, 0, keepdims=False)
        allowed = query_mask(reach_row, tile_row, 0, row_total, col_total, per_tile)
        query_split = query_rows.astype(jnp.float32).reshape(col_total, per_tile, head_count, head_size)
        grad_split = grad_rows.astype(jnp.float32).reshape(col_total, per_tile, head_count, head_size)
        key_split = key_window.astype(jnp.float32).reshape(col_total, 9 * per_tile, head_count, head_size)
        value_split = value_window.astype(jnp.float32).reshape(col_total, 9 * per_tile, head_count, head_size)
        scores = jnp.einsum("cqhd,ckhd->chqk", query_split, key_split) * score_scale
        scores = jnp.where(allowed[:, None, None, :], scores, NEGATIVE)
        row_top = jnp.max(scores, axis=-1, keepdims=True)
        log_total = row_top + jnp.log(jnp.sum(jnp.exp(scores - row_top), axis=-1, keepdims=True))
        weights = jnp.exp(scores - log_total)
        weights_low = lax.optimization_barrier(weights.astype(jnp.bfloat16)).astype(jnp.float32)
        attended = jnp.einsum("chqk,ckhd->cqhd", weights_low, value_split).astype(jnp.bfloat16)
        delta_sum = jnp.sum(grad_split * attended.astype(jnp.float32), axis=-1)
        delta_col = delta_sum.transpose(0, 2, 1)[..., None]
        dweights = jnp.einsum("cqhd,ckhd->chqk", grad_split, value_split)
        dscores = lax.optimization_barrier((weights * (dweights - delta_col)).astype(jnp.bfloat16)).astype(jnp.float32)
        query_grad = (jnp.einsum("chqk,ckhd->cqhd", dscores, key_split) * score_scale).astype(jnp.bfloat16)
        key_part = jnp.einsum("chqk,cqhd->ckhd", dscores, query_split) * score_scale
        value_part = jnp.einsum("chqk,cqhd->ckhd", weights_low, grad_split)
        key_sum = add_window(key_sum, key_part.reshape(col_total, 9 * per_tile, channels), tile_row, tile_side)
        value_sum = add_window(value_sum, value_part.reshape(col_total, 9 * per_tile, channels), tile_row, tile_side)
        attended_field = from_tiles(attended.reshape(col_total, per_tile, channels), frame_count, tile_side)
        grad_field = from_tiles(query_grad.reshape(col_total, per_tile, channels), frame_count, tile_side)
        return (key_sum, value_sum), (attended_field, grad_field)

    (key_sum, value_sum), (attended_rows, grad_rows_all) = lax.scan(row_step, (empty, empty), jnp.arange(row_total, dtype=jnp.int32))
    attended = assemble(attended_rows)
    query_grad = assemble(grad_rows_all)
    key_grad = key_sum[:, tile_side:tile_side + grid_rows, tile_side:tile_side + grid_cols, :].astype(jnp.bfloat16)
    value_grad = value_sum[:, tile_side:tile_side + grid_rows, tile_side:tile_side + grid_cols, :].astype(jnp.bfloat16)
    return (attended, query_grad, key_grad, value_grad)
```

```python
import functools
import math

import jax
import jax.numpy as jnp
from jax import lax
from jax.experimental import pallas as pl
from jax.experimental.pallas import tpu as pltpu
from jax.sharding import PartitionSpec as P

HEADS = 12
TS = 4
D = 128
MESH = pl.DeviceIdType.MESH
AHEAD = 4
CORNERS_AHEAD = 2
NEGATIVE = -1e30
SCALE = 1.0 / math.sqrt(D)
LOG2E = 1.4426950408889634

F32 = jnp.float32
BF16 = jnp.bfloat16


def dot(a, b, ca, cb):
    return lax.dot_general(a, b, (((ca,), (cb,)), ((), ())), preferred_element_type=F32)


def kernel(
    size_a, size_w, reach, q_in, k_in, v_in, g_in, o_out, dq_out, dk_out, dv_out,
    kall, qg, pack, acc, own, g3s, g3r, g4s, g4r, ob, bias, perm, perm_t,
    in_sem, out_sem, ss1, rs1, ss2, rs2, ss3, rs3, ss4, rs4,
):
    half_a = size_a // 2
    ia = lax.axis_index("ha")
    iw = lax.axis_index("wa")
    has_u, has_d = ia > 0, ia < size_a - 1
    has_l, has_r = iw > 0, iw < size_w - 1
    up, down = (ia - 1, iw), (ia + 1, iw)
    left, right = (ia, iw - 1), (ia, iw + 1)
    sides = ((has_l, left), (has_r, right))
    ends = ((has_u, up), (has_d, down))
    crossed = (ia == half_a, ia == half_a - 1)

    def lanes(h):
        return pl.ds(pl.multiple_of(h * D, D), D)

    def load(h, n):
        src = (k_in, v_in, q_in, g_in)[n].at[:, :, :, lanes(h)]
        dst = kall.at[h, n, 2:6, 1:4] if n < 2 else qg.at[h, n - 2]
        return pltpu.make_async_copy(src, dst, in_sem.at[h, n])

    def store(h, n):
        dst = (o_out, dq_out, dk_out, dv_out)[n].at[:, :, :, lanes(h)]
        return pltpu.make_async_copy(ob.at[h, n], dst, out_sem.at[h, n])

    def remote(src, dst, ss, rs, dev):
        return pltpu.make_async_remote_copy(
            src_ref=src, dst_ref=dst, send_sem=ss, recv_sem=rs, device_id=dev, device_id_type=MESH
        )

    def col_copy(h, s, dev):
        lo = 6 - 6 * s
        return remote(
            pack.at[h, :, 2 * s : 2 * s + 2], kall.at[h, :, lo : lo + 2, 1:4], ss1.at[h, s], rs1.at[h, 1 - s], dev
        )

    def row_place(s, j):
        moved = crossed[s] & sides[j // 2][0]
        col = jnp.where(moved, iw + (2 * (j // 2) - 1), iw)
        return jnp.where(moved, (j + 2) % 4, j), (ia + (2 * s - 1), col)

    def row_there(s, j):
        return ends[s][0] if j in (1, 2) else ends[s][0] & sides[j // 2][0]

    def row_copy(h, s, j):
        slot, dev = row_place(s, j)
        src = pack.at[h, :, 2 * j - 2 : 2 * j, 2 * s] if j in (1, 2) else kall.at[h, :, 2 * j : 2 * j + 2, 1 + 2 * s]
        dst = kall.at[h, :, pl.ds(2 * slot, 2), 4 - 4 * s]
        return remote(src, dst, ss2.at[h, s, j], rs2.at[h, 1 - s, slot], dev)

    def send_rows(h, columns):
        for s in range(2):
            for j in columns:

                @pl.when(row_there(s, j))
                def _():
                    row_copy(h, s, j).start()

    def receive_row(h, s, j):
        @pl.when(row_there(s, j))
        def _():
            ref = kall.at[h, :, 2 * j : 2 * j + 2, 4 * s]
            remote(ref, ref, ss2.at[h, s, j], rs2.at[h, s, j], ends[s][1]).wait_recv()

    def grad_row_copy(h, s, half):
        moved = crossed[s] & sides[half][0]
        col = jnp.where(moved, iw + (2 * half - 1), iw)
        to = jnp.where(moved, 1 - half, half)
        return remote(
            g3s.at[h, s, half], g3r.at[h, 1 - s, to], ss3.at[h, s, half], rs3.at[h, 1 - s, to], (ia + (2 * s - 1), col)
        )

    def grad_col_copy(h, s, dev):
        return remote(g4s.at[h, s], g4r.at[h, 1 - s], ss4.at[h, s], rs4.at[h, 1 - s], dev)

    def send(copy, h, group):
        for s, (there, dev) in enumerate(group):

            @pl.when(there)
            def _():
                copy(h, s, dev).start()

    def receive(copy, h, group, s):
        there, dev = group[s]

        @pl.when(there)
        def _():
            copy(h, 1 - s, dev).wait_recv()

    def loop(body):
        lax.fori_loop(0, HEADS, lambda h, c: (body(h), c)[1], 0)

    def load_kv(h):
        load(h, 0).start()
        load(h, 1).start()

    def load_qg(h):
        load(h, 2).start()
        load(h, 3).start()

    loop(load_kv)
    loop(load_qg)

    barrier = pltpu.get_barrier_semaphore()
    greeted = sides + ends
    for s, row in ((0, ia - 1), (1, ia + 1)):
        greeted += ((crossed[s] & has_l, (row, iw - 1)), (crossed[s] & has_r, (row, iw + 1)))
    for there, dev in greeted:

        @pl.when(there)
        def _():
            pl.semaphore_signal(barrier, inc=1, device_id=dev, device_id_type=MESH)

    def packed_of(i):
        return ((i >> 2) & 1) * 64 + (i >> 5) * 16 + ((i >> 3) & 3) * 4 + (i & 3)

    first = lax.broadcasted_iota(jnp.int32, (128, 128), 0)
    second = lax.broadcasted_iota(jnp.int32, (128, 128), 1)
    perm[...] = jnp.where(packed_of(first) == second, 1.0, 0.0).astype(BF16)
    perm_t[...] = jnp.where(packed_of(second) == first, 1.0, 0.0).astype(BF16)

    for s, (there, _) in enumerate(sides):

        @pl.when(jnp.logical_not(there))
        def _():
            def fill(h):
                kall[h, :, 6 * s : 6 * s + 2] = jnp.zeros((2, 2, 5, 32, D), BF16)
                g4r[h, s] = jnp.zeros((2, 2, 3, 32, D), BF16)

            loop(fill)

    for s, (there, _) in enumerate(ends):

        @pl.when(jnp.logical_not(there))
        def _():
            def fill(h):
                kall[h, :, :, 4 * s] = jnp.zeros((2, 8, 32, D), BF16)

            loop(fill)

    count = sum(there.astype(jnp.int32) for there, _ in greeted)
    pl.semaphore_wait(barrier, count)

    def send_edges(h):
        load(h, 0).wait()
        load(h, 1).wait()
        for kv in range(2):
            for a in range(3):
                x = kall[h, kv, 2:6, a + 1].reshape(128, D)
                pack[h, kv, :, a] = dot(perm_t[...], x, 1, 0).astype(BF16).reshape(4, 32, D)
        send_rows(h, (1, 2))
        send(col_copy, h, sides)

    for h in range(AHEAD):
        send_edges(h)

    shape = (8, 3, 32, 128)
    unit = lax.broadcasted_iota(jnp.int32, shape, 0)
    drow = lax.broadcasted_iota(jnp.int32, shape, 1) - 1
    token = lax.broadcasted_iota(jnp.int32, shape, 2)
    query = lax.broadcasted_iota(jnp.int32, shape, 3)
    qcol = (query >> 2) & 1
    for a in range(3):
        own_col = (token >> 2) & 1
        if a != 1:
            own_col = jnp.where(drow == a - 1, (unit >> 1) - 1, own_col)
        kcol = jnp.where((unit >= 2) & (unit < 6), own_col, (unit >> 1) - 1)
        dcol = kcol - qcol
        acol = iw * 2 + kcol
        in_cols = (acol >= 0) & (acol < 2 * size_w)

        def of(n):
            return jnp.where(qcol == 0, reach[a, 0, n], reach[a, 1, n])

        arow = ia * 3 + a + drow
        ok = in_cols & (arow >= 0) & (arow < 3 * size_a)
        ok = ok & (drow >= -of(0)) & (drow <= of(1)) & (dcol >= -of(2)) & (dcol <= of(3))
        bias[a] = jnp.where(ok, 0.0, NEGATIVE).astype(F32).reshape(768, 128)

    def forward(h):
        receive(col_copy, h, sides, 0)
        receive(col_copy, h, sides, 1)
        send_rows(h, (0, 3))

    def attend(h, slot, a):
        kk = kall[h, 0, :, pl.ds(a, 3)].reshape(768, D)
        vv = kall[h, 1, :, pl.ds(a, 3)].reshape(768, D)
        q = qg[h, 0, :, a].reshape(128, D)
        g = qg[h, 1, :, a].reshape(128, D)
        s = dot(kk, q, 1, 1) * (SCALE * LOG2E) + bias[a]
        p = jnp.exp2(s - jnp.max(s, axis=0, keepdims=True))
        p = p * (1.0 / jnp.sum(p, axis=0, keepdims=True))
        low = p.astype(BF16)
        dp = dot(vv, g, 1, 1)
        delta = jnp.sum(p * dp, axis=0, keepdims=True)
        ds = (p * (dp - delta)).astype(BF16)
        ob[h, 0, :, a] = dot(low, vv, 0, 0).astype(BF16).reshape(4, 32, D)
        ob[h, 1, :, a] = (dot(ds, kk, 0, 0) * SCALE).astype(BF16).reshape(4, 32, D)
        acc[slot, 0, :, pl.ds(a, 3)] += dot(ds, q, 1, 0).reshape(8, 3, 32, D)
        acc[slot, 1, :, pl.ds(a, 3)] += dot(low, g, 1, 0).reshape(8, 3, 32, D)

    def reduce_rows(h, slot):
        for s, row in ((0, 1), (1, 3)):
            @pl.when(ends[s][0])
            def _():
                for half in range(2):
                    ref = g3r.at[h, s, half]
                    remote(ref, ref, ss3.at[h, s, half], rs3.at[h, s, half], ends[s][1]).wait_recv()
                acc[slot, :, 0:2, row] += g3r[h, s, 0, :, 0:2].astype(F32)
                acc[slot, :, 6:8, row] += g3r[h, s, 1, :, 2:4].astype(F32)
                for kv in range(2):
                    x = jnp.concatenate([g3r[h, s, 0, kv, 2:4], g3r[h, s, 1, kv, 0:2]]).reshape(128, D)
                    acc[slot, kv, 2:6, row] += dot(perm[...], x, 1, 0).reshape(4, 32, D)

        for s in range(2):
            g4s[h, s] = acc[slot, :, 6 * s : 6 * s + 2, 1:4].astype(BF16)
        send(grad_col_copy, h, sides)
        own[h] = acc[slot, :, 2:6, 1:4]

    for h in range(CORNERS_AHEAD):
        forward(h)

    def step(h):
        slot = h % 2

        @pl.when(h + CORNERS_AHEAD < HEADS)
        def _():
            forward(h + CORNERS_AHEAD)

        @pl.when(h + AHEAD < HEADS)
        def _():
            send_edges(h + AHEAD)

        load(h, 2).wait()
        load(h, 3).wait()
        for s in range(2):
            for j in range(4):
                receive_row(h, s, j)
        acc[slot] = jnp.zeros((2, 8, 5, 32, D), F32)
        lax.fori_loop(0, 3, lambda a, c: (attend(h, slot, a), c)[1], 0)
        store(h, 0).start()
        store(h, 1).start()
        for s in range(2):
            for half in range(2):
                g3s[h, s, half] = acc[slot, :, 4 * half : 4 * half + 4, 4 * s].astype(BF16)

            @pl.when(ends[s][0])
            def _():
                for half in range(2):
                    grad_row_copy(h, s, half).start()


        @pl.when(h >= 1)
        def _():
            reduce_rows(h - 1, 1 - slot)

    loop(step)
    reduce_rows(HEADS - 1, (HEADS - 1) % 2)

    def finish(h):
        for s in range(2):
            receive(grad_col_copy, h, sides, s)
        for kv in range(2):
            for a in range(3):
                x = g4r[h, :, kv, :, a].reshape(128, D)
                y = dot(perm[...], x, 1, 0) + own[h, kv, :, a].reshape(128, D)
                if kv == 0:
                    y = y * SCALE
                ob[h, 2 + kv, :, a] = y.astype(BF16).reshape(4, 32, D)
        store(h, 2).start()
        store(h, 3).start()

    loop(finish)

    def drain(h):
        for n in range(4):
            store(h, n).wait()
        for copy in (col_copy, grad_col_copy):
            for s, (there, dev) in enumerate(sides):

                @pl.when(there)
                def _():
                    copy(h, s, dev).wait_send()

        for s in range(2):
            for j in range(4):

                @pl.when(row_there(s, j))
                def _():
                    row_copy(h, s, j).wait_send()

            @pl.when(ends[s][0])
            def _():
                for half in range(2):
                    grad_row_copy(h, s, half).wait_send()

    loop(drain)


def per_device(size_a, size_w, queries, key_heads, value_heads, out_grad, reach_tiles):
    shape = queries.shape
    ins = [x.reshape(4, 3, 32, HEADS * D) for x in (queries, key_heads, value_heads, out_grad)]
    any_spec = pl.BlockSpec(memory_space=pl.ANY)
    pair = pltpu.SemaphoreType.DMA((HEADS, 2))
    outs = pl.pallas_call(
        functools.partial(kernel, size_a, size_w),
        out_shape=[jax.ShapeDtypeStruct((4, 3, 32, HEADS * D), BF16)] * 4,
        in_specs=[pl.BlockSpec(memory_space=pltpu.SMEM)] + [any_spec] * 4,
        out_specs=[any_spec] * 4,
        scratch_shapes=[
            pltpu.VMEM((HEADS, 2, 8, 5, 32, D), BF16),
            pltpu.VMEM((HEADS, 2, 4, 3, 32, D), BF16),
            pltpu.VMEM((HEADS, 2, 4, 3, 32, D), BF16),
            pltpu.VMEM((2, 2, 8, 5, 32, D), F32),
            pltpu.VMEM((HEADS, 2, 4, 3, 32, D), F32),
            pltpu.VMEM((HEADS, 2, 2, 2, 4, 32, D), BF16),
            pltpu.VMEM((HEADS, 2, 2, 2, 4, 32, D), BF16),
            pltpu.VMEM((HEADS, 2, 2, 2, 3, 32, D), BF16),
            pltpu.VMEM((HEADS, 2, 2, 2, 3, 32, D), BF16),
            pltpu.VMEM((HEADS, 4, 4, 3, 32, D), BF16),
            pltpu.VMEM((3, 768, 128), F32),
            pltpu.VMEM((128, 128), BF16),
            pltpu.VMEM((128, 128), BF16),
            pltpu.SemaphoreType.DMA((HEADS, 4)),
            pltpu.SemaphoreType.DMA((HEADS, 4)),
        ]
        + [pair] * 2
        + [pltpu.SemaphoreType.DMA((HEADS, 2, 4))] * 2
        + [pltpu.SemaphoreType.DMA((HEADS, 2, 2))] * 2
        + [pair] * 2,
        compiler_params=pltpu.CompilerParams(
            collective_id=0, has_side_effects=True, vmem_limit_bytes=56 * 1024 * 1024
        ),
    )(reach_tiles, *ins)
    return tuple(x.reshape(shape) for x in outs)


def solution(mesh):
    spec = P(None, "ha", "wa", None)
    return jax.shard_map(
        functools.partial(per_device, mesh.shape["ha"], mesh.shape["wa"]),
        mesh=mesh,
        in_specs=(spec, spec, spec, spec, P("ha", "wa", None)),
        out_specs=(spec, spec, spec, spec),
        check_vma=False,
    )
```

```python
import functools
import math

import jax
import jax.numpy as jnp
from jax import lax
from jax.experimental import pallas as pl
from jax.experimental.pallas import tpu as pltpu
from jax.sharding import PartitionSpec as P

HEADS = 12
TS = 4
D = 128
MESH = pl.DeviceIdType.MESH
AHEAD = 4
CORNERS_AHEAD = 2
BEHIND = 4
NEGATIVE = -1e30
SCALE = 1.0 / math.sqrt(D)
LOG2E = 1.4426950408889634

F32 = jnp.float32
BF16 = jnp.bfloat16


def dot(a, b, ca, cb):
    return lax.dot_general(a, b, (((ca,), (cb,)), ((), ())), preferred_element_type=F32)


def kernel(
    size_a, size_w, reach, q_in, k_in, v_in, g_in, o_out, dq_out, dk_out, dv_out,
    kall, qg, pack, acc, own, g3s, g3r, g4s, g4r, bias, perm, perm_t,
    in_sem, ss1, rs1, ss2, rs2, ss3, rs3, ss4, rs4,
):
    half_a = size_a // 2
    ia = lax.axis_index("ha")
    iw = lax.axis_index("wa")
    has_u, has_d = ia > 0, ia < size_a - 1
    has_l, has_r = iw > 0, iw < size_w - 1
    up, down = (ia - 1, iw), (ia + 1, iw)
    left, right = (ia, iw - 1), (ia, iw + 1)
    sides = ((has_l, left), (has_r, right))
    ends = ((has_u, up), (has_d, down))
    crossed = (ia == half_a, ia == half_a - 1)

    def lanes(h):
        return pl.ds(pl.multiple_of(h * D, D), D)

    def load(h, n):
        src = (k_in, v_in, q_in, g_in)[n].at[:, :, :, lanes(h)]
        dst = kall.at[h, n, 2:6, 1:4] if n < 2 else qg.at[h, n - 2]
        return pltpu.make_async_copy(src, dst, in_sem.at[h, n])

    def remote(src, dst, ss, rs, dev):
        return pltpu.make_async_remote_copy(
            src_ref=src, dst_ref=dst, send_sem=ss, recv_sem=rs, device_id=dev, device_id_type=MESH
        )

    def col_copy(h, s, dev):
        lo = 6 - 6 * s
        return remote(
            pack.at[h, :, 2 * s : 2 * s + 2], kall.at[h, :, lo : lo + 2, 1:4], ss1.at[h, s], rs1.at[h, 1 - s], dev
        )

    def row_place(s, j):
        moved = crossed[s] & sides[j // 2][0]
        col = jnp.where(moved, iw + (2 * (j // 2) - 1), iw)
        return jnp.where(moved, (j + 2) % 4, j), (ia + (2 * s - 1), col)

    def row_there(s, j):
        return ends[s][0] if j in (1, 2) else ends[s][0] & sides[j // 2][0]

    def row_copy(h, s, j):
        slot, dev = row_place(s, j)
        src = pack.at[h, :, 2 * j - 2 : 2 * j, 2 * s] if j in (1, 2) else kall.at[h, :, 2 * j : 2 * j + 2, 1 + 2 * s]
        dst = kall.at[h, :, pl.ds(2 * slot, 2), 4 - 4 * s]
        return remote(src, dst, ss2.at[h, s, j], rs2.at[h, 1 - s, slot], dev)

    def send_rows(h, columns):
        for s in range(2):
            for j in columns:

                @pl.when(row_there(s, j))
                def _():
                    row_copy(h, s, j).start()

    def receive_row(h, s, j):
        @pl.when(row_there(s, j))
        def _():
            ref = kall.at[h, :, 2 * j : 2 * j + 2, 4 * s]
            remote(ref, ref, ss2.at[h, s, j], rs2.at[h, s, j], ends[s][1]).wait_recv()

    def grad_row_copy(h, s, half):
        moved = crossed[s] & sides[half][0]
        col = jnp.where(moved, iw + (2 * half - 1), iw)
        to = jnp.where(moved, 1 - half, half)
        return remote(
            g3s.at[h, s, half], g3r.at[h, 1 - s, to], ss3.at[h, s, half], rs3.at[h, 1 - s, to], (ia + (2 * s - 1), col)
        )

    def grad_col_copy(h, s, dev):
        return remote(g4s.at[h, s], g4r.at[h, 1 - s], ss4.at[h, s], rs4.at[h, 1 - s], dev)

    def send(copy, h, group):
        for s, (there, dev) in enumerate(group):

            @pl.when(there)
            def _():
                copy(h, s, dev).start()

    def receive(copy, h, group, s):
        there, dev = group[s]

        @pl.when(there)
        def _():
            copy(h, 1 - s, dev).wait_recv()

    def loop(body):
        lax.fori_loop(0, HEADS, lambda h, c: (body(h), c)[1], 0)

    def load_kv(h):
        load(h, 0).start()
        load(h, 1).start()

    def load_qg(h):
        load(h, 2).start()
        load(h, 3).start()

    loop(load_kv)
    loop(load_qg)

    barrier = pltpu.get_barrier_semaphore()
    greeted = sides + ends
    for s, row in ((0, ia - 1), (1, ia + 1)):
        greeted += ((crossed[s] & has_l, (row, iw - 1)), (crossed[s] & has_r, (row, iw + 1)))
    for there, dev in greeted:

        @pl.when(there)
        def _():
            pl.semaphore_signal(barrier, inc=1, device_id=dev, device_id_type=MESH)

    def packed_of(i):
        return ((i >> 2) & 1) * 64 + (i >> 5) * 16 + ((i >> 3) & 3) * 4 + (i & 3)

    first = lax.broadcasted_iota(jnp.int32, (128, 128), 0)
    second = lax.broadcasted_iota(jnp.int32, (128, 128), 1)
    perm[...] = jnp.where(packed_of(first) == second, 1.0, 0.0).astype(BF16)
    perm_t[...] = jnp.where(packed_of(second) == first, 1.0, 0.0).astype(BF16)

    for s, (there, _) in enumerate(sides):

        @pl.when(jnp.logical_not(there))
        def _():
            def fill(h):
                kall[h, :, 6 * s : 6 * s + 2] = jnp.zeros((2, 2, 5, 32, D), BF16)
                g4r[h, s] = jnp.zeros((2, 2, 3, 32, D), BF16)

            loop(fill)

    for s, (there, _) in enumerate(ends):

        @pl.when(jnp.logical_not(there))
        def _():
            def fill(h):
                kall[h, :, :, 4 * s] = jnp.zeros((2, 8, 32, D), BF16)

            loop(fill)

    count = sum(there.astype(jnp.int32) for there, _ in greeted)
    pl.semaphore_wait(barrier, count)

    def send_edges(h):
        load(h, 0).wait()
        load(h, 1).wait()
        for kv in range(2):
            for a in range(3):
                x = kall[h, kv, 2:6, a + 1].reshape(128, D)
                pack[h, kv, :, a] = dot(perm_t[...], x, 1, 0).astype(BF16).reshape(4, 32, D)
        send_rows(h, (1, 2))
        send(col_copy, h, sides)

    for h in range(AHEAD):
        send_edges(h)

    shape = (8, 3, 32, 128)
    unit = lax.broadcasted_iota(jnp.int32, shape, 0)
    drow = lax.broadcasted_iota(jnp.int32, shape, 1) - 1
    token = lax.broadcasted_iota(jnp.int32, shape, 2)
    query = lax.broadcasted_iota(jnp.int32, shape, 3)
    qcol = (query >> 2) & 1
    for a in range(3):
        own_col = (token >> 2) & 1
        if a != 1:
            own_col = jnp.where(drow == a - 1, (unit >> 1) - 1, own_col)
        kcol = jnp.where((unit >= 2) & (unit < 6), own_col, (unit >> 1) - 1)
        dcol = kcol - qcol
        acol = iw * 2 + kcol
        in_cols = (acol >= 0) & (acol < 2 * size_w)

        def of(n):
            return jnp.where(qcol == 0, reach[a, 0, n], reach[a, 1, n])

        arow = ia * 3 + a + drow
        ok = in_cols & (arow >= 0) & (arow < 3 * size_a)
        ok = ok & (drow >= -of(0)) & (drow <= of(1)) & (dcol >= -of(2)) & (dcol <= of(3))
        bias[a] = jnp.where(ok, 0.0, NEGATIVE).astype(F32).reshape(768, 128)

    def forward(h):
        receive(col_copy, h, sides, 0)
        receive(col_copy, h, sides, 1)
        send_rows(h, (0, 3))

    def attend(h, slot, a):
        kk = kall[h, 0, :, a : a + 3].reshape(768, D)
        vv = kall[h, 1, :, a : a + 3].reshape(768, D)
        q = qg[h, 0, :, a].reshape(128, D)
        g = qg[h, 1, :, a].reshape(128, D)
        s = dot(kk, q, 1, 1) * (SCALE * LOG2E) + bias[a]
        p = jnp.exp2(s - jnp.max(s, axis=0, keepdims=True))
        p = p * (1.0 / jnp.sum(p, axis=0, keepdims=True))
        low = p.astype(BF16)
        dp = dot(vv, g, 1, 1)
        delta = jnp.sum(p * dp, axis=0, keepdims=True)
        ds = (p * (dp - delta)).astype(BF16)
        o_out[:, a, :, lanes(h)] = dot(low, vv, 0, 0).astype(BF16).reshape(4, 32, D)
        dq_out[:, a, :, lanes(h)] = (dot(ds, kk, 0, 0) * SCALE).astype(BF16).reshape(4, 32, D)
        acc[slot, 0, :, a : a + 3] += dot(ds, q, 1, 0).reshape(8, 3, 32, D)
        acc[slot, 1, :, a : a + 3] += dot(low, g, 1, 0).reshape(8, 3, 32, D)

    def reduce_rows(h, slot):
        for s, row in ((0, 1), (1, 3)):
            @pl.when(ends[s][0])
            def _():
                for half in range(2):
                    ref = g3r.at[h, s, half]
                    remote(ref, ref, ss3.at[h, s, half], rs3.at[h, s, half], ends[s][1]).wait_recv()
                acc[slot, :, 0:2, row] += g3r[h, s, 0, :, 0:2].astype(F32)
                acc[slot, :, 6:8, row] += g3r[h, s, 1, :, 2:4].astype(F32)
                for kv in range(2):
                    x = jnp.concatenate([g3r[h, s, 0, kv, 2:4], g3r[h, s, 1, kv, 0:2]]).reshape(128, D)
                    acc[slot, kv, 2:6, row] += dot(perm[...], x, 1, 0).reshape(4, 32, D)

        for s in range(2):
            g4s[h, s] = acc[slot, :, 6 * s : 6 * s + 2, 1:4].astype(BF16)
        send(grad_col_copy, h, sides)
        own[h] = acc[slot, :, 2:6, 1:4]

    def finish(h):
        for s in range(2):
            receive(grad_col_copy, h, sides, s)
        for kv in range(2):
            for a in range(3):
                x = g4r[h, :, kv, :, a].reshape(128, D)
                y = dot(perm[...], x, 1, 0) + own[h, kv, :, a].reshape(128, D)
                if kv == 0:
                    y = y * SCALE
                (dk_out, dv_out)[kv][:, a, :, lanes(h)] = y.astype(BF16).reshape(4, 32, D)

    for h in range(CORNERS_AHEAD):
        forward(h)

    def step(h):
        slot = h % 2

        @pl.when(h + CORNERS_AHEAD < HEADS)
        def _():
            forward(h + CORNERS_AHEAD)

        @pl.when(h + AHEAD < HEADS)
        def _():
            send_edges(h + AHEAD)

        load(h, 2).wait()
        load(h, 3).wait()
        for s in range(2):
            for j in range(4):
                receive_row(h, s, j)
        acc[slot] = jnp.zeros((2, 8, 5, 32, D), F32)
        for a in range(3):
            attend(h, slot, a)
        for s in range(2):
            for half in range(2):
                g3s[h, s, half] = acc[slot, :, 4 * half : 4 * half + 4, 4 * s].astype(BF16)

            @pl.when(ends[s][0])
            def _():
                for half in range(2):
                    grad_row_copy(h, s, half).start()


        @pl.when(h >= 1)
        def _():
            reduce_rows(h - 1, 1 - slot)

        @pl.when(h >= BEHIND)
        def _():
            finish(h - BEHIND)

    loop(step)
    reduce_rows(HEADS - 1, (HEADS - 1) % 2)

    for h in range(HEADS - BEHIND, HEADS):
        finish(h)

    def drain(h):
        for copy in (col_copy, grad_col_copy):
            for s, (there, dev) in enumerate(sides):

                @pl.when(there)
                def _():
                    copy(h, s, dev).wait_send()

        for s in range(2):
            for j in range(4):

                @pl.when(row_there(s, j))
                def _():
                    row_copy(h, s, j).wait_send()

            @pl.when(ends[s][0])
            def _():
                for half in range(2):
                    grad_row_copy(h, s, half).wait_send()

    loop(drain)


def write_out(*refs):
    sources, outs, sem = refs[:4], refs[4:8], refs[8]
    copies = [pltpu.make_async_copy(x.at[f], y.at[f], sem.at[n, f]) for n, (x, y) in enumerate(zip(sources, outs)) for f in range(4)]
    for copy in copies:
        copy.start()
    for copy in copies:
        copy.wait()


def per_device(size_a, size_w, queries, key_heads, value_heads, out_grad, reach_tiles):
    shape = queries.shape
    ins = [x.reshape(4, 3, 32, HEADS * D) for x in (queries, key_heads, value_heads, out_grad)]
    ins = [pltpu.with_memory_space_constraint(x, pltpu.HBM) for x in ins]
    any_spec = pl.BlockSpec(memory_space=pl.ANY)
    pair = pltpu.SemaphoreType.DMA((HEADS, 2))
    results = pl.pallas_call(
        functools.partial(kernel, size_a, size_w),
        out_shape=[pltpu.VMEM((4, 3, 32, HEADS * D), BF16)] * 4,
        in_specs=[pl.BlockSpec(memory_space=pltpu.SMEM)] + [any_spec] * 4,
        out_specs=[pl.BlockSpec(memory_space=pltpu.VMEM)] * 4,
        scratch_shapes=[
            pltpu.VMEM((HEADS, 2, 8, 5, 32, D), BF16),
            pltpu.VMEM((HEADS, 2, 4, 3, 32, D), BF16),
            pltpu.VMEM((HEADS, 2, 4, 3, 32, D), BF16),
            pltpu.VMEM((2, 2, 8, 5, 32, D), F32),
            pltpu.VMEM((HEADS, 2, 4, 3, 32, D), F32),
            pltpu.VMEM((HEADS, 2, 2, 2, 4, 32, D), BF16),
            pltpu.VMEM((HEADS, 2, 2, 2, 4, 32, D), BF16),
            pltpu.VMEM((HEADS, 2, 2, 2, 3, 32, D), BF16),
            pltpu.VMEM((HEADS, 2, 2, 2, 3, 32, D), BF16),
            pltpu.VMEM((3, 768, 128), F32),
            pltpu.VMEM((128, 128), BF16),
            pltpu.VMEM((128, 128), BF16),
            pltpu.SemaphoreType.DMA((HEADS, 4)),
        ]
        + [pair] * 2
        + [pltpu.SemaphoreType.DMA((HEADS, 2, 4))] * 2
        + [pltpu.SemaphoreType.DMA((HEADS, 2, 2))] * 2
        + [pair] * 2,
        compiler_params=pltpu.CompilerParams(
            collective_id=0, has_side_effects=True, vmem_limit_bytes=56 * 1024 * 1024
        ),
    )(reach_tiles, *ins)
    outs = pl.pallas_call(
        write_out,
        out_shape=[jax.ShapeDtypeStruct((4, 3, 32, HEADS * D), BF16)] * 4,
        in_specs=[pl.BlockSpec(memory_space=pltpu.VMEM)] * 4,
        out_specs=[any_spec] * 4,
        scratch_shapes=[pltpu.SemaphoreType.DMA((4, 4))],
        compiler_params=pltpu.CompilerParams(vmem_limit_bytes=8 * 1024 * 1024),
    )(*(pltpu.with_memory_space_constraint(x, pltpu.VMEM) for x in results))
    return tuple(x.reshape(shape) for x in outs)


def solution(mesh):
    spec = P(None, "ha", "wa", None)
    return jax.shard_map(
        functools.partial(per_device, mesh.shape["ha"], mesh.shape["wa"]),
        mesh=mesh,
        in_specs=(spec, spec, spec, spec, P("ha", "wa", None)),
        out_specs=(spec, spec, spec, spec),
        check_vma=False,
    )
```

```python
import functools
import math

import jax
import jax.numpy as jnp
from jax import lax
from jax.experimental import pallas as pl
from jax.experimental.pallas import tpu as pltpu
from jax.sharding import PartitionSpec as P

HEADS = 12
TS = 4
D = 128
MESH = pl.DeviceIdType.MESH
AHEAD = 7
RELAY_AHEAD = 5
CORNERS_AHEAD = 3
ROWS_BEHIND = 2
RELAY_BEHIND = 4
BEHIND = 6
SLOTS = ROWS_BEHIND + 1
NEGATIVE = -1e30
SCALE = 1.0 / math.sqrt(D)
LOG2E = 1.4426950408889634

F32 = jnp.float32
BF16 = jnp.bfloat16


def dot(a, b, ca, cb):
    return lax.dot_general(a, b, (((ca,), (cb,)), ((), ())), preferred_element_type=F32)


def kernel(
    size_a, size_w, reach, q_in, k_in, v_in, g_in, o_out, dq_out, dk_out, dv_out,
    kall, k_own, v_own, q_own, g_own, pack, acc, own, g3s, g3r, g4s, g4r, r1, r4, bias, perm, perm_t,
    in_sem, ss1, rs1, ss2, rs2, ss3, rs3, ss4, rs4, ri1, ro1, ri4, ro4,
):
    half_a = size_a // 2
    ia = lax.axis_index("ha")
    iw = lax.axis_index("wa")
    has_u, has_d = ia > 0, ia < size_a - 1
    has_l, has_r = iw > 0, iw < size_w - 1
    up, down = (ia - 1, iw), (ia + 1, iw)
    left, right = (ia, iw - 1), (ia, iw + 1)
    sides = ((has_l, left), (has_r, right))
    ends = ((has_u, up), (has_d, down))
    crossed = (ia == half_a, ia == half_a - 1)

    parity, ring, rings = iw % 2, iw // 2, size_w // 2
    out = 2 * parity - 1
    shared = jnp.where(parity == 1, ring + 1, rings - ring)
    carried = jnp.where(parity == 1, ring, rings - 1 - ring)
    middle = (ia >= half_a - 2) & (ia < half_a + 2)

    def chosen(k, part, fewer):
        n = part * HEADS // rings - jnp.where(middle & (part > 0), fewer, 0)
        return (k * n) % HEADS >= HEADS - n

    def relayed_col(h, part):
        return chosen(h, part, jnp.where(part >= 2, 1, 0))

    def relayed_grad(h, part):
        return chosen(HEADS - 1 - h, part, jnp.where(part >= 3, 2, 1))

    def lanes(h):
        return pl.ds(pl.multiple_of(h * D, D), D)

    loads = [
        pltpu.make_async_copy(src, dst, in_sem.at[n])
        for n, (src, dst) in enumerate(((k_in, k_own), (v_in, v_own), (q_in, q_own), (g_in, g_own)))
    ]

    def remote(src, dst, ss, rs, dev):
        return pltpu.make_async_remote_copy(
            src_ref=src, dst_ref=dst, send_sem=ss, recv_sem=rs, device_id=dev, device_id_type=MESH
        )

    def col_copy(h, s, dev):
        lo = 6 - 6 * s
        return remote(
            pack.at[h, :, 2 * s : 2 * s + 2], kall.at[h, :, lo : lo + 2, 1:4], ss1.at[h, s], rs1.at[h, 1 - s], dev
        )

    def row_place(s, j):
        moved = crossed[s] & sides[j // 2][0]
        col = jnp.where(moved, iw + (2 * (j // 2) - 1), iw)
        return jnp.where(moved, (j + 2) % 4, j), (ia + (2 * s - 1), col)

    def row_there(s, j):
        return ends[s][0] if j in (1, 2) else ends[s][0] & sides[j // 2][0]

    def row_copy(h, s, j):
        slot, dev = row_place(s, j)
        src = pack.at[h, :, 2 * j - 2 : 2 * j, 2 * s] if j in (1, 2) else kall.at[h, :, 2 * j : 2 * j + 2, 1 + 2 * s]
        dst = kall.at[h, :, pl.ds(2 * slot, 2), 4 - 4 * s]
        return remote(src, dst, ss2.at[h, s, j], rs2.at[h, 1 - s, slot], dev)

    def send_rows(h, columns):
        for s in range(2):
            for j in columns:

                @pl.when(row_there(s, j))
                def _():
                    row_copy(h, s, j).start()

    def receive_row(h, s, j):
        @pl.when(row_there(s, j))
        def _():
            ref = kall.at[h, :, 2 * j : 2 * j + 2, 4 * s]
            remote(ref, ref, ss2.at[h, s, j], rs2.at[h, s, j], ends[s][1]).wait_recv()

    def grad_row_copy(h, s, half):
        moved = crossed[s] & sides[half][0]
        col = jnp.where(moved, iw + (2 * half - 1), iw)
        to = jnp.where(moved, 1 - half, half)
        return remote(
            g3s.at[h, s, half], g3r.at[h, 1 - s, to], ss3.at[h, s, half], rs3.at[h, 1 - s, to], (ia + (2 * s - 1), col)
        )

    def col_relay_in(h, s):
        return remote(pack.at[h, :, 2 * s : 2 * s + 2], r1.at[h], ss1.at[h, s], ri1.at[h], (ia, iw + 2 * out))

    def col_relay_out(h):
        dst = kall.at[h, :, pl.ds(6 - 6 * parity, 2), 1:4]
        return remote(r1.at[h], dst, ro1.at[h], rs1.at[h, 1 - parity], (ia, iw - out))

    def grad_relay_in(h, s):
        return remote(g4s.at[h, s], r4.at[h], ss4.at[h, s], ri4.at[h], (ia, iw + 2 * out))

    def grad_relay_out(h):
        return remote(r4.at[h], g4r.at[h, 1 - parity], ro4.at[h], rs4.at[h, 1 - parity], (ia, iw - out))

    def grad_col_copy(h, s, dev):
        return remote(g4s.at[h, s], g4r.at[h, 1 - s], ss4.at[h, s], rs4.at[h, 1 - s], dev)

    def send(direct, by_relay, relayed, h):
        for s, (there, dev) in enumerate(sides):
            through = (parity == s) & relayed(h, shared)

            @pl.when(there & through)
            def _():
                by_relay(h, s).start()

            @pl.when(there & jnp.logical_not(through))
            def _():
                direct(h, s, dev).start()

    def relay_col(h):
        @pl.when(relayed_col(h, carried))
        def _():
            remote(r1.at[h], r1.at[h], ro1.at[h], ri1.at[h], (ia, iw - out)).wait_recv()
            col_relay_out(h).start()

    def relay_grad(h):
        @pl.when(relayed_grad(h, carried))
        def _():
            remote(r4.at[h], r4.at[h], ro4.at[h], ri4.at[h], (ia, iw - out)).wait_recv()
            grad_relay_out(h).start()

    def receive(copy, h, group, s):
        there, dev = group[s]

        @pl.when(there)
        def _():
            copy(h, 1 - s, dev).wait_recv()

    def loop(body):
        lax.fori_loop(0, HEADS, lambda h, c: (body(h), c)[1], 0)

    for load in loads:
        load.start()

    barrier = pltpu.get_barrier_semaphore()
    greeted = sides + ends
    for s, row in ((0, ia - 1), (1, ia + 1)):
        greeted += ((crossed[s] & has_l, (row, iw - 1)), (crossed[s] & has_r, (row, iw + 1)))
    greeted += ((iw >= 2, (ia, iw - 2)), (iw < size_w - 2, (ia, iw + 2)))
    for there, dev in greeted:

        @pl.when(there)
        def _():
            pl.semaphore_signal(barrier, inc=1, device_id=dev, device_id_type=MESH)

    def packed_of(i):
        return ((i >> 2) & 1) * 64 + (i >> 5) * 16 + ((i >> 3) & 3) * 4 + (i & 3)

    first = lax.broadcasted_iota(jnp.int32, (128, 128), 0)
    second = lax.broadcasted_iota(jnp.int32, (128, 128), 1)
    perm[...] = jnp.where(packed_of(first) == second, 1.0, 0.0).astype(BF16)
    perm_t[...] = jnp.where(packed_of(second) == first, 1.0, 0.0).astype(BF16)

    for s, (there, _) in enumerate(sides):

        @pl.when(jnp.logical_not(there))
        def _():
            def fill(h):
                kall[h, :, 6 * s : 6 * s + 2] = jnp.zeros((2, 2, 5, 32, D), BF16)
                g4r[h, s] = jnp.zeros((2, 2, 3, 32, D), BF16)

            loop(fill)

    for s, (there, _) in enumerate(ends):

        @pl.when(jnp.logical_not(there))
        def _():
            def fill(h):
                kall[h, :, :, 4 * s] = jnp.zeros((2, 8, 32, D), BF16)

            loop(fill)

    count = sum(there.astype(jnp.int32) for there, _ in greeted)
    pl.semaphore_wait(barrier, count)

    loads[0].wait()
    loads[1].wait()

    def send_edges(h):
        for kv in range(2):
            for a in range(3):
                x = (k_own, v_own)[kv][:, a, :, lanes(h)]
                kall[h, kv, 2:6, a + 1] = x
                x = x.reshape(128, D)
                pack[h, kv, :, a] = dot(perm_t[...], x, 1, 0).astype(BF16).reshape(4, 32, D)
        send_rows(h, (1, 2))
        send(col_copy, col_relay_in, relayed_col, h)

    for h in range(3):
        send_edges(h)

    shape = (8, 3, 32, 128)
    unit = lax.broadcasted_iota(jnp.int32, shape, 0)
    drow = lax.broadcasted_iota(jnp.int32, shape, 1) - 1
    token = lax.broadcasted_iota(jnp.int32, shape, 2)
    query = lax.broadcasted_iota(jnp.int32, shape, 3)
    qcol = (query >> 2) & 1
    for a in range(3):
        own_col = (token >> 2) & 1
        if a != 1:
            own_col = jnp.where(drow == a - 1, (unit >> 1) - 1, own_col)
        kcol = jnp.where((unit >= 2) & (unit < 6), own_col, (unit >> 1) - 1)
        dcol = kcol - qcol
        acol = iw * 2 + kcol
        in_cols = (acol >= 0) & (acol < 2 * size_w)

        def of(n):
            return jnp.where(qcol == 0, reach[a, 0, n], reach[a, 1, n])

        arow = ia * 3 + a + drow
        ok = in_cols & (arow >= 0) & (arow < 3 * size_a)
        ok = ok & (drow >= -of(0)) & (drow <= of(1)) & (dcol >= -of(2)) & (dcol <= of(3))
        bias[a] = jnp.where(ok, 0.0, NEGATIVE).astype(F32).reshape(768, 128)

    def forward(h):
        receive(col_copy, h, sides, 0)
        receive(col_copy, h, sides, 1)
        send_rows(h, (0, 3))

    def attend(h, slot, a):
        kk = kall[h, 0, :, a : a + 3].reshape(768, D)
        vv = kall[h, 1, :, a : a + 3].reshape(768, D)
        q = q_own[:, a, :, lanes(h)].reshape(128, D)
        g = g_own[:, a, :, lanes(h)].reshape(128, D)
        s = dot(kk, q, 1, 1) * (SCALE * LOG2E) + bias[a]
        p = jnp.exp2(s - jnp.max(s, axis=0, keepdims=True))
        p = p * (1.0 / jnp.sum(p, axis=0, keepdims=True))
        low = p.astype(BF16)
        dp = dot(vv, g, 1, 1)
        delta = jnp.sum(p * dp, axis=0, keepdims=True)
        ds = (p * (dp - delta)).astype(BF16)
        o_out[:, a, :, lanes(h)] = dot(low, vv, 0, 0).astype(BF16).reshape(4, 32, D)
        dq_out[:, a, :, lanes(h)] = (dot(ds, kk, 0, 0) * SCALE).astype(BF16).reshape(4, 32, D)
        acc[slot, 0, :, a : a + 3] += dot(ds, q, 1, 0).reshape(8, 3, 32, D)
        acc[slot, 1, :, a : a + 3] += dot(low, g, 1, 0).reshape(8, 3, 32, D)

    def reduce_rows(h, slot):
        for s, row in ((0, 1), (1, 3)):
            @pl.when(ends[s][0])
            def _():
                for half in range(2):
                    ref = g3r.at[h, s, half]
                    remote(ref, ref, ss3.at[h, s, half], rs3.at[h, s, half], ends[s][1]).wait_recv()
                acc[slot, :, 0:2, row] += g3r[h, s, 0, :, 0:2].astype(F32)
                acc[slot, :, 6:8, row] += g3r[h, s, 1, :, 2:4].astype(F32)
                for kv in range(2):
                    x = jnp.concatenate([g3r[h, s, 0, kv, 2:4], g3r[h, s, 1, kv, 0:2]]).reshape(128, D)
                    acc[slot, kv, 2:6, row] += dot(perm[...], x, 1, 0).reshape(4, 32, D)

        for s in range(2):
            g4s[h, s] = acc[slot, :, 6 * s : 6 * s + 2, 1:4].astype(BF16)
        send(grad_col_copy, grad_relay_in, relayed_grad, h)
        own[h] = acc[slot, :, 2:6, 1:4]

    def finish(h):
        for s in range(2):
            receive(grad_col_copy, h, sides, s)
        for kv in range(2):
            for a in range(3):
                x = g4r[h, :, kv, :, a].reshape(128, D)
                y = dot(perm[...], x, 1, 0) + own[h, kv, :, a].reshape(128, D)
                if kv == 0:
                    y = y * SCALE
                (dk_out, dv_out)[kv][:, a, :, lanes(h)] = y.astype(BF16).reshape(4, 32, D)

    for h in range(RELAY_AHEAD):
        relay_col(h)
        if h < CORNERS_AHEAD:
            forward(h)
        if h + 3 < AHEAD:
            send_edges(h + 3)

    loads[2].wait()
    loads[3].wait()

    def step(h):
        slot = h % SLOTS

        @pl.when(h + CORNERS_AHEAD < HEADS)
        def _():
            forward(h + CORNERS_AHEAD)

        @pl.when(h + RELAY_AHEAD < HEADS)
        def _():
            relay_col(h + RELAY_AHEAD)

        @pl.when(h + AHEAD < HEADS)
        def _():
            send_edges(h + AHEAD)

        for s in range(2):
            for j in range(4):
                receive_row(h, s, j)
        acc[slot] = jnp.zeros((2, 8, 5, 32, D), F32)
        for a in range(3):
            attend(h, slot, a)
        for s in range(2):
            for half in range(2):
                g3s[h, s, half] = acc[slot, :, 4 * half : 4 * half + 4, 4 * s].astype(BF16)

            @pl.when(ends[s][0])
            def _():
                for half in range(2):
                    grad_row_copy(h, s, half).start()


        @pl.when(h >= ROWS_BEHIND)
        def _():
            reduce_rows(h - ROWS_BEHIND, (h - ROWS_BEHIND) % SLOTS)

        @pl.when(h >= RELAY_BEHIND)
        def _():
            relay_grad(h - RELAY_BEHIND)

        @pl.when(h >= BEHIND)
        def _():
            finish(h - BEHIND)

    loop(step)
    for h in range(HEADS - ROWS_BEHIND, HEADS):
        reduce_rows(h, h % SLOTS)

    for h in range(HEADS - RELAY_BEHIND, HEADS):
        relay_grad(h)
    for h in range(HEADS - BEHIND, HEADS):
        finish(h)

    def drain(h):
        @pl.when(relayed_col(h, carried))
        def _():
            col_relay_out(h).wait_send()

        @pl.when(relayed_grad(h, carried))
        def _():
            grad_relay_out(h).wait_send()

        for copy in (col_copy, grad_col_copy):
            for s, (there, dev) in enumerate(sides):

                @pl.when(there)
                def _():
                    copy(h, s, dev).wait_send()

        for s in range(2):
            for j in range(4):

                @pl.when(row_there(s, j))
                def _():
                    row_copy(h, s, j).wait_send()

            @pl.when(ends[s][0])
            def _():
                for half in range(2):
                    grad_row_copy(h, s, half).wait_send()

    loop(drain)


def write_out(*refs):
    sources, outs, sem = refs[:4], refs[4:8], refs[8]
    copies = [pltpu.make_async_copy(x.at[f], y.at[f], sem.at[n, f]) for n, (x, y) in enumerate(zip(sources, outs)) for f in range(4)]
    for copy in copies:
        copy.start()
    for copy in copies:
        copy.wait()


def per_device(size_a, size_w, queries, key_heads, value_heads, out_grad, reach_tiles):
    shape = queries.shape
    ins = [x.reshape(4, 3, 32, HEADS * D) for x in (queries, key_heads, value_heads, out_grad)]
    ins = [pltpu.with_memory_space_constraint(x, pltpu.HBM) for x in ins]
    any_spec = pl.BlockSpec(memory_space=pl.ANY)
    pair = pltpu.SemaphoreType.DMA((HEADS, 2))
    results = pl.pallas_call(
        functools.partial(kernel, size_a, size_w),
        out_shape=[pltpu.VMEM((4, 3, 32, HEADS * D), BF16)] * 4,
        in_specs=[pl.BlockSpec(memory_space=pltpu.SMEM)] + [any_spec] * 4,
        out_specs=[pl.BlockSpec(memory_space=pltpu.VMEM)] * 4,
        scratch_shapes=[
            pltpu.VMEM((HEADS, 2, 8, 5, 32, D), BF16),
            pltpu.VMEM((4, 3, 32, HEADS * D), BF16),
            pltpu.VMEM((4, 3, 32, HEADS * D), BF16),
            pltpu.VMEM((4, 3, 32, HEADS * D), BF16),
            pltpu.VMEM((4, 3, 32, HEADS * D), BF16),
            pltpu.VMEM((HEADS, 2, 4, 3, 32, D), BF16),
            pltpu.VMEM((SLOTS, 2, 8, 5, 32, D), F32),
            pltpu.VMEM((HEADS, 2, 4, 3, 32, D), F32),
            pltpu.VMEM((HEADS, 2, 2, 2, 4, 32, D), BF16),
            pltpu.VMEM((HEADS, 2, 2, 2, 4, 32, D), BF16),
            pltpu.VMEM((HEADS, 2, 2, 2, 3, 32, D), BF16),
            pltpu.VMEM((HEADS, 2, 2, 2, 3, 32, D), BF16),
            pltpu.VMEM((HEADS, 2, 2, 3, 32, D), BF16),
            pltpu.VMEM((HEADS, 2, 2, 3, 32, D), BF16),
            pltpu.VMEM((3, 768, 128), F32),
            pltpu.VMEM((128, 128), BF16),
            pltpu.VMEM((128, 128), BF16),
            pltpu.SemaphoreType.DMA((4,)),
        ]
        + [pair] * 2
        + [pltpu.SemaphoreType.DMA((HEADS, 2, 4))] * 2
        + [pltpu.SemaphoreType.DMA((HEADS, 2, 2))] * 2
        + [pair] * 2
        + [pltpu.SemaphoreType.DMA((HEADS,))] * 4,
        compiler_params=pltpu.CompilerParams(
            collective_id=0, has_side_effects=True, vmem_limit_bytes=56 * 1024 * 1024
        ),
    )(reach_tiles, *ins)
    outs = pl.pallas_call(
        write_out,
        out_shape=[jax.ShapeDtypeStruct((4, 3, 32, HEADS * D), BF16)] * 4,
        in_specs=[pl.BlockSpec(memory_space=pltpu.VMEM)] * 4,
        out_specs=[any_spec] * 4,
        scratch_shapes=[pltpu.SemaphoreType.DMA((4, 4))],
        compiler_params=pltpu.CompilerParams(vmem_limit_bytes=8 * 1024 * 1024),
    )(*(pltpu.with_memory_space_constraint(x, pltpu.VMEM) for x in results))
    return tuple(x.reshape(shape) for x in outs)


def solution(mesh):
    spec = P(None, "ha", "wa", None)
    return jax.shard_map(
        functools.partial(per_device, mesh.shape["ha"], mesh.shape["wa"]),
        mesh=mesh,
        in_specs=(spec, spec, spec, spec, P("ha", "wa", None)),
        out_specs=(spec, spec, spec, spec),
        check_vma=False,
    )
```

```python
import functools
import math

import jax
import jax.numpy as jnp
from jax import lax
from jax.experimental import pallas as pl
from jax.experimental.pallas import tpu as pltpu
from jax.sharding import PartitionSpec as P

HEADS = 12
TS = 4
D = 128
MESH = pl.DeviceIdType.MESH
AHEAD = 7
RELAY_AHEAD = 5
CORNERS_AHEAD = 3
ROWS_BEHIND = 2
RELAY_BEHIND = 4
BEHIND = 6
NEGATIVE = -1e30
SCALE = 1.0 / math.sqrt(D)
LOG2E = 1.4426950408889634

F32 = jnp.float32
BF16 = jnp.bfloat16


def dot(a, b, ca, cb):
    return lax.dot_general(a, b, (((ca,), (cb,)), ((), ())), preferred_element_type=F32)


def kernel(
    size_a, size_w, reach, q_in, k_in, v_in, g_in, o_out, dq_out, dk_out, dv_out,
    kall, k_own, v_own, q_own, g_own, pack, acc, g3s, g3r, g4s, g4r, r1, r4, bias, perm, perm_t,
    in_sem, ss1, rs1, ss2, rs2, ss3, rs3, ss4, rs4, ri1, ro1, ri4, ro4,
):
    half_a = size_a // 2
    ia = lax.axis_index("ha")
    iw = lax.axis_index("wa")
    has_u, has_d = ia > 0, ia < size_a - 1
    has_l, has_r = iw > 0, iw < size_w - 1
    up, down = (ia - 1, iw), (ia + 1, iw)
    left, right = (ia, iw - 1), (ia, iw + 1)
    sides = ((has_l, left), (has_r, right))
    ends = ((has_u, up), (has_d, down))
    crossed = (ia == half_a, ia == half_a - 1)

    parity, ring, rings = iw % 2, iw // 2, size_w // 2
    out = 2 * parity - 1
    shared = jnp.where(parity == 1, ring + 1, rings - ring)
    carried = jnp.where(parity == 1, ring, rings - 1 - ring)
    middle = (ia >= half_a - 2) & (ia < half_a + 2)

    def chosen(k, part, fewer):
        n = part * HEADS // rings - jnp.where(middle & (part > 0), fewer, 0)
        return (k * n) % HEADS >= HEADS - n

    def relayed_col(h, part):
        return chosen(h, part, jnp.where(part >= 2, 1, 0))

    def relayed_grad(h, part):
        return chosen(HEADS - 1 - h, part, jnp.where(part >= 3, 2, 1))

    def lanes(h):
        return pl.ds(pl.multiple_of(h * D, D), D)

    loads = [
        pltpu.make_async_copy(src, dst, in_sem.at[n])
        for n, (src, dst) in enumerate(((k_in, k_own), (v_in, v_own), (q_in, q_own), (g_in, g_own)))
    ]

    def remote(src, dst, ss, rs, dev):
        return pltpu.make_async_remote_copy(
            src_ref=src, dst_ref=dst, send_sem=ss, recv_sem=rs, device_id=dev, device_id_type=MESH
        )

    def col_copy(h, s, dev):
        lo = 6 - 6 * s
        return remote(
            pack.at[h, :, 2 * s : 2 * s + 2], kall.at[h, :, lo : lo + 2, 1:4], ss1.at[h, s], rs1.at[h, 1 - s], dev
        )

    def row_place(s, j):
        moved = crossed[s] & sides[j // 2][0]
        col = jnp.where(moved, iw + (2 * (j // 2) - 1), iw)
        return jnp.where(moved, (j + 2) % 4, j), (ia + (2 * s - 1), col)

    def row_there(s, j):
        return ends[s][0] if j in (1, 2) else ends[s][0] & sides[j // 2][0]

    def row_copy(h, s, j):
        slot, dev = row_place(s, j)
        src = pack.at[h, :, 2 * j - 2 : 2 * j, 2 * s] if j in (1, 2) else kall.at[h, :, 2 * j : 2 * j + 2, 1 + 2 * s]
        dst = kall.at[h, :, pl.ds(2 * slot, 2), 4 - 4 * s]
        return remote(src, dst, ss2.at[h, s, j], rs2.at[h, 1 - s, slot], dev)

    def send_rows(h, columns):
        for s in range(2):
            for j in columns:

                @pl.when(row_there(s, j))
                def _():
                    row_copy(h, s, j).start()

    def receive_row(h, s, j):
        @pl.when(row_there(s, j))
        def _():
            ref = kall.at[h, :, 2 * j : 2 * j + 2, 4 * s]
            remote(ref, ref, ss2.at[h, s, j], rs2.at[h, s, j], ends[s][1]).wait_recv()

    def grad_row_copy(h, s, half):
        moved = crossed[s] & sides[half][0]
        col = jnp.where(moved, iw + (2 * half - 1), iw)
        to = jnp.where(moved, 1 - half, half)
        return remote(
            g3s.at[h, s, half], g3r.at[h, 1 - s, to], ss3.at[h, s, half], rs3.at[h, 1 - s, to], (ia + (2 * s - 1), col)
        )

    def col_relay_in(h, s):
        return remote(pack.at[h, :, 2 * s : 2 * s + 2], r1.at[h], ss1.at[h, s], ri1.at[h], (ia, iw + 2 * out))

    def col_relay_out(h):
        dst = kall.at[h, :, pl.ds(6 - 6 * parity, 2), 1:4]
        return remote(r1.at[h], dst, ro1.at[h], rs1.at[h, 1 - parity], (ia, iw - out))

    def grad_relay_in(h, s):
        return remote(g4s.at[h, s], r4.at[h], ss4.at[h, s], ri4.at[h], (ia, iw + 2 * out))

    def grad_relay_out(h):
        return remote(r4.at[h], g4r.at[h, 1 - parity], ro4.at[h], rs4.at[h, 1 - parity], (ia, iw - out))

    def grad_col_copy(h, s, dev):
        return remote(g4s.at[h, s], g4r.at[h, 1 - s], ss4.at[h, s], rs4.at[h, 1 - s], dev)

    def send(direct, by_relay, relayed, h):
        for s, (there, dev) in enumerate(sides):
            through = (parity == s) & relayed(h, shared)

            @pl.when(there & through)
            def _():
                by_relay(h, s).start()

            @pl.when(there & jnp.logical_not(through))
            def _():
                direct(h, s, dev).start()

    def relay_col(h):
        @pl.when(relayed_col(h, carried))
        def _():
            remote(r1.at[h], r1.at[h], ro1.at[h], ri1.at[h], (ia, iw - out)).wait_recv()
            col_relay_out(h).start()

    def relay_grad(h):
        @pl.when(relayed_grad(h, carried))
        def _():
            remote(r4.at[h], r4.at[h], ro4.at[h], ri4.at[h], (ia, iw - out)).wait_recv()
            grad_relay_out(h).start()

    def receive(copy, h, group, s):
        there, dev = group[s]

        @pl.when(there)
        def _():
            copy(h, 1 - s, dev).wait_recv()

    def loop(body):
        lax.fori_loop(0, HEADS, lambda h, c: (body(h), c)[1], 0)

    for load in loads:
        load.start()

    barrier = pltpu.get_barrier_semaphore()
    greeted = sides + ends
    for s, row in ((0, ia - 1), (1, ia + 1)):
        greeted += ((crossed[s] & has_l, (row, iw - 1)), (crossed[s] & has_r, (row, iw + 1)))
    greeted += ((iw >= 2, (ia, iw - 2)), (iw < size_w - 2, (ia, iw + 2)))
    for there, dev in greeted:

        @pl.when(there)
        def _():
            pl.semaphore_signal(barrier, inc=1, device_id=dev, device_id_type=MESH)

    def packed_of(i):
        return ((i >> 2) & 1) * 64 + (i >> 5) * 16 + ((i >> 3) & 3) * 4 + (i & 3)

    first = lax.broadcasted_iota(jnp.int32, (128, 128), 0)
    second = lax.broadcasted_iota(jnp.int32, (128, 128), 1)
    perm[...] = jnp.where(packed_of(first) == second, 1.0, 0.0).astype(BF16)
    perm_t[...] = jnp.where(packed_of(second) == first, 1.0, 0.0).astype(BF16)

    for s, (there, _) in enumerate(sides):

        @pl.when(jnp.logical_not(there))
        def _():
            def fill(h):
                kall[h, :, 6 * s : 6 * s + 2] = jnp.zeros((2, 2, 5, 32, D), BF16)
                g4r[h, s] = jnp.zeros((2, 2, 3, 32, D), BF16)

            loop(fill)

    for s, (there, _) in enumerate(ends):

        @pl.when(jnp.logical_not(there))
        def _():
            def fill(h):
                kall[h, :, :, 4 * s] = jnp.zeros((2, 8, 32, D), BF16)

            loop(fill)

    count = sum(there.astype(jnp.int32) for there, _ in greeted)
    pl.semaphore_wait(barrier, count)

    def permute(matrix, x, y):
        z = dot(matrix[...], jnp.concatenate([x, y], axis=1), 1, 0)
        return z[:, :D], z[:, D:]

    loads[0].wait()
    loads[1].wait()

    def send_edges(h):
        for a in range(3):
            x = [own[:, a, :, lanes(h)] for own in (k_own, v_own)]
            kall[h, 0, 2:6, a + 1] = x[0]
            kall[h, 1, 2:6, a + 1] = x[1]
            y = permute(perm_t, x[0].reshape(128, D), x[1].reshape(128, D))
            pack[h, 0, :, a] = y[0].astype(BF16).reshape(4, 32, D)
            pack[h, 1, :, a] = y[1].astype(BF16).reshape(4, 32, D)
        send_rows(h, (1, 2))
        send(col_copy, col_relay_in, relayed_col, h)

    for h in range(3):
        send_edges(h)

    shape = (6, 3, 32, 128)
    unit = lax.broadcasted_iota(jnp.int32, shape, 0)
    drow = lax.broadcasted_iota(jnp.int32, shape, 1) - 1
    token = lax.broadcasted_iota(jnp.int32, shape, 2)
    query = lax.broadcasted_iota(jnp.int32, shape, 3)
    qcol = (query >> 2) & 1
    for a in range(3):
        own_col = (token >> 2) & 1
        if a != 1:
            own_col = jnp.where(drow == a - 1, unit >> 1, own_col)
        kcol = jnp.where(unit < 4, own_col, 3 * qcol - 1)
        dcol = kcol - qcol
        acol = iw * 2 + kcol
        in_cols = (acol >= 0) & (acol < 2 * size_w)

        def of(n):
            return jnp.where(qcol == 0, reach[a, 0, n], reach[a, 1, n])

        arow = ia * 3 + a + drow
        ok = in_cols & (arow >= 0) & (arow < 3 * size_a)
        ok = ok & (drow >= -of(0)) & (drow <= of(1)) & (dcol >= -of(2)) & (dcol <= of(3))
        bias[a] = jnp.where(ok, 0.0, NEGATIVE).astype(F32).reshape(576, 128)

    def forward(h):
        receive(col_copy, h, sides, 0)
        receive(col_copy, h, sides, 1)
        send_rows(h, (0, 3))

    left_query = ((lax.broadcasted_iota(jnp.int32, (128, D), 0) >> 2) & 1) == 0
    none = jnp.zeros((128, D), BF16)

    def attend(h, a):
        def keys(kv, lo, hi):
            return kall[h, kv, lo:hi, a : a + 3].reshape((hi - lo) * 96, D)

        def halo(kv):
            return jnp.concatenate([keys(kv, 0, 2), keys(kv, 6, 8)], axis=1)

        def by_side(x):
            return jnp.concatenate([jnp.where(left_query, x, none), jnp.where(left_query, none, x)], axis=1)

        def own_side(x):
            return jnp.where(left_query, x[:, :D], x[:, D:])

        k_mid, v_mid, k_halo, v_halo = keys(0, 2, 6), keys(1, 2, 6), halo(0), halo(1)
        q = q_own[:, a, :, lanes(h)].reshape(128, D)
        g = g_own[:, a, :, lanes(h)].reshape(128, D)
        both = jnp.concatenate([jnp.concatenate([q, none], axis=1), jnp.concatenate([none, g], axis=1)], axis=0)
        q_side, g_side = by_side(q), by_side(g)
        mid = dot(jnp.concatenate([k_mid, v_mid], axis=1), both, 1, 1)
        s = jnp.concatenate([mid[:, :128], dot(k_halo, q_side, 1, 1)], axis=0)
        dp = jnp.concatenate([mid[:, 128:], dot(v_halo, g_side, 1, 1)], axis=0)
        s = s * (SCALE * LOG2E) + bias[a]
        p = jnp.exp2(s - jnp.max(s, axis=0, keepdims=True))
        p = p * (1.0 / jnp.sum(p, axis=0, keepdims=True))
        low = p.astype(BF16)
        t = p * dp
        ds = (t - p * jnp.sum(t, axis=0, keepdims=True)).astype(BF16)
        o = dot(low[:384], v_mid, 0, 0) + own_side(dot(low[384:], v_halo, 0, 0))
        dq = dot(ds[:384], k_mid, 0, 0) + own_side(dot(ds[384:], k_halo, 0, 0))
        o_out[:, a, :, lanes(h)] = o.astype(BF16).reshape(4, 32, D)
        dq_out[:, a, :, lanes(h)] = (dq * SCALE).astype(BF16).reshape(4, 32, D)
        mid = dot(jnp.concatenate([ds[:384], low[:384]], axis=1), both, 1, 0)
        sums = ((mid[:, :D], dot(ds[384:], q_side, 1, 0)), (mid[:, D:], dot(low[384:], g_side, 1, 0)))
        for kv, (own, beside) in enumerate(sums):
            own = own.reshape(4, 3, 32, D)
            two = (beside[:, :D].reshape(2, 3, 32, D), beside[:, D:].reshape(2, 3, 32, D))
            for i in range(3):
                row = a + i - 1
                if row in (-1, 3):
                    end = 0 if row < 0 else 1
                    g3s[h, end, 0, kv, 0:2] = two[0][:, i].astype(BF16)
                    g3s[h, end, 0, kv, 2:4] = own[0:2, i].astype(BF16)
                    g3s[h, end, 1, kv, 0:2] = own[2:4, i].astype(BF16)
                    g3s[h, end, 1, kv, 2:4] = two[1][:, i].astype(BF16)
                elif row > a or a == 0:
                    acc[h, kv, 0:2, row] = two[0][:, i]
                    acc[h, kv, 2:6, row] = own[:, i]
                    acc[h, kv, 6:8, row] = two[1][:, i]
                else:
                    acc[h, kv, 0:2, row] += two[0][:, i]
                    acc[h, kv, 2:6, row] += own[:, i]
                    acc[h, kv, 6:8, row] += two[1][:, i]

    def send_grad_rows(h, s):
        @pl.when(ends[s][0])
        def _():
            for half in range(2):
                grad_row_copy(h, s, half).start()

    def reduce_rows(h):
        for s in range(2):
            row = 2 * s

            @pl.when(ends[s][0])
            def _():
                for half in range(2):
                    ref = g3r.at[h, s, half]
                    remote(ref, ref, ss3.at[h, s, half], rs3.at[h, s, half], ends[s][1]).wait_recv()
                acc[h, :, 0:2, row] += g3r[h, s, 0, :, 0:2].astype(F32)
                acc[h, :, 6:8, row] += g3r[h, s, 1, :, 2:4].astype(F32)
                x = [jnp.concatenate([g3r[h, s, 0, kv, 2:4], g3r[h, s, 1, kv, 0:2]]).reshape(128, D) for kv in range(2)]
                for kv, y in enumerate(permute(perm, x[0], x[1])):
                    acc[h, kv, 2:6, row] += y.reshape(4, 32, D)

        for s in range(2):
            g4s[h, s] = acc[h, :, 6 * s : 6 * s + 2].astype(BF16)
        send(grad_col_copy, grad_relay_in, relayed_grad, h)

    def finish(h):
        for s in range(2):
            receive(grad_col_copy, h, sides, s)
        for a in range(3):
            x = [g4r[h, :, kv, :, a].reshape(128, D) for kv in range(2)]
            y = permute(perm, x[0], x[1])
            dk = (y[0].reshape(4, 32, D) + acc[h, 0, 2:6, a]) * SCALE
            dv = y[1].reshape(4, 32, D) + acc[h, 1, 2:6, a]
            dk_out[:, a, :, lanes(h)] = dk.astype(BF16)
            dv_out[:, a, :, lanes(h)] = dv.astype(BF16)

    for h in range(RELAY_AHEAD):
        relay_col(h)
        if h < CORNERS_AHEAD:
            forward(h)
        if h + 3 < AHEAD:
            send_edges(h + 3)

    loads[2].wait()
    loads[3].wait()

    def step(h):
        @pl.when(h + CORNERS_AHEAD < HEADS)
        def _():
            forward(h + CORNERS_AHEAD)

        @pl.when(h + RELAY_AHEAD < HEADS)
        def _():
            relay_col(h + RELAY_AHEAD)

        @pl.when(h + AHEAD < HEADS)
        def _():
            send_edges(h + AHEAD)

        for a in range(3):
            if a != 1:
                for j in range(4):
                    receive_row(h, a // 2, j)
            attend(h, a)
            if a != 1:
                send_grad_rows(h, a // 2)

        @pl.when(h >= ROWS_BEHIND)
        def _():
            reduce_rows(h - ROWS_BEHIND)

        @pl.when(h >= RELAY_BEHIND)
        def _():
            relay_grad(h - RELAY_BEHIND)

        @pl.when(h >= BEHIND)
        def _():
            finish(h - BEHIND)

    loop(step)
    for h in range(HEADS - ROWS_BEHIND, HEADS):
        reduce_rows(h)

    for h in range(HEADS - RELAY_BEHIND, HEADS):
        relay_grad(h)
    for h in range(HEADS - BEHIND, HEADS):
        finish(h)

    def drain(h):
        @pl.when(relayed_col(h, carried))
        def _():
            col_relay_out(h).wait_send()

        @pl.when(relayed_grad(h, carried))
        def _():
            grad_relay_out(h).wait_send()

        for copy in (col_copy, grad_col_copy):
            for s, (there, dev) in enumerate(sides):

                @pl.when(there)
                def _():
                    copy(h, s, dev).wait_send()

        for s in range(2):
            for j in range(4):

                @pl.when(row_there(s, j))
                def _():
                    row_copy(h, s, j).wait_send()

            @pl.when(ends[s][0])
            def _():
                for half in range(2):
                    grad_row_copy(h, s, half).wait_send()

    loop(drain)


def write_out(*refs):
    sources, outs, sem = refs[:4], refs[4:8], refs[8]
    copies = [pltpu.make_async_copy(x.at[f], y.at[f], sem.at[n, f]) for n, (x, y) in enumerate(zip(sources, outs)) for f in range(4)]
    for copy in copies:
        copy.start()
    for copy in copies:
        copy.wait()


def per_device(size_a, size_w, queries, key_heads, value_heads, out_grad, reach_tiles):
    shape = queries.shape
    ins = [x.reshape(4, 3, 32, HEADS * D) for x in (queries, key_heads, value_heads, out_grad)]
    ins = [pltpu.with_memory_space_constraint(x, pltpu.HBM) for x in ins]
    any_spec = pl.BlockSpec(memory_space=pl.ANY)
    pair = pltpu.SemaphoreType.DMA((HEADS, 2))
    results = pl.pallas_call(
        functools.partial(kernel, size_a, size_w),
        out_shape=[pltpu.VMEM((4, 3, 32, HEADS * D), BF16)] * 4,
        in_specs=[pl.BlockSpec(memory_space=pltpu.SMEM)] + [any_spec] * 4,
        out_specs=[pl.BlockSpec(memory_space=pltpu.VMEM)] * 4,
        scratch_shapes=[
            pltpu.VMEM((HEADS, 2, 8, 5, 32, D), BF16),
            pltpu.VMEM((4, 3, 32, HEADS * D), BF16),
            pltpu.VMEM((4, 3, 32, HEADS * D), BF16),
            pltpu.VMEM((4, 3, 32, HEADS * D), BF16),
            pltpu.VMEM((4, 3, 32, HEADS * D), BF16),
            pltpu.VMEM((HEADS, 2, 4, 3, 32, D), BF16),
            pltpu.VMEM((HEADS, 2, 8, 3, 32, D), F32),
            pltpu.VMEM((HEADS, 2, 2, 2, 4, 32, D), BF16),
            pltpu.VMEM((HEADS, 2, 2, 2, 4, 32, D), BF16),
            pltpu.VMEM((HEADS, 2, 2, 2, 3, 32, D), BF16),
            pltpu.VMEM((HEADS, 2, 2, 2, 3, 32, D), BF16),
            pltpu.VMEM((HEADS, 2, 2, 3, 32, D), BF16),
            pltpu.VMEM((HEADS, 2, 2, 3, 32, D), BF16),
            pltpu.VMEM((3, 576, 128), F32),
            pltpu.VMEM((128, 128), BF16),
            pltpu.VMEM((128, 128), BF16),
            pltpu.SemaphoreType.DMA((4,)),
        ]
        + [pair] * 2
        + [pltpu.SemaphoreType.DMA((HEADS, 2, 4))] * 2
        + [pltpu.SemaphoreType.DMA((HEADS, 2, 2))] * 2
        + [pair] * 2
        + [pltpu.SemaphoreType.DMA((HEADS,))] * 4,
        compiler_params=pltpu.CompilerParams(
            collective_id=0, has_side_effects=True, vmem_limit_bytes=56 * 1024 * 1024
        ),
    )(reach_tiles, *ins)
    outs = pl.pallas_call(
        write_out,
        out_shape=[jax.ShapeDtypeStruct((4, 3, 32, HEADS * D), BF16)] * 4,
        in_specs=[pl.BlockSpec(memory_space=pltpu.VMEM)] * 4,
        out_specs=[any_spec] * 4,
        scratch_shapes=[pltpu.SemaphoreType.DMA((4, 4))],
        compiler_params=pltpu.CompilerParams(vmem_limit_bytes=8 * 1024 * 1024),
    )(*(pltpu.with_memory_space_constraint(x, pltpu.VMEM) for x in results))
    return tuple(x.reshape(shape) for x in outs)


def solution(mesh):
    spec = P(None, "ha", "wa", None)
    return jax.shard_map(
        functools.partial(per_device, mesh.shape["ha"], mesh.shape["wa"]),
        mesh=mesh,
        in_specs=(spec, spec, spec, spec, P("ha", "wa", None)),
        out_specs=(spec, spec, spec, spec),
        check_vma=False,
    )
```

```python
import functools
import math

import jax
import jax.numpy as jnp
from jax import lax
from jax.experimental import pallas as pl
from jax.experimental.pallas import tpu as pltpu
from jax.sharding import PartitionSpec as P

HEADS = 12
TS = 4
D = 128
MESH = pl.DeviceIdType.MESH
AHEAD = 7
RELAY_AHEAD = 5
CORNERS_AHEAD = 3
ROWS_BEHIND = 2
BEHIND = 6
NEGATIVE = -1e30
SCALE = 1.0 / math.sqrt(D)
LOG2E = 1.4426950408889634

F32 = jnp.float32
BF16 = jnp.bfloat16


def dot(a, b, ca, cb):
    return lax.dot_general(a, b, (((ca,), (cb,)), ((), ())), preferred_element_type=F32)


def kernel(
    size_a, size_w, reach, q_in, k_in, v_in, g_in, o_out, dq_out, dk_out, dv_out,
    kall, k_own, v_own, q_own, g_own, pack, acc, g3s, g3r, g4s, g4r, r1, r4, bias, perm, perm_t,
    in_sem, ss1, rs1, ss2, rs2, ss3, rs3, ss4, rs4, ri1, ro1, ri4, ro4,
):
    half_a = size_a // 2
    ia = lax.axis_index("ha")
    even = ia % 2 == 0
    iw = lax.axis_index("wa")
    has_u, has_d = ia > 0, ia < size_a - 1
    has_l, has_r = iw > 0, iw < size_w - 1
    up, down = (ia - 1, iw), (ia + 1, iw)
    left, right = (ia, iw - 1), (ia, iw + 1)
    sides = ((has_l, left), (has_r, right))
    ends = ((has_u, up), (has_d, down))
    crossed = (ia == half_a, ia == half_a - 1)

    parity, ring, rings = iw % 2, iw // 2, size_w // 2
    out = 2 * parity - 1
    shared = jnp.where(parity == 1, ring + 1, rings - ring)
    carried = jnp.where(parity == 1, ring, rings - 1 - ring)
    middle = (ia >= half_a - 2) & (ia < half_a + 2)

    def chosen(k, part, fewer):
        n = part * HEADS // rings - jnp.where(middle & (part > 0), fewer, 0)
        return (k * n) % HEADS >= HEADS - n

    def relayed_col(h, part):
        return chosen(h, part, jnp.where(part >= 2, 1, 0))

    def relayed_grad(h, part):
        return chosen(HEADS - 1 - h, part, jnp.where(part >= 3, 2, 1))

    def lanes(h):
        return pl.ds(pl.multiple_of(h * D, D), D)

    loads = [
        pltpu.make_async_copy(src, dst, in_sem.at[n])
        for n, (src, dst) in enumerate(((k_in, k_own), (v_in, v_own), (q_in, q_own), (g_in, g_own)))
    ]

    def remote(src, dst, ss, rs, dev):
        return pltpu.make_async_remote_copy(
            src_ref=src, dst_ref=dst, send_sem=ss, recv_sem=rs, device_id=dev, device_id_type=MESH
        )

    def col_copy(h, s, dev):
        lo = 6 - 6 * s
        return remote(
            pack.at[h, :, 2 * s : 2 * s + 2], kall.at[h, :, lo : lo + 2, 1:4], ss1.at[h, s], rs1.at[h, 1 - s], dev
        )

    def row_place(s, j):
        moved = crossed[s] & sides[j // 2][0]
        col = jnp.where(moved, iw + (2 * (j // 2) - 1), iw)
        return jnp.where(moved, (j + 2) % 4, j), (ia + (2 * s - 1), col)

    def row_there(s, j):
        return ends[s][0] if j in (1, 2) else ends[s][0] & sides[j // 2][0]

    def row_copy(h, s, j):
        slot, dev = row_place(s, j)
        src = pack.at[h, :, 2 * j - 2 : 2 * j, 2 * s] if j in (1, 2) else kall.at[h, :, 2 * j : 2 * j + 2, 1 + 2 * s]
        dst = kall.at[h, :, pl.ds(2 * slot, 2), 4 - 4 * s]
        return remote(src, dst, ss2.at[h, s, j], rs2.at[h, 1 - s, slot], dev)

    def send_rows(h, columns):
        for s in range(2):
            for j in columns:

                @pl.when(row_there(s, j))
                def _():
                    row_copy(h, s, j).start()

    def receive_row(h, s, j):
        @pl.when(row_there(s, j))
        def _():
            ref = kall.at[h, :, 2 * j : 2 * j + 2, 4 * s]
            remote(ref, ref, ss2.at[h, s, j], rs2.at[h, s, j], ends[s][1]).wait_recv()

    def grad_row_copy(h, s, half):
        moved = crossed[s] & sides[half][0]
        col = jnp.where(moved, iw + (2 * half - 1), iw)
        to = jnp.where(moved, 1 - half, half)
        return remote(
            g3s.at[h, s, half], g3r.at[h, 1 - s, to], ss3.at[h, s, half], rs3.at[h, 1 - s, to], (ia + (2 * s - 1), col)
        )

    def col_relay_in(h, s):
        return remote(pack.at[h, :, 2 * s : 2 * s + 2], r1.at[h], ss1.at[h, s], ri1.at[h], (ia, iw + 2 * out))

    def col_relay_out(h):
        dst = kall.at[h, :, pl.ds(6 - 6 * parity, 2), 1:4]
        return remote(r1.at[h], dst, ro1.at[h], rs1.at[h, 1 - parity], (ia, iw - out))

    def grad_relay_in(h, s):
        return remote(g4s.at[h, s], r4.at[h], ss4.at[h, s], ri4.at[h], (ia, iw + 2 * out))

    def grad_relay_out(h):
        return remote(r4.at[h], g4r.at[h, 1 - parity], ro4.at[h], rs4.at[h, 1 - parity], (ia, iw - out))

    def grad_col_copy(h, s, dev):
        return remote(g4s.at[h, s], g4r.at[h, 1 - s], ss4.at[h, s], rs4.at[h, 1 - s], dev)

    def send(direct, by_relay, relayed, h):
        for s, (there, dev) in enumerate(sides):
            through = (parity == s) & relayed(h, shared)

            @pl.when(there & through)
            def _():
                by_relay(h, s).start()

            @pl.when(there & jnp.logical_not(through))
            def _():
                direct(h, s, dev).start()

    def relay_col(h):
        @pl.when(relayed_col(h, carried))
        def _():
            remote(r1.at[h], r1.at[h], ro1.at[h], ri1.at[h], (ia, iw - out)).wait_recv()
            col_relay_out(h).start()

    def relay_grad(h):
        @pl.when(relayed_grad(h, carried))
        def _():
            remote(r4.at[h], r4.at[h], ro4.at[h], ri4.at[h], (ia, iw - out)).wait_recv()
            grad_relay_out(h).start()

    def receive(copy, h, group, s):
        there, dev = group[s]

        @pl.when(there)
        def _():
            copy(h, 1 - s, dev).wait_recv()

    def loop(body):
        lax.fori_loop(0, HEADS, lambda h, c: (body(h), c)[1], 0)

    for load in loads:
        load.start()

    barrier = pltpu.get_barrier_semaphore()
    greeted = sides + ends
    for s, row in ((0, ia - 1), (1, ia + 1)):
        greeted += ((crossed[s] & has_l, (row, iw - 1)), (crossed[s] & has_r, (row, iw + 1)))
    greeted += ((iw >= 2, (ia, iw - 2)), (iw < size_w - 2, (ia, iw + 2)))
    for there, dev in greeted:

        @pl.when(there)
        def _():
            pl.semaphore_signal(barrier, inc=1, device_id=dev, device_id_type=MESH)

    def packed_of(i):
        return ((i >> 2) & 1) * 64 + (i >> 5) * 16 + ((i >> 3) & 3) * 4 + (i & 3)

    first = lax.broadcasted_iota(jnp.int32, (128, 128), 0)
    second = lax.broadcasted_iota(jnp.int32, (128, 128), 1)
    perm[...] = jnp.where(packed_of(first) == second, 1.0, 0.0).astype(BF16)
    perm_t[...] = jnp.where(packed_of(second) == first, 1.0, 0.0).astype(BF16)

    for s, (there, _) in enumerate(sides):

        @pl.when(jnp.logical_not(there))
        def _():
            def fill(h):
                kall[h, :, 6 * s : 6 * s + 2] = jnp.zeros((2, 2, 5, 32, D), BF16)
                g4r[h, s] = jnp.zeros((2, 2, 3, 32, D), BF16)

            loop(fill)

    for s, (there, _) in enumerate(ends):

        @pl.when(jnp.logical_not(there))
        def _():
            def fill(h):
                kall[h, :, :, 4 * s] = jnp.zeros((2, 8, 32, D), BF16)

            loop(fill)

    count = sum(there.astype(jnp.int32) for there, _ in greeted)
    pl.semaphore_wait(barrier, count)

    def send_cols(h):
        send(col_copy, col_relay_in, relayed_col, h)

    def begin(h):
        pack_edges(h)

        @pl.when(even)
        def _():
            send_cols(h)

        send_rows(h, (1, 2))

        @pl.when(jnp.logical_not(even))
        def _():
            send_cols(h)

    def permute(matrix, x, y):
        z = dot(matrix[...], jnp.concatenate([x, y], axis=1), 1, 0)
        return z[:, :D], z[:, D:]

    loads[0].wait()
    loads[1].wait()

    def pack_edges(h):
        for a in range(3):
            x = [own[:, a, :, lanes(h)] for own in (k_own, v_own)]
            kall[h, 0, 2:6, a + 1] = x[0]
            kall[h, 1, 2:6, a + 1] = x[1]
            y = permute(perm_t, x[0].reshape(128, D), x[1].reshape(128, D))
            pack[h, 0, :, a] = y[0].astype(BF16).reshape(4, 32, D)
            pack[h, 1, :, a] = y[1].astype(BF16).reshape(4, 32, D)

    for h in range(3):
        begin(h)

    shape = (6, 3, 32, 128)
    unit = lax.broadcasted_iota(jnp.int32, shape, 0)
    drow = lax.broadcasted_iota(jnp.int32, shape, 1) - 1
    token = lax.broadcasted_iota(jnp.int32, shape, 2)
    query = lax.broadcasted_iota(jnp.int32, shape, 3)
    qcol = (query >> 2) & 1
    for a in range(3):
        own_col = (token >> 2) & 1
        if a != 1:
            own_col = jnp.where(drow == a - 1, unit >> 1, own_col)
        kcol = jnp.where(unit < 4, own_col, 3 * qcol - 1)
        dcol = kcol - qcol
        acol = iw * 2 + kcol
        in_cols = (acol >= 0) & (acol < 2 * size_w)

        def of(n):
            return jnp.where(qcol == 0, reach[a, 0, n], reach[a, 1, n])

        arow = ia * 3 + a + drow
        ok = in_cols & (arow >= 0) & (arow < 3 * size_a)
        ok = ok & (drow >= -of(0)) & (drow <= of(1)) & (dcol >= -of(2)) & (dcol <= of(3))
        bias[a] = jnp.where(ok, 0.0, NEGATIVE).astype(F32).reshape(576, 128)

    def forward(h):
        receive(col_copy, h, sides, 0)
        receive(col_copy, h, sides, 1)
        send_rows(h, (0, 3))

    left_query = ((lax.broadcasted_iota(jnp.int32, (128, D), 0) >> 2) & 1) == 0
    none = jnp.zeros((128, D), BF16)

    def attend(h, a):
        def keys(kv, lo, hi):
            return kall[h, kv, lo:hi, a : a + 3].reshape((hi - lo) * 96, D)

        def halo(kv):
            return jnp.concatenate([keys(kv, 0, 2), keys(kv, 6, 8)], axis=1)

        def by_side(x):
            return jnp.concatenate([jnp.where(left_query, x, none), jnp.where(left_query, none, x)], axis=1)

        def own_side(x):
            return jnp.where(left_query, x[:, :D], x[:, D:])

        k_mid, v_mid, k_halo, v_halo = keys(0, 2, 6), keys(1, 2, 6), halo(0), halo(1)
        q = q_own[:, a, :, lanes(h)].reshape(128, D)
        g = g_own[:, a, :, lanes(h)].reshape(128, D)
        both = jnp.concatenate([jnp.concatenate([q, none], axis=1), jnp.concatenate([none, g], axis=1)], axis=0)
        q_side, g_side = by_side(q), by_side(g)
        mid = dot(jnp.concatenate([k_mid, v_mid], axis=1), both, 1, 1)
        s = jnp.concatenate([mid[:, :128], dot(k_halo, q_side, 1, 1)], axis=0)
        dp = jnp.concatenate([mid[:, 128:], dot(v_halo, g_side, 1, 1)], axis=0)
        s = s * (SCALE * LOG2E) + bias[a]
        p = jnp.exp2(s - jnp.max(s, axis=0, keepdims=True))
        p = p * (1.0 / jnp.sum(p, axis=0, keepdims=True))
        low = p.astype(BF16)
        t = p * dp
        ds = (t - p * jnp.sum(t, axis=0, keepdims=True)).astype(BF16)
        o = dot(low[:384], v_mid, 0, 0) + own_side(dot(low[384:], v_halo, 0, 0))
        dq = dot(ds[:384], k_mid, 0, 0) + own_side(dot(ds[384:], k_halo, 0, 0))
        o_out[:, a, :, lanes(h)] = o.astype(BF16).reshape(4, 32, D)
        dq_out[:, a, :, lanes(h)] = (dq * SCALE).astype(BF16).reshape(4, 32, D)
        mid = dot(jnp.concatenate([ds[:384], low[:384]], axis=1), both, 1, 0)
        sums = ((mid[:, :D], dot(ds[384:], q_side, 1, 0)), (mid[:, D:], dot(low[384:], g_side, 1, 0)))
        for kv, (own, beside) in enumerate(sums):
            own = own.reshape(4, 3, 32, D)
            two = (beside[:, :D].reshape(2, 3, 32, D), beside[:, D:].reshape(2, 3, 32, D))
            for i in range(3):
                row = a + i - 1
                if row in (-1, 3):
                    end = 0 if row < 0 else 1
                    g3s[h, end, 0, kv, 0:2] = two[0][:, i].astype(BF16)
                    g3s[h, end, 0, kv, 2:4] = own[0:2, i].astype(BF16)
                    g3s[h, end, 1, kv, 0:2] = own[2:4, i].astype(BF16)
                    g3s[h, end, 1, kv, 2:4] = two[1][:, i].astype(BF16)
                elif row > a or a == 0:
                    acc[h, kv, 0:2, row] = two[0][:, i]
                    acc[h, kv, 2:6, row] = own[:, i]
                    acc[h, kv, 6:8, row] = two[1][:, i]
                else:
                    acc[h, kv, 0:2, row] += two[0][:, i]
                    acc[h, kv, 2:6, row] += own[:, i]
                    acc[h, kv, 6:8, row] += two[1][:, i]

    def send_grad_rows(h, s):
        @pl.when(ends[s][0])
        def _():
            for half in range(2):
                grad_row_copy(h, s, half).start()

    def reduce_rows(h):
        for s in range(2):
            row = 2 * s

            @pl.when(ends[s][0])
            def _():
                for half in range(2):
                    ref = g3r.at[h, s, half]
                    remote(ref, ref, ss3.at[h, s, half], rs3.at[h, s, half], ends[s][1]).wait_recv()
                acc[h, :, 0:2, row] += g3r[h, s, 0, :, 0:2].astype(F32)
                acc[h, :, 6:8, row] += g3r[h, s, 1, :, 2:4].astype(F32)
                x = [jnp.concatenate([g3r[h, s, 0, kv, 2:4], g3r[h, s, 1, kv, 0:2]]).reshape(128, D) for kv in range(2)]
                for kv, y in enumerate(permute(perm, x[0], x[1])):
                    acc[h, kv, 2:6, row] += y.reshape(4, 32, D)

        for s in range(2):
            g4s[h, s] = acc[h, :, 6 * s : 6 * s + 2].astype(BF16)
        send(grad_col_copy, grad_relay_in, relayed_grad, h)

    def finish(h):
        for s in range(2):
            receive(grad_col_copy, h, sides, s)
        for a in range(3):
            x = [g4r[h, :, kv, :, a].reshape(128, D) for kv in range(2)]
            y = permute(perm, x[0], x[1])
            dk = (y[0].reshape(4, 32, D) + acc[h, 0, 2:6, a]) * SCALE
            dv = y[1].reshape(4, 32, D) + acc[h, 1, 2:6, a]
            dk_out[:, a, :, lanes(h)] = dk.astype(BF16)
            dv_out[:, a, :, lanes(h)] = dv.astype(BF16)

    for h in range(RELAY_AHEAD):
        relay_col(h)
        if h < CORNERS_AHEAD:
            forward(h)
        if h + 3 < AHEAD:
            begin(h + 3)

    loads[2].wait()
    loads[3].wait()

    def columns(h, behind):
        @pl.when(h + RELAY_AHEAD < HEADS)
        def _():
            relay_col(h + RELAY_AHEAD)

        @pl.when(h + AHEAD < HEADS)
        def _():
            send_cols(h + AHEAD)

        @pl.when(h >= behind)
        def _():
            reduce_rows(h - behind)

        @pl.when(h >= behind + 2)
        def _():
            relay_grad(h - behind - 2)

    def step(h):
        @pl.when(h + AHEAD < HEADS)
        def _():
            pack_edges(h + AHEAD)

        @pl.when(even)
        def _():
            columns(h, ROWS_BEHIND + 1)

        @pl.when(h + CORNERS_AHEAD < HEADS)
        def _():
            forward(h + CORNERS_AHEAD)

        @pl.when(h + AHEAD < HEADS)
        def _():
            send_rows(h + AHEAD, (1, 2))

        for a in range(3):
            if a != 1:
                for j in range(4):
                    receive_row(h, a // 2, j)
            attend(h, a)
            if a != 1:
                send_grad_rows(h, a // 2)

        @pl.when(jnp.logical_not(even))
        def _():
            columns(h, ROWS_BEHIND)

        @pl.when(h >= BEHIND)
        def _():
            finish(h - BEHIND)

    loop(step)

    @pl.when(even)
    def _():
        reduce_rows(HEADS - ROWS_BEHIND - 1)
        relay_grad(HEADS - ROWS_BEHIND - 3)

    for h in range(HEADS - ROWS_BEHIND, HEADS):
        reduce_rows(h)
    for h in range(HEADS - ROWS_BEHIND - 2, HEADS):
        relay_grad(h)
    for h in range(HEADS - BEHIND, HEADS):
        finish(h)

    def drain(h):
        @pl.when(relayed_col(h, carried))
        def _():
            col_relay_out(h).wait_send()

        @pl.when(relayed_grad(h, carried))
        def _():
            grad_relay_out(h).wait_send()

        for copy in (col_copy, grad_col_copy):
            for s, (there, dev) in enumerate(sides):

                @pl.when(there)
                def _():
                    copy(h, s, dev).wait_send()

        for s in range(2):
            for j in range(4):

                @pl.when(row_there(s, j))
                def _():
                    row_copy(h, s, j).wait_send()

            @pl.when(ends[s][0])
            def _():
                for half in range(2):
                    grad_row_copy(h, s, half).wait_send()

    loop(drain)


def write_out(*refs):
    sources, outs, sem = refs[:4], refs[4:8], refs[8]
    copies = [pltpu.make_async_copy(x.at[f], y.at[f], sem.at[n, f]) for n, (x, y) in enumerate(zip(sources, outs)) for f in range(4)]
    for copy in copies:
        copy.start()
    for copy in copies:
        copy.wait()


def per_device(size_a, size_w, queries, key_heads, value_heads, out_grad, reach_tiles):
    shape = queries.shape
    ins = [x.reshape(4, 3, 32, HEADS * D) for x in (queries, key_heads, value_heads, out_grad)]
    ins = [pltpu.with_memory_space_constraint(x, pltpu.HBM) for x in ins]
    any_spec = pl.BlockSpec(memory_space=pl.ANY)
    pair = pltpu.SemaphoreType.DMA((HEADS, 2))
    results = pl.pallas_call(
        functools.partial(kernel, size_a, size_w),
        out_shape=[pltpu.VMEM((4, 3, 32, HEADS * D), BF16)] * 4,
        in_specs=[pl.BlockSpec(memory_space=pltpu.SMEM)] + [any_spec] * 4,
        out_specs=[pl.BlockSpec(memory_space=pltpu.VMEM)] * 4,
        scratch_shapes=[
            pltpu.VMEM((HEADS, 2, 8, 5, 32, D), BF16),
            pltpu.VMEM((4, 3, 32, HEADS * D), BF16),
            pltpu.VMEM((4, 3, 32, HEADS * D), BF16),
            pltpu.VMEM((4, 3, 32, HEADS * D), BF16),
            pltpu.VMEM((4, 3, 32, HEADS * D), BF16),
            pltpu.VMEM((HEADS, 2, 4, 3, 32, D), BF16),
            pltpu.VMEM((HEADS, 2, 8, 3, 32, D), F32),
            pltpu.VMEM((HEADS, 2, 2, 2, 4, 32, D), BF16),
            pltpu.VMEM((HEADS, 2, 2, 2, 4, 32, D), BF16),
            pltpu.VMEM((HEADS, 2, 2, 2, 3, 32, D), BF16),
            pltpu.VMEM((HEADS, 2, 2, 2, 3, 32, D), BF16),
            pltpu.VMEM((HEADS, 2, 2, 3, 32, D), BF16),
            pltpu.VMEM((HEADS, 2, 2, 3, 32, D), BF16),
            pltpu.VMEM((3, 576, 128), F32),
            pltpu.VMEM((128, 128), BF16),
            pltpu.VMEM((128, 128), BF16),
            pltpu.SemaphoreType.DMA((4,)),
        ]
        + [pair] * 2
        + [pltpu.SemaphoreType.DMA((HEADS, 2, 4))] * 2
        + [pltpu.SemaphoreType.DMA((HEADS, 2, 2))] * 2
        + [pair] * 2
        + [pltpu.SemaphoreType.DMA((HEADS,))] * 4,
        compiler_params=pltpu.CompilerParams(
            collective_id=0, has_side_effects=True, vmem_limit_bytes=56 * 1024 * 1024
        ),
    )(reach_tiles, *ins)
    outs = pl.pallas_call(
        write_out,
        out_shape=[jax.ShapeDtypeStruct((4, 3, 32, HEADS * D), BF16)] * 4,
        in_specs=[pl.BlockSpec(memory_space=pltpu.VMEM)] * 4,
        out_specs=[any_spec] * 4,
        scratch_shapes=[pltpu.SemaphoreType.DMA((4, 4))],
        compiler_params=pltpu.CompilerParams(vmem_limit_bytes=8 * 1024 * 1024),
    )(*(pltpu.with_memory_space_constraint(x, pltpu.VMEM) for x in results))
    return tuple(x.reshape(shape) for x in outs)


def solution(mesh):
    spec = P(None, "ha", "wa", None)
    return jax.shard_map(
        functools.partial(per_device, mesh.shape["ha"], mesh.shape["wa"]),
        mesh=mesh,
        in_specs=(spec, spec, spec, spec, P("ha", "wa", None)),
        out_specs=(spec, spec, spec, spec),
        check_vma=False,
    )
```

```python
import functools
import math

import jax
import jax.numpy as jnp
from jax import lax
from jax.experimental import pallas as pl
from jax.experimental.pallas import tpu as pltpu
from jax.sharding import PartitionSpec as P

HEADS = 12
TS = 4
D = 128
MESH = pl.DeviceIdType.MESH
AHEAD = 7
RELAY_AHEAD = 5
CORNERS_AHEAD = 3
ROWS_BEHIND = 2
RELAY_BEHIND = 4
BEHIND = 6
NEGATIVE = -1e30
SCALE = 1.0 / math.sqrt(D)
LOG2E = 1.4426950408889634

F32 = jnp.float32
BF16 = jnp.bfloat16


def dot(a, b, ca, cb):
    return lax.dot_general(a, b, (((ca,), (cb,)), ((), ())), preferred_element_type=F32)


def kernel(
    size_a, size_w, reach, q_in, k_in, v_in, g_in, o_out, dq_out, dk_out, dv_out,
    kall, k_own, v_own, q_own, g_own, pack, acc, g3s, g3r, g4s, g4r, r1, r4, bias, perm, perm_t,
    in_sem, ss1, rs1, ss2, rs2, ss3, rs3, ss4, rs4, ri1, ro1, ri4, ro4,
):
    half_a = size_a // 2
    ia = lax.axis_index("ha")
    iw = lax.axis_index("wa")
    has_u, has_d = ia > 0, ia < size_a - 1
    has_l, has_r = iw > 0, iw < size_w - 1
    up, down = (ia - 1, iw), (ia + 1, iw)
    left, right = (ia, iw - 1), (ia, iw + 1)
    sides = ((has_l, left), (has_r, right))
    ends = ((has_u, up), (has_d, down))
    crossed = (ia == half_a, ia == half_a - 1)

    parity, ring, rings = iw % 2, iw // 2, size_w // 2
    out = 2 * parity - 1
    shared = jnp.where(parity == 1, ring + 1, rings - ring)
    carried = jnp.where(parity == 1, ring, rings - 1 - ring)
    middle = (ia >= half_a - 2) & (ia < half_a + 2)

    def chosen(k, part, fewer):
        n = part * HEADS // rings - jnp.where(middle & (part > 0), fewer, 0)
        return (k * n) % HEADS >= HEADS - n

    def relayed_col(h, part):
        return chosen(h, part, jnp.where(part >= 2, 1, 0))

    def relayed_grad(h, part):
        return chosen(HEADS - 1 - h, part, jnp.where(part >= 3, 2, 1))

    def lanes(h):
        return pl.ds(pl.multiple_of(h * D, D), D)

    loads = [
        pltpu.make_async_copy(src, dst, in_sem.at[n])
        for n, (src, dst) in enumerate(((k_in, k_own), (v_in, v_own), (q_in, q_own), (g_in, g_own)))
    ]

    def remote(src, dst, ss, rs, dev):
        return pltpu.make_async_remote_copy(
            src_ref=src, dst_ref=dst, send_sem=ss, recv_sem=rs, device_id=dev, device_id_type=MESH
        )

    def col_copy(h, s, dev):
        lo = 6 - 6 * s
        return remote(
            pack.at[h, :, 2 * s : 2 * s + 2], kall.at[h, :, lo : lo + 2, 1:4], ss1.at[h, s], rs1.at[h, 1 - s], dev
        )

    def row_place(s, j):
        moved = crossed[s] & sides[j // 2][0]
        col = jnp.where(moved, iw + (2 * (j // 2) - 1), iw)
        return jnp.where(moved, (j + 2) % 4, j), (ia + (2 * s - 1), col)

    def row_there(s, j):
        return ends[s][0] if j in (1, 2) else ends[s][0] & sides[j // 2][0]

    def row_copy(h, s, j):
        slot, dev = row_place(s, j)
        src = pack.at[h, :, 2 * j - 2 : 2 * j, 2 * s] if j in (1, 2) else kall.at[h, :, 2 * j : 2 * j + 2, 1 + 2 * s]
        dst = kall.at[h, :, pl.ds(2 * slot, 2), 4 - 4 * s]
        return remote(src, dst, ss2.at[h, s, j], rs2.at[h, 1 - s, slot], dev)

    def send_rows(h, columns):
        for s in range(2):
            for j in columns:

                @pl.when(row_there(s, j))
                def _():
                    row_copy(h, s, j).start()

    def receive_row(h, s, j):
        @pl.when(row_there(s, j))
        def _():
            ref = kall.at[h, :, 2 * j : 2 * j + 2, 4 * s]
            remote(ref, ref, ss2.at[h, s, j], rs2.at[h, s, j], ends[s][1]).wait_recv()

    def alone(s, half):
        return crossed[s] & jnp.logical_not(sides[half][0])

    def part_of(ref, half):
        return ref.at[:, 2 - 2 * half : 4 - 2 * half]

    def lone_row_copy(h, s, half):
        return remote(
            part_of(g3s.at[h, s, half], half), part_of(g3r.at[h, 1 - s, half], half),
            ss3.at[h, s, half], rs3.at[h, 1 - s, half], ends[s][1],
        )

    def for_grad_rows(s, lone, full):
        for half in range(2):

            @pl.when(ends[s][0] & alone(s, half))
            def _():
                lone(half)

            @pl.when(ends[s][0] & jnp.logical_not(alone(s, half)))
            def _():
                full(half)

    def grad_row_copy(h, s, half):
        moved = crossed[s] & sides[half][0]
        col = jnp.where(moved, iw + (2 * half - 1), iw)
        to = jnp.where(moved, 1 - half, half)
        return remote(
            g3s.at[h, s, half], g3r.at[h, 1 - s, to], ss3.at[h, s, half], rs3.at[h, 1 - s, to], (ia + (2 * s - 1), col)
        )

    def col_relay_in(h, s):
        return remote(pack.at[h, :, 2 * s : 2 * s + 2], r1.at[h], ss1.at[h, s], ri1.at[h], (ia, iw + 2 * out))

    def col_relay_out(h):
        dst = kall.at[h, :, pl.ds(6 - 6 * parity, 2), 1:4]
        return remote(r1.at[h], dst, ro1.at[h], rs1.at[h, 1 - parity], (ia, iw - out))

    def grad_relay_in(h, s):
        return remote(g4s.at[h, s], r4.at[h], ss4.at[h, s], ri4.at[h], (ia, iw + 2 * out))

    def grad_relay_out(h):
        return remote(r4.at[h], g4r.at[h, 1 - parity], ro4.at[h], rs4.at[h, 1 - parity], (ia, iw - out))

    def grad_col_copy(h, s, dev):
        return remote(g4s.at[h, s], g4r.at[h, 1 - s], ss4.at[h, s], rs4.at[h, 1 - s], dev)

    def send(direct, by_relay, relayed, h):
        for s, (there, dev) in enumerate(sides):
            through = (parity == s) & relayed(h, shared)

            @pl.when(there & through)
            def _():
                by_relay(h, s).start()

            @pl.when(there & jnp.logical_not(through))
            def _():
                direct(h, s, dev).start()

    def relay_col(h):
        @pl.when(relayed_col(h, carried))
        def _():
            remote(r1.at[h], r1.at[h], ro1.at[h], ri1.at[h], (ia, iw - out)).wait_recv()
            col_relay_out(h).start()

    def relay_grad(h):
        @pl.when(relayed_grad(h, carried))
        def _():
            remote(r4.at[h], r4.at[h], ro4.at[h], ri4.at[h], (ia, iw - out)).wait_recv()
            grad_relay_out(h).start()

    def receive(copy, h, group, s):
        there, dev = group[s]

        @pl.when(there)
        def _():
            copy(h, 1 - s, dev).wait_recv()

    def loop(body):
        lax.fori_loop(0, HEADS, lambda h, c: (body(h), c)[1], 0)

    for load in loads:
        load.start()

    barrier = pltpu.get_barrier_semaphore()
    greeted = sides + ends
    for s, row in ((0, ia - 1), (1, ia + 1)):
        greeted += ((crossed[s] & has_l, (row, iw - 1)), (crossed[s] & has_r, (row, iw + 1)))
    greeted += ((iw >= 2, (ia, iw - 2)), (iw < size_w - 2, (ia, iw + 2)))
    for there, dev in greeted:

        @pl.when(there)
        def _():
            pl.semaphore_signal(barrier, inc=1, device_id=dev, device_id_type=MESH)

    def packed_of(i):
        return ((i >> 2) & 1) * 64 + (i >> 5) * 16 + ((i >> 3) & 3) * 4 + (i & 3)

    first = lax.broadcasted_iota(jnp.int32, (128, 128), 0)
    second = lax.broadcasted_iota(jnp.int32, (128, 128), 1)
    perm[...] = jnp.where(packed_of(first) == second, 1.0, 0.0).astype(BF16)
    perm_t[...] = jnp.where(packed_of(second) == first, 1.0, 0.0).astype(BF16)

    for s, (there, _) in enumerate(sides):

        @pl.when(jnp.logical_not(there))
        def _():
            def fill(h):
                kall[h, :, 6 * s : 6 * s + 2] = jnp.zeros((2, 2, 5, 32, D), BF16)
                g4r[h, s] = jnp.zeros((2, 2, 3, 32, D), BF16)

            loop(fill)

    for s, (there, _) in enumerate(ends):

        @pl.when(jnp.logical_not(there))
        def _():
            def fill(h):
                kall[h, :, :, 4 * s] = jnp.zeros((2, 8, 32, D), BF16)

            loop(fill)

    count = sum(there.astype(jnp.int32) for there, _ in greeted)
    pl.semaphore_wait(barrier, count)

    def permute(matrix, x, y):
        z = dot(matrix[...], jnp.concatenate([x, y], axis=1), 1, 0)
        return z[:, :D], z[:, D:]

    loads[0].wait()
    loads[1].wait()

    def send_edges(h):
        for a in range(3):
            x = [own[:, a, :, lanes(h)] for own in (k_own, v_own)]
            kall[h, 0, 2:6, a + 1] = x[0]
            kall[h, 1, 2:6, a + 1] = x[1]
            y = permute(perm_t, x[0].reshape(128, D), x[1].reshape(128, D))
            pack[h, 0, :, a] = y[0].astype(BF16).reshape(4, 32, D)
            pack[h, 1, :, a] = y[1].astype(BF16).reshape(4, 32, D)
        send_rows(h, (1, 2))
        send(col_copy, col_relay_in, relayed_col, h)

    for h in range(3):
        send_edges(h)

    shape = (6, 3, 32, 128)
    unit = lax.broadcasted_iota(jnp.int32, shape, 0)
    drow = lax.broadcasted_iota(jnp.int32, shape, 1) - 1
    token = lax.broadcasted_iota(jnp.int32, shape, 2)
    query = lax.broadcasted_iota(jnp.int32, shape, 3)
    qcol = (query >> 2) & 1
    for a in range(3):
        own_col = (token >> 2) & 1
        if a != 1:
            own_col = jnp.where(drow == a - 1, unit >> 1, own_col)
        kcol = jnp.where(unit < 4, own_col, 3 * qcol - 1)
        dcol = kcol - qcol
        acol = iw * 2 + kcol
        in_cols = (acol >= 0) & (acol < 2 * size_w)

        def of(n):
            return jnp.where(qcol == 0, reach[a, 0, n], reach[a, 1, n])

        arow = ia * 3 + a + drow
        ok = in_cols & (arow >= 0) & (arow < 3 * size_a)
        ok = ok & (drow >= -of(0)) & (drow <= of(1)) & (dcol >= -of(2)) & (dcol <= of(3))
        bias[a] = jnp.where(ok, 0.0, NEGATIVE).astype(F32).reshape(576, 128)

    def forward(h):
        receive(col_copy, h, sides, 0)
        receive(col_copy, h, sides, 1)
        send_rows(h, (0, 3))

    left_query = ((lax.broadcasted_iota(jnp.int32, (128, D), 0) >> 2) & 1) == 0
    none = jnp.zeros((128, D), BF16)

    def attend(h, a):
        def keys(kv, lo, hi):
            return kall[h, kv, lo:hi, a : a + 3].reshape((hi - lo) * 96, D)

        def halo(kv):
            return jnp.concatenate([keys(kv, 0, 2), keys(kv, 6, 8)], axis=1)

        def by_side(x):
            return jnp.concatenate([jnp.where(left_query, x, none), jnp.where(left_query, none, x)], axis=1)

        def own_side(x):
            return jnp.where(left_query, x[:, :D], x[:, D:])

        k_mid, v_mid, k_halo, v_halo = keys(0, 2, 6), keys(1, 2, 6), halo(0), halo(1)
        q = q_own[:, a, :, lanes(h)].reshape(128, D)
        g = g_own[:, a, :, lanes(h)].reshape(128, D)
        both = jnp.concatenate([jnp.concatenate([q, none], axis=1), jnp.concatenate([none, g], axis=1)], axis=0)
        q_side, g_side = by_side(q), by_side(g)
        mid = dot(jnp.concatenate([k_mid, v_mid], axis=1), both, 1, 1)
        s = jnp.concatenate([mid[:, :128], dot(k_halo, q_side, 1, 1)], axis=0)
        dp = jnp.concatenate([mid[:, 128:], dot(v_halo, g_side, 1, 1)], axis=0)
        s = s * (SCALE * LOG2E) + bias[a]
        p = jnp.exp2(s - jnp.max(s, axis=0, keepdims=True))
        p = p * (1.0 / jnp.sum(p, axis=0, keepdims=True))
        low = p.astype(BF16)
        t = p * dp
        ds = (t - p * jnp.sum(t, axis=0, keepdims=True)).astype(BF16)
        o = dot(low[:384], v_mid, 0, 0) + own_side(dot(low[384:], v_halo, 0, 0))
        dq = dot(ds[:384], k_mid, 0, 0) + own_side(dot(ds[384:], k_halo, 0, 0))
        o_out[:, a, :, lanes(h)] = o.astype(BF16).reshape(4, 32, D)
        dq_out[:, a, :, lanes(h)] = (dq * SCALE).astype(BF16).reshape(4, 32, D)
        mid = dot(jnp.concatenate([ds[:384], low[:384]], axis=1), both, 1, 0)
        sums = ((mid[:, :D], dot(ds[384:], q_side, 1, 0)), (mid[:, D:], dot(low[384:], g_side, 1, 0)))
        for kv, (own, beside) in enumerate(sums):
            own = own.reshape(4, 3, 32, D)
            two = (beside[:, :D].reshape(2, 3, 32, D), beside[:, D:].reshape(2, 3, 32, D))
            for i in range(3):
                row = a + i - 1
                if row in (-1, 3):
                    end = 0 if row < 0 else 1
                    g3s[h, end, 0, kv, 0:2] = two[0][:, i].astype(BF16)
                    g3s[h, end, 0, kv, 2:4] = own[0:2, i].astype(BF16)
                    g3s[h, end, 1, kv, 0:2] = own[2:4, i].astype(BF16)
                    g3s[h, end, 1, kv, 2:4] = two[1][:, i].astype(BF16)
                elif row > a or a == 0:
                    acc[h, kv, 0:2, row] = two[0][:, i]
                    acc[h, kv, 2:6, row] = own[:, i]
                    acc[h, kv, 6:8, row] = two[1][:, i]
                else:
                    acc[h, kv, 0:2, row] += two[0][:, i]
                    acc[h, kv, 2:6, row] += own[:, i]
                    acc[h, kv, 6:8, row] += two[1][:, i]

    def send_grad_rows(h, s):
        for_grad_rows(s, lambda half: lone_row_copy(h, s, half).start(), lambda half: grad_row_copy(h, s, half).start())

    def reduce_rows(h):
        for s in range(2):
            row = 2 * s

            def arrived(half, ref):
                remote(ref, ref, ss3.at[h, s, half], rs3.at[h, s, half], ends[s][1]).wait_recv()

            for_grad_rows(
                s,
                lambda half: arrived(half, part_of(g3r.at[h, s, half], half)),
                lambda half: arrived(half, g3r.at[h, s, half]),
            )
            for half, (there, _) in enumerate(sides):

                @pl.when(ends[s][0] & there)
                def _():
                    units = slice(6 * half, 6 * half + 2)
                    acc[h, :, units, row] += g3r[h, s, half, :, 2 * half : 2 * half + 2].astype(F32)

            @pl.when(ends[s][0])
            def _():
                x = [jnp.concatenate([g3r[h, s, 0, kv, 2:4], g3r[h, s, 1, kv, 0:2]]).reshape(128, D) for kv in range(2)]
                for kv, y in enumerate(permute(perm, x[0], x[1])):
                    acc[h, kv, 2:6, row] += y.reshape(4, 32, D)

        for s in range(2):
            g4s[h, s] = acc[h, :, 6 * s : 6 * s + 2].astype(BF16)
        send(grad_col_copy, grad_relay_in, relayed_grad, h)

    def finish(h):
        for s in range(2):
            receive(grad_col_copy, h, sides, s)
        for a in range(3):
            x = [g4r[h, :, kv, :, a].reshape(128, D) for kv in range(2)]
            y = permute(perm, x[0], x[1])
            dk = (y[0].reshape(4, 32, D) + acc[h, 0, 2:6, a]) * SCALE
            dv = y[1].reshape(4, 32, D) + acc[h, 1, 2:6, a]
            dk_out[:, a, :, lanes(h)] = dk.astype(BF16)
            dv_out[:, a, :, lanes(h)] = dv.astype(BF16)

    for h in range(RELAY_AHEAD):
        relay_col(h)
        if h < CORNERS_AHEAD:
            forward(h)
        if h + 3 < AHEAD:
            send_edges(h + 3)

    loads[2].wait()
    loads[3].wait()

    def step(h):
        @pl.when(h + CORNERS_AHEAD < HEADS)
        def _():
            forward(h + CORNERS_AHEAD)

        @pl.when(h + RELAY_AHEAD < HEADS)
        def _():
            relay_col(h + RELAY_AHEAD)

        @pl.when(h + AHEAD < HEADS)
        def _():
            send_edges(h + AHEAD)

        for a in range(3):
            if a != 1:
                for j in range(4):
                    receive_row(h, a // 2, j)
            attend(h, a)
            if a != 1:
                send_grad_rows(h, a // 2)

        @pl.when(h >= ROWS_BEHIND)
        def _():
            reduce_rows(h - ROWS_BEHIND)

        @pl.when(h >= RELAY_BEHIND)
        def _():
            relay_grad(h - RELAY_BEHIND)

        @pl.when(h >= BEHIND)
        def _():
            finish(h - BEHIND)

    loop(step)
    for h in range(HEADS - ROWS_BEHIND, HEADS):
        reduce_rows(h)

    for h in range(HEADS - RELAY_BEHIND, HEADS):
        relay_grad(h)
    for h in range(HEADS - BEHIND, HEADS):
        finish(h)

    def drain(h):
        @pl.when(relayed_col(h, carried))
        def _():
            col_relay_out(h).wait_send()

        @pl.when(relayed_grad(h, carried))
        def _():
            grad_relay_out(h).wait_send()

        for copy in (col_copy, grad_col_copy):
            for s, (there, dev) in enumerate(sides):

                @pl.when(there)
                def _():
                    copy(h, s, dev).wait_send()

        for s in range(2):
            for j in range(4):

                @pl.when(row_there(s, j))
                def _():
                    row_copy(h, s, j).wait_send()

            for_grad_rows(
                s, lambda half: lone_row_copy(h, s, half).wait_send(), lambda half: grad_row_copy(h, s, half).wait_send()
            )

    loop(drain)


def write_out(*refs):
    sources, outs, sem = refs[:4], refs[4:8], refs[8]
    copies = [pltpu.make_async_copy(x.at[f], y.at[f], sem.at[n, f]) for n, (x, y) in enumerate(zip(sources, outs)) for f in range(4)]
    for copy in copies:
        copy.start()
    for copy in copies:
        copy.wait()


def per_device(size_a, size_w, queries, key_heads, value_heads, out_grad, reach_tiles):
    shape = queries.shape
    ins = [x.reshape(4, 3, 32, HEADS * D) for x in (queries, key_heads, value_heads, out_grad)]
    ins = [pltpu.with_memory_space_constraint(x, pltpu.HBM) for x in ins]
    any_spec = pl.BlockSpec(memory_space=pl.ANY)
    pair = pltpu.SemaphoreType.DMA((HEADS, 2))
    results = pl.pallas_call(
        functools.partial(kernel, size_a, size_w),
        out_shape=[pltpu.VMEM((4, 3, 32, HEADS * D), BF16)] * 4,
        in_specs=[pl.BlockSpec(memory_space=pltpu.SMEM)] + [any_spec] * 4,
        out_specs=[pl.BlockSpec(memory_space=pltpu.VMEM)] * 4,
        scratch_shapes=[
            pltpu.VMEM((HEADS, 2, 8, 5, 32, D), BF16),
            pltpu.VMEM((4, 3, 32, HEADS * D), BF16),
            pltpu.VMEM((4, 3, 32, HEADS * D), BF16),
            pltpu.VMEM((4, 3, 32, HEADS * D), BF16),
            pltpu.VMEM((4, 3, 32, HEADS * D), BF16),
            pltpu.VMEM((HEADS, 2, 4, 3, 32, D), BF16),
            pltpu.VMEM((HEADS, 2, 8, 3, 32, D), F32),
            pltpu.VMEM((HEADS, 2, 2, 2, 4, 32, D), BF16),
            pltpu.VMEM((HEADS, 2, 2, 2, 4, 32, D), BF16),
            pltpu.VMEM((HEADS, 2, 2, 2, 3, 32, D), BF16),
            pltpu.VMEM((HEADS, 2, 2, 2, 3, 32, D), BF16),
            pltpu.VMEM((HEADS, 2, 2, 3, 32, D), BF16),
            pltpu.VMEM((HEADS, 2, 2, 3, 32, D), BF16),
            pltpu.VMEM((3, 576, 128), F32),
            pltpu.VMEM((128, 128), BF16),
            pltpu.VMEM((128, 128), BF16),
            pltpu.SemaphoreType.DMA((4,)),
        ]
        + [pair] * 2
        + [pltpu.SemaphoreType.DMA((HEADS, 2, 4))] * 2
        + [pltpu.SemaphoreType.DMA((HEADS, 2, 2))] * 2
        + [pair] * 2
        + [pltpu.SemaphoreType.DMA((HEADS,))] * 4,
        compiler_params=pltpu.CompilerParams(
            collective_id=0, has_side_effects=True, vmem_limit_bytes=56 * 1024 * 1024
        ),
    )(reach_tiles, *ins)
    outs = pl.pallas_call(
        write_out,
        out_shape=[jax.ShapeDtypeStruct((4, 3, 32, HEADS * D), BF16)] * 4,
        in_specs=[pl.BlockSpec(memory_space=pltpu.VMEM)] * 4,
        out_specs=[any_spec] * 4,
        scratch_shapes=[pltpu.SemaphoreType.DMA((4, 4))],
        compiler_params=pltpu.CompilerParams(vmem_limit_bytes=8 * 1024 * 1024),
    )(*(pltpu.with_memory_space_constraint(x, pltpu.VMEM) for x in results))
    return tuple(x.reshape(shape) for x in outs)


def solution(mesh):
    spec = P(None, "ha", "wa", None)
    return jax.shard_map(
        functools.partial(per_device, mesh.shape["ha"], mesh.shape["wa"]),
        mesh=mesh,
        in_specs=(spec, spec, spec, spec, P("ha", "wa", None)),
        out_specs=(spec, spec, spec, spec),
        check_vma=False,
    )
```

```python
import functools
import math

import jax
import jax.numpy as jnp
from jax import lax
from jax.experimental import pallas as pl
from jax.experimental.pallas import tpu as pltpu
from jax.sharding import PartitionSpec as P

HEADS = 12
TS = 4
D = 128
MESH = pl.DeviceIdType.MESH
AHEAD = 9
RELAY_AHEAD = 6
CORNERS_AHEAD = 3
ROWS_BEHIND = 3
RELAY_BEHIND = 6
BEHIND = 9
NEGATIVE = -1e30
SCALE = 1.0 / math.sqrt(D)
LOG2E = 1.4426950408889634

F32 = jnp.float32
BF16 = jnp.bfloat16


def dot(a, b, ca, cb):
    return lax.dot_general(a, b, (((ca,), (cb,)), ((), ())), preferred_element_type=F32)


def kernel(
    size_a, size_w, reach, q_in, k_in, v_in, g_in, o_out, dq_out, dk_out, dv_out,
    kall, k_own, v_own, q_own, g_own, pack, acc, g3s, g3r, g4s, g4r, r1, r4, bias, perm, perm_t,
    in_sem, ss1, rs1, ss2, rs2, ss3, rs3, ss4, rs4, ri1, ro1, ri4, ro4,
):
    half_a = size_a // 2
    ia = lax.axis_index("ha")
    iw = lax.axis_index("wa")
    has_u, has_d = ia > 0, ia < size_a - 1
    has_l, has_r = iw > 0, iw < size_w - 1
    up, down = (ia - 1, iw), (ia + 1, iw)
    left, right = (ia, iw - 1), (ia, iw + 1)
    sides = ((has_l, left), (has_r, right))
    ends = ((has_u, up), (has_d, down))
    crossed = (ia == half_a, ia == half_a - 1)

    parity, ring, rings = iw % 2, iw // 2, size_w // 2
    out = 2 * parity - 1
    shared = jnp.where(parity == 1, ring + 1, rings - ring)
    carried = jnp.where(parity == 1, ring, rings - 1 - ring)
    middle = (ia >= half_a - 2) & (ia < half_a + 2)

    def chosen(k, part, fewer):
        n = part * HEADS // rings - jnp.where(middle & (part > 0), fewer, 0)
        return (k * n) % HEADS >= HEADS - n

    def relayed_col(h, part):
        return chosen(h, part, jnp.where(part >= 2, 1, 0))

    def relayed_grad(h, part):
        return chosen(HEADS - 1 - h, part, jnp.where(part >= 3, 2, 1))

    def lanes(h):
        return pl.ds(pl.multiple_of(h * D, D), D)

    loads = [
        pltpu.make_async_copy(src, dst, in_sem.at[n])
        for n, (src, dst) in enumerate(((k_in, k_own), (v_in, v_own), (q_in, q_own), (g_in, g_own)))
    ]

    def remote(src, dst, ss, rs, dev):
        return pltpu.make_async_remote_copy(
            src_ref=src, dst_ref=dst, send_sem=ss, recv_sem=rs, device_id=dev, device_id_type=MESH
        )

    def col_copy(h, s, dev):
        lo = 6 - 6 * s
        return remote(
            pack.at[h, :, 2 * s : 2 * s + 2], kall.at[h, :, lo : lo + 2, 1:4], ss1.at[h, s], rs1.at[h, 1 - s], dev
        )

    def row_place(s, j):
        moved = crossed[s] & sides[j // 2][0]
        col = jnp.where(moved, iw + (2 * (j // 2) - 1), iw)
        return jnp.where(moved, (j + 2) % 4, j), (ia + (2 * s - 1), col)

    def row_there(s, j):
        return ends[s][0] if j in (1, 2) else ends[s][0] & sides[j // 2][0]

    def row_copy(h, s, j):
        slot, dev = row_place(s, j)
        src = pack.at[h, :, 2 * j - 2 : 2 * j, 2 * s] if j in (1, 2) else kall.at[h, :, 2 * j : 2 * j + 2, 1 + 2 * s]
        dst = kall.at[h, :, pl.ds(2 * slot, 2), 4 - 4 * s]
        return remote(src, dst, ss2.at[h, s, j], rs2.at[h, 1 - s, slot], dev)

    def send_rows(h, columns):
        for s in range(2):
            for j in columns:

                @pl.when(row_there(s, j))
                def _():
                    row_copy(h, s, j).start()

    def receive_row(h, s, j):
        @pl.when(row_there(s, j))
        def _():
            ref = kall.at[h, :, 2 * j : 2 * j + 2, 4 * s]
            remote(ref, ref, ss2.at[h, s, j], rs2.at[h, s, j], ends[s][1]).wait_recv()

    def alone(s, half):
        return crossed[s] & jnp.logical_not(sides[half][0])

    def part_of(ref, half):
        return ref.at[:, 2 - 2 * half : 4 - 2 * half]

    def lone_row_copy(h, s, half):
        return remote(
            part_of(g3s.at[h, s, half], half), part_of(g3r.at[h, 1 - s, half], half),
            ss3.at[h, s, half], rs3.at[h, 1 - s, half], ends[s][1],
        )

    def for_grad_rows(s, lone, full):
        for half in range(2):

            @pl.when(ends[s][0] & alone(s, half))
            def _():
                lone(half)

            @pl.when(ends[s][0] & jnp.logical_not(alone(s, half)))
            def _():
                full(half)

    def grad_row_copy(h, s, half):
        moved = crossed[s] & sides[half][0]
        col = jnp.where(moved, iw + (2 * half - 1), iw)
        to = jnp.where(moved, 1 - half, half)
        return remote(
            g3s.at[h, s, half], g3r.at[h, 1 - s, to], ss3.at[h, s, half], rs3.at[h, 1 - s, to], (ia + (2 * s - 1), col)
        )

    def col_relay_in(h, s):
        return remote(pack.at[h, :, 2 * s : 2 * s + 2], r1.at[h], ss1.at[h, s], ri1.at[h], (ia, iw + 2 * out))

    def col_relay_out(h):
        dst = kall.at[h, :, pl.ds(6 - 6 * parity, 2), 1:4]
        return remote(r1.at[h], dst, ro1.at[h], rs1.at[h, 1 - parity], (ia, iw - out))

    def grad_relay_in(h, s):
        return remote(g4s.at[h, s], r4.at[h], ss4.at[h, s], ri4.at[h], (ia, iw + 2 * out))

    def grad_relay_out(h):
        return remote(r4.at[h], g4r.at[h, 1 - parity], ro4.at[h], rs4.at[h, 1 - parity], (ia, iw - out))

    def grad_col_copy(h, s, dev):
        return remote(g4s.at[h, s], g4r.at[h, 1 - s], ss4.at[h, s], rs4.at[h, 1 - s], dev)

    def send(direct, by_relay, relayed, h):
        for s, (there, dev) in enumerate(sides):
            through = (parity == s) & relayed(h, shared)

            @pl.when(there & through)
            def _():
                by_relay(h, s).start()

            @pl.when(there & jnp.logical_not(through))
            def _():
                direct(h, s, dev).start()

    def relay_col(h):
        @pl.when(relayed_col(h, carried))
        def _():
            remote(r1.at[h], r1.at[h], ro1.at[h], ri1.at[h], (ia, iw - out)).wait_recv()
            col_relay_out(h).start()

    def relay_grad(h):
        @pl.when(relayed_grad(h, carried))
        def _():
            remote(r4.at[h], r4.at[h], ro4.at[h], ri4.at[h], (ia, iw - out)).wait_recv()
            grad_relay_out(h).start()

    def receive(copy, h, group, s):
        there, dev = group[s]

        @pl.when(there)
        def _():
            copy(h, 1 - s, dev).wait_recv()

    def loop(body):
        lax.fori_loop(0, HEADS, lambda h, c: (body(h), c)[1], 0)

    for load in loads:
        load.start()

    barrier = pltpu.get_barrier_semaphore()
    greeted = sides + ends
    for s, row in ((0, ia - 1), (1, ia + 1)):
        greeted += ((crossed[s] & has_l, (row, iw - 1)), (crossed[s] & has_r, (row, iw + 1)))
    greeted += ((iw >= 2, (ia, iw - 2)), (iw < size_w - 2, (ia, iw + 2)))
    for there, dev in greeted:

        @pl.when(there)
        def _():
            pl.semaphore_signal(barrier, inc=1, device_id=dev, device_id_type=MESH)

    def packed_of(i):
        return ((i >> 2) & 1) * 64 + (i >> 5) * 16 + ((i >> 3) & 3) * 4 + (i & 3)

    first = lax.broadcasted_iota(jnp.int32, (128, 128), 0)
    second = lax.broadcasted_iota(jnp.int32, (128, 128), 1)
    perm[...] = jnp.where(packed_of(first) == second, 1.0, 0.0).astype(BF16)
    perm_t[...] = jnp.where(packed_of(second) == first, 1.0, 0.0).astype(BF16)

    for s, (there, _) in enumerate(sides):

        @pl.when(jnp.logical_not(there))
        def _():
            def fill(h):
                kall[h, :, 6 * s : 6 * s + 2] = jnp.zeros((2, 2, 5, 32, D), BF16)
                g4r[h, s] = jnp.zeros((2, 2, 3, 32, D), BF16)

            loop(fill)

    for s, (there, _) in enumerate(ends):

        @pl.when(jnp.logical_not(there))
        def _():
            def fill(h):
                kall[h, :, :, 4 * s] = jnp.zeros((2, 8, 32, D), BF16)

            loop(fill)

    count = sum(there.astype(jnp.int32) for there, _ in greeted)
    pl.semaphore_wait(barrier, count)

    def permute(matrix, x, y):
        z = dot(matrix[...], jnp.concatenate([x, y], axis=1), 1, 0)
        return z[:, :D], z[:, D:]

    loads[0].wait()
    loads[1].wait()

    def send_edges(h):
        for a in range(3):
            x = [own[:, a, :, lanes(h)] for own in (k_own, v_own)]
            kall[h, 0, 2:6, a + 1] = x[0]
            kall[h, 1, 2:6, a + 1] = x[1]
            y = permute(perm_t, x[0].reshape(128, D), x[1].reshape(128, D))
            pack[h, 0, :, a] = y[0].astype(BF16).reshape(4, 32, D)
            pack[h, 1, :, a] = y[1].astype(BF16).reshape(4, 32, D)
        send_rows(h, (1, 2))
        send(col_copy, col_relay_in, relayed_col, h)

    for h in range(3):
        send_edges(h)

    shape = (6, 3, 32, 128)
    unit = lax.broadcasted_iota(jnp.int32, shape, 0)
    drow = lax.broadcasted_iota(jnp.int32, shape, 1) - 1
    token = lax.broadcasted_iota(jnp.int32, shape, 2)
    query = lax.broadcasted_iota(jnp.int32, shape, 3)
    qcol = (query >> 2) & 1
    for a in range(3):
        own_col = (token >> 2) & 1
        if a != 1:
            own_col = jnp.where(drow == a - 1, unit >> 1, own_col)
        kcol = jnp.where(unit < 4, own_col, 3 * qcol - 1)
        dcol = kcol - qcol
        acol = iw * 2 + kcol
        in_cols = (acol >= 0) & (acol < 2 * size_w)

        def of(n):
            return jnp.where(qcol == 0, reach[a, 0, n], reach[a, 1, n])

        arow = ia * 3 + a + drow
        ok = in_cols & (arow >= 0) & (arow < 3 * size_a)
        ok = ok & (drow >= -of(0)) & (drow <= of(1)) & (dcol >= -of(2)) & (dcol <= of(3))
        bias[a] = jnp.where(ok, 0.0, NEGATIVE).astype(F32).reshape(576, 128)

    def forward(h):
        receive(col_copy, h, sides, 0)
        receive(col_copy, h, sides, 1)
        send_rows(h, (0, 3))

    left_query = ((lax.broadcasted_iota(jnp.int32, (128, D), 0) >> 2) & 1) == 0
    none = jnp.zeros((128, D), BF16)

    def attend(h, a):
        def keys(kv, lo, hi):
            return kall[h, kv, lo:hi, a : a + 3].reshape((hi - lo) * 96, D)

        def halo(kv):
            return jnp.concatenate([keys(kv, 0, 2), keys(kv, 6, 8)], axis=1)

        def by_side(x):
            return jnp.concatenate([jnp.where(left_query, x, none), jnp.where(left_query, none, x)], axis=1)

        def own_side(x):
            return jnp.where(left_query, x[:, :D], x[:, D:])

        k_mid, v_mid, k_halo, v_halo = keys(0, 2, 6), keys(1, 2, 6), halo(0), halo(1)
        q = q_own[:, a, :, lanes(h)].reshape(128, D)
        g = g_own[:, a, :, lanes(h)].reshape(128, D)
        both = jnp.concatenate([jnp.concatenate([q, none], axis=1), jnp.concatenate([none, g], axis=1)], axis=0)
        q_side, g_side = by_side(q), by_side(g)
        mid = dot(jnp.concatenate([k_mid, v_mid], axis=1), both, 1, 1)
        s = jnp.concatenate([mid[:, :128], dot(k_halo, q_side, 1, 1)], axis=0)
        dp = jnp.concatenate([mid[:, 128:], dot(v_halo, g_side, 1, 1)], axis=0)
        s = s * (SCALE * LOG2E) + bias[a]
        p = jnp.exp2(s - jnp.max(s, axis=0, keepdims=True))
        p = p * (1.0 / jnp.sum(p, axis=0, keepdims=True))
        low = p.astype(BF16)
        t = p * dp
        ds = (t - p * jnp.sum(t, axis=0, keepdims=True)).astype(BF16)
        o = dot(low[:384], v_mid, 0, 0) + own_side(dot(low[384:], v_halo, 0, 0))
        dq = dot(ds[:384], k_mid, 0, 0) + own_side(dot(ds[384:], k_halo, 0, 0))
        o_out[:, a, :, lanes(h)] = o.astype(BF16).reshape(4, 32, D)
        dq_out[:, a, :, lanes(h)] = (dq * SCALE).astype(BF16).reshape(4, 32, D)
        mid = dot(jnp.concatenate([ds[:384], low[:384]], axis=1), both, 1, 0)
        sums = ((mid[:, :D], dot(ds[384:], q_side, 1, 0)), (mid[:, D:], dot(low[384:], g_side, 1, 0)))
        for kv, (own, beside) in enumerate(sums):
            own = own.reshape(4, 3, 32, D)
            two = (beside[:, :D].reshape(2, 3, 32, D), beside[:, D:].reshape(2, 3, 32, D))
            for i in range(3):
                row = a + i - 1
                if row in (-1, 3):
                    end = 0 if row < 0 else 1
                    g3s[h, end, 0, kv, 0:2] = two[0][:, i].astype(BF16)
                    g3s[h, end, 0, kv, 2:4] = own[0:2, i].astype(BF16)
                    g3s[h, end, 1, kv, 0:2] = own[2:4, i].astype(BF16)
                    g3s[h, end, 1, kv, 2:4] = two[1][:, i].astype(BF16)
                elif row > a or a == 0:
                    acc[h, kv, 0:2, row] = two[0][:, i]
                    acc[h, kv, 2:6, row] = own[:, i]
                    acc[h, kv, 6:8, row] = two[1][:, i]
                else:
                    acc[h, kv, 0:2, row] += two[0][:, i]
                    acc[h, kv, 2:6, row] += own[:, i]
                    acc[h, kv, 6:8, row] += two[1][:, i]

    def send_grad_rows(h, s):
        for_grad_rows(s, lambda half: lone_row_copy(h, s, half).start(), lambda half: grad_row_copy(h, s, half).start())

    def reduce_rows(h):
        for s in range(2):
            row = 2 * s

            def arrived(half, ref):
                remote(ref, ref, ss3.at[h, s, half], rs3.at[h, s, half], ends[s][1]).wait_recv()

            for_grad_rows(
                s,
                lambda half: arrived(half, part_of(g3r.at[h, s, half], half)),
                lambda half: arrived(half, g3r.at[h, s, half]),
            )
            for half, (there, _) in enumerate(sides):

                @pl.when(ends[s][0] & there)
                def _():
                    units = slice(6 * half, 6 * half + 2)
                    acc[h, :, units, row] += g3r[h, s, half, :, 2 * half : 2 * half + 2].astype(F32)

            @pl.when(ends[s][0])
            def _():
                x = [jnp.concatenate([g3r[h, s, 0, kv, 2:4], g3r[h, s, 1, kv, 0:2]]).reshape(128, D) for kv in range(2)]
                for kv, y in enumerate(permute(perm, x[0], x[1])):
                    acc[h, kv, 2:6, row] += y.reshape(4, 32, D)

        for s in range(2):
            g4s[h, s] = acc[h, :, 6 * s : 6 * s + 2].astype(BF16)
        send(grad_col_copy, grad_relay_in, relayed_grad, h)

    def finish(h):
        for s in range(2):
            receive(grad_col_copy, h, sides, s)
        for a in range(3):
            x = [g4r[h, :, kv, :, a].reshape(128, D) for kv in range(2)]
            y = permute(perm, x[0], x[1])
            dk = (y[0].reshape(4, 32, D) + acc[h, 0, 2:6, a]) * SCALE
            dv = y[1].reshape(4, 32, D) + acc[h, 1, 2:6, a]
            dk_out[:, a, :, lanes(h)] = dk.astype(BF16)
            dv_out[:, a, :, lanes(h)] = dv.astype(BF16)

    for h in range(RELAY_AHEAD):
        relay_col(h)
        if h < CORNERS_AHEAD:
            forward(h)
        if h + 3 < AHEAD:
            send_edges(h + 3)

    loads[2].wait()
    loads[3].wait()

    def step(h):
        @pl.when(h + CORNERS_AHEAD < HEADS)
        def _():
            forward(h + CORNERS_AHEAD)

        @pl.when(h + RELAY_AHEAD < HEADS)
        def _():
            relay_col(h + RELAY_AHEAD)

        @pl.when(h + AHEAD < HEADS)
        def _():
            send_edges(h + AHEAD)

        for a in range(3):
            if a != 1:
                for j in range(4):
                    receive_row(h, a // 2, j)
            attend(h, a)
            if a != 1:
                send_grad_rows(h, a // 2)

        @pl.when(h >= ROWS_BEHIND)
        def _():
            reduce_rows(h - ROWS_BEHIND)

        @pl.when(h >= RELAY_BEHIND)
        def _():
            relay_grad(h - RELAY_BEHIND)

        @pl.when(h >= BEHIND)
        def _():
            finish(h - BEHIND)

    loop(step)
    for h in range(HEADS - ROWS_BEHIND, HEADS):
        reduce_rows(h)

    for h in range(HEADS - RELAY_BEHIND, HEADS):
        relay_grad(h)
    for h in range(HEADS - BEHIND, HEADS):
        finish(h)

    def drain(h):
        @pl.when(relayed_col(h, carried))
        def _():
            col_relay_out(h).wait_send()

        @pl.when(relayed_grad(h, carried))
        def _():
            grad_relay_out(h).wait_send()

        for copy in (col_copy, grad_col_copy):
            for s, (there, dev) in enumerate(sides):

                @pl.when(there)
                def _():
                    copy(h, s, dev).wait_send()

        for s in range(2):
            for j in range(4):

                @pl.when(row_there(s, j))
                def _():
                    row_copy(h, s, j).wait_send()

            for_grad_rows(
                s, lambda half: lone_row_copy(h, s, half).wait_send(), lambda half: grad_row_copy(h, s, half).wait_send()
            )

    loop(drain)


def write_out(*refs):
    sources, outs, sem = refs[:4], refs[4:8], refs[8]
    copies = [pltpu.make_async_copy(x.at[f], y.at[f], sem.at[n, f]) for n, (x, y) in enumerate(zip(sources, outs)) for f in range(4)]
    for copy in copies:
        copy.start()
    for copy in copies:
        copy.wait()


def per_device(size_a, size_w, queries, key_heads, value_heads, out_grad, reach_tiles):
    shape = queries.shape
    ins = [x.reshape(4, 3, 32, HEADS * D) for x in (queries, key_heads, value_heads, out_grad)]
    ins = [pltpu.with_memory_space_constraint(x, pltpu.HBM) for x in ins]
    any_spec = pl.BlockSpec(memory_space=pl.ANY)
    pair = pltpu.SemaphoreType.DMA((HEADS, 2))
    results = pl.pallas_call(
        functools.partial(kernel, size_a, size_w),
        out_shape=[pltpu.VMEM((4, 3, 32, HEADS * D), BF16)] * 4,
        in_specs=[pl.BlockSpec(memory_space=pltpu.SMEM)] + [any_spec] * 4,
        out_specs=[pl.BlockSpec(memory_space=pltpu.VMEM)] * 4,
        scratch_shapes=[
            pltpu.VMEM((HEADS, 2, 8, 5, 32, D), BF16),
            pltpu.VMEM((4, 3, 32, HEADS * D), BF16),
            pltpu.VMEM((4, 3, 32, HEADS * D), BF16),
            pltpu.VMEM((4, 3, 32, HEADS * D), BF16),
            pltpu.VMEM((4, 3, 32, HEADS * D), BF16),
            pltpu.VMEM((HEADS, 2, 4, 3, 32, D), BF16),
            pltpu.VMEM((HEADS, 2, 8, 3, 32, D), F32),
            pltpu.VMEM((HEADS, 2, 2, 2, 4, 32, D), BF16),
            pltpu.VMEM((HEADS, 2, 2, 2, 4, 32, D), BF16),
            pltpu.VMEM((HEADS, 2, 2, 2, 3, 32, D), BF16),
            pltpu.VMEM((HEADS, 2, 2, 2, 3, 32, D), BF16),
            pltpu.VMEM((HEADS, 2, 2, 3, 32, D), BF16),
            pltpu.VMEM((HEADS, 2, 2, 3, 32, D), BF16),
            pltpu.VMEM((3, 576, 128), F32),
            pltpu.VMEM((128, 128), BF16),
            pltpu.VMEM((128, 128), BF16),
            pltpu.SemaphoreType.DMA((4,)),
        ]
        + [pair] * 2
        + [pltpu.SemaphoreType.DMA((HEADS, 2, 4))] * 2
        + [pltpu.SemaphoreType.DMA((HEADS, 2, 2))] * 2
        + [pair] * 2
        + [pltpu.SemaphoreType.DMA((HEADS,))] * 4,
        compiler_params=pltpu.CompilerParams(
            collective_id=0, has_side_effects=True, vmem_limit_bytes=56 * 1024 * 1024
        ),
    )(reach_tiles, *ins)
    outs = pl.pallas_call(
        write_out,
        out_shape=[jax.ShapeDtypeStruct((4, 3, 32, HEADS * D), BF16)] * 4,
        in_specs=[pl.BlockSpec(memory_space=pltpu.VMEM)] * 4,
        out_specs=[any_spec] * 4,
        scratch_shapes=[pltpu.SemaphoreType.DMA((4, 4))],
        compiler_params=pltpu.CompilerParams(vmem_limit_bytes=8 * 1024 * 1024),
    )(*(pltpu.with_memory_space_constraint(x, pltpu.VMEM) for x in results))
    return tuple(x.reshape(shape) for x in outs)


def solution(mesh):
    spec = P(None, "ha", "wa", None)
    return jax.shard_map(
        functools.partial(per_device, mesh.shape["ha"], mesh.shape["wa"]),
        mesh=mesh,
        in_specs=(spec, spec, spec, spec, P("ha", "wa", None)),
        out_specs=(spec, spec, spec, spec),
        check_vma=False,
    )
```

```python
import functools
import math

import jax
import jax.numpy as jnp
from jax import lax
from jax.experimental import pallas as pl
from jax.experimental.pallas import tpu as pltpu
from jax.sharding import PartitionSpec as P

HEADS = 12
TS = 4
D = 128
MESH = pl.DeviceIdType.MESH
AHEAD = 10
RELAY_AHEAD = 6
CORNERS_AHEAD = 3
ROWS_BEHIND = 3
RELAY_BEHIND = 7
BEHIND = 10
NEGATIVE = -1e30
SCALE = 1.0 / math.sqrt(D)
LOG2E = 1.4426950408889634

F32 = jnp.float32
BF16 = jnp.bfloat16


def dot(a, b, ca, cb):
    return lax.dot_general(a, b, (((ca,), (cb,)), ((), ())), preferred_element_type=F32)


def kernel(
    size_a, size_w, reach, q_in, k_in, v_in, g_in, o_out, dq_out, dk_out, dv_out,
    kall, k_own, v_own, q_own, g_own, pack, acc, g3s, g3r, g4s, g4r, r1, r4, bias, perm, perm_t,
    in_sem, ss1, rs1, ss2, rs2, ss3, rs3, ss4, rs4, ri1, ro1, ri4, ro4,
):
    half_a = size_a // 2
    ia = lax.axis_index("ha")
    iw = lax.axis_index("wa")
    has_u, has_d = ia > 0, ia < size_a - 1
    has_l, has_r = iw > 0, iw < size_w - 1
    up, down = (ia - 1, iw), (ia + 1, iw)
    left, right = (ia, iw - 1), (ia, iw + 1)
    sides = ((has_l, left), (has_r, right))
    ends = ((has_u, up), (has_d, down))
    crossed = (ia == half_a, ia == half_a - 1)

    parity, ring, rings = iw % 2, iw // 2, size_w // 2
    out = 2 * parity - 1
    shared = jnp.where(parity == 1, ring + 1, rings - ring)
    carried = jnp.where(parity == 1, ring, rings - 1 - ring)
    middle = (ia >= half_a - 2) & (ia < half_a + 2)

    def chosen(k, part, fewer, more):
        n = part * HEADS // rings - jnp.where(middle & (part > 0), fewer, 0) + more
        return (k * n) % HEADS >= HEADS - n

    def relayed_col(h, part):
        return chosen(h, part, jnp.where(part >= 2, 1, 0), jnp.where(part == 3, 1, 0))

    def relayed_grad(h, part):
        return chosen(HEADS - 1 - h, part, jnp.where(part >= 3, 2, 1), 0)

    def lanes(h):
        return pl.ds(pl.multiple_of(h * D, D), D)

    loads = [
        pltpu.make_async_copy(src, dst, in_sem.at[n])
        for n, (src, dst) in enumerate(((k_in, k_own), (v_in, v_own), (q_in, q_own), (g_in, g_own)))
    ]

    def remote(src, dst, ss, rs, dev):
        return pltpu.make_async_remote_copy(
            src_ref=src, dst_ref=dst, send_sem=ss, recv_sem=rs, device_id=dev, device_id_type=MESH
        )

    def col_copy(h, s, dev):
        lo = 6 - 6 * s
        return remote(
            pack.at[h, :, 2 * s : 2 * s + 2], kall.at[h, :, lo : lo + 2, 1:4], ss1.at[h, s], rs1.at[h, 1 - s], dev
        )

    def row_place(s, j):
        moved = crossed[s] & sides[j // 2][0]
        col = jnp.where(moved, iw + (2 * (j // 2) - 1), iw)
        return jnp.where(moved, (j + 2) % 4, j), (ia + (2 * s - 1), col)

    def row_there(s, j):
        return ends[s][0] if j in (1, 2) else ends[s][0] & sides[j // 2][0]

    def row_copy(h, s, j):
        slot, dev = row_place(s, j)
        src = pack.at[h, :, 2 * j - 2 : 2 * j, 2 * s] if j in (1, 2) else kall.at[h, :, 2 * j : 2 * j + 2, 1 + 2 * s]
        dst = kall.at[h, :, pl.ds(2 * slot, 2), 4 - 4 * s]
        return remote(src, dst, ss2.at[h, s, j], rs2.at[h, 1 - s, slot], dev)

    def send_rows(h, columns):
        for s in range(2):
            for j in columns:

                @pl.when(row_there(s, j))
                def _():
                    row_copy(h, s, j).start()

    def receive_row(h, s, j):
        @pl.when(row_there(s, j))
        def _():
            ref = kall.at[h, :, 2 * j : 2 * j + 2, 4 * s]
            remote(ref, ref, ss2.at[h, s, j], rs2.at[h, s, j], ends[s][1]).wait_recv()

    def alone(s, half):
        return crossed[s] & jnp.logical_not(sides[half][0])

    def part_of(ref, half):
        return ref.at[:, 2 - 2 * half : 4 - 2 * half]

    def lone_row_copy(h, s, half):
        return remote(
            part_of(g3s.at[h, s, half], half), part_of(g3r.at[h, 1 - s, half], half),
            ss3.at[h, s, half], rs3.at[h, 1 - s, half], ends[s][1],
        )

    def for_grad_rows(s, lone, full):
        for half in range(2):

            @pl.when(ends[s][0] & alone(s, half))
            def _():
                lone(half)

            @pl.when(ends[s][0] & jnp.logical_not(alone(s, half)))
            def _():
                full(half)

    def grad_row_copy(h, s, half):
        moved = crossed[s] & sides[half][0]
        col = jnp.where(moved, iw + (2 * half - 1), iw)
        to = jnp.where(moved, 1 - half, half)
        return remote(
            g3s.at[h, s, half], g3r.at[h, 1 - s, to], ss3.at[h, s, half], rs3.at[h, 1 - s, to], (ia + (2 * s - 1), col)
        )

    def col_relay_in(h, s):
        return remote(pack.at[h, :, 2 * s : 2 * s + 2], r1.at[h], ss1.at[h, s], ri1.at[h], (ia, iw + 2 * out))

    def col_relay_out(h):
        dst = kall.at[h, :, pl.ds(6 - 6 * parity, 2), 1:4]
        return remote(r1.at[h], dst, ro1.at[h], rs1.at[h, 1 - parity], (ia, iw - out))

    def grad_relay_in(h, s):
        return remote(g4s.at[h, s], r4.at[h], ss4.at[h, s], ri4.at[h], (ia, iw + 2 * out))

    def grad_relay_out(h):
        return remote(r4.at[h], g4r.at[h, 1 - parity], ro4.at[h], rs4.at[h, 1 - parity], (ia, iw - out))

    def grad_col_copy(h, s, dev):
        return remote(g4s.at[h, s], g4r.at[h, 1 - s], ss4.at[h, s], rs4.at[h, 1 - s], dev)

    def send(direct, by_relay, relayed, h):
        for s, (there, dev) in enumerate(sides):
            through = (parity == s) & relayed(h, shared)

            @pl.when(there & through)
            def _():
                by_relay(h, s).start()

            @pl.when(there & jnp.logical_not(through))
            def _():
                direct(h, s, dev).start()

    def relay_col(h):
        @pl.when(relayed_col(h, carried))
        def _():
            remote(r1.at[h], r1.at[h], ro1.at[h], ri1.at[h], (ia, iw - out)).wait_recv()
            col_relay_out(h).start()

    def relay_grad(h):
        @pl.when(relayed_grad(h, carried))
        def _():
            remote(r4.at[h], r4.at[h], ro4.at[h], ri4.at[h], (ia, iw - out)).wait_recv()
            grad_relay_out(h).start()

    def receive(copy, h, group, s):
        there, dev = group[s]

        @pl.when(there)
        def _():
            copy(h, 1 - s, dev).wait_recv()

    def loop(body):
        lax.fori_loop(0, HEADS, lambda h, c: (body(h), c)[1], 0)

    for load in loads:
        load.start()

    barrier = pltpu.get_barrier_semaphore()
    greeted = sides + ends
    for s, row in ((0, ia - 1), (1, ia + 1)):
        greeted += ((crossed[s] & has_l, (row, iw - 1)), (crossed[s] & has_r, (row, iw + 1)))
    greeted += ((iw >= 2, (ia, iw - 2)), (iw < size_w - 2, (ia, iw + 2)))
    for there, dev in greeted:

        @pl.when(there)
        def _():
            pl.semaphore_signal(barrier, inc=1, device_id=dev, device_id_type=MESH)

    def packed_of(i):
        return ((i >> 2) & 1) * 64 + (i >> 5) * 16 + ((i >> 3) & 3) * 4 + (i & 3)

    first = lax.broadcasted_iota(jnp.int32, (128, 128), 0)
    second = lax.broadcasted_iota(jnp.int32, (128, 128), 1)
    perm[...] = jnp.where(packed_of(first) == second, 1.0, 0.0).astype(BF16)
    perm_t[...] = jnp.where(packed_of(second) == first, 1.0, 0.0).astype(BF16)

    for s, (there, _) in enumerate(sides):

        @pl.when(jnp.logical_not(there))
        def _():
            def fill(h):
                kall[h, :, 6 * s : 6 * s + 2] = jnp.zeros((2, 2, 5, 32, D), BF16)
                g4r[h, s] = jnp.zeros((2, 2, 3, 32, D), BF16)

            loop(fill)

    for s, (there, _) in enumerate(ends):

        @pl.when(jnp.logical_not(there))
        def _():
            def fill(h):
                kall[h, :, :, 4 * s] = jnp.zeros((2, 8, 32, D), BF16)

            loop(fill)

    count = sum(there.astype(jnp.int32) for there, _ in greeted)
    pl.semaphore_wait(barrier, count)

    def permute(matrix, x, y):
        z = dot(matrix[...], jnp.concatenate([x, y], axis=1), 1, 0)
        return z[:, :D], z[:, D:]

    loads[0].wait()
    loads[1].wait()

    def send_edges(h):
        for a in range(3):
            x = [own[:, a, :, lanes(h)] for own in (k_own, v_own)]
            kall[h, 0, 2:6, a + 1] = x[0]
            kall[h, 1, 2:6, a + 1] = x[1]
            y = permute(perm_t, x[0].reshape(128, D), x[1].reshape(128, D))
            pack[h, 0, :, a] = y[0].astype(BF16).reshape(4, 32, D)
            pack[h, 1, :, a] = y[1].astype(BF16).reshape(4, 32, D)
        send_rows(h, (1, 2))
        send(col_copy, col_relay_in, relayed_col, h)

    for h in range(4):
        send_edges(h)

    shape = (6, 3, 32, 128)
    unit = lax.broadcasted_iota(jnp.int32, shape, 0)
    drow = lax.broadcasted_iota(jnp.int32, shape, 1) - 1
    token = lax.broadcasted_iota(jnp.int32, shape, 2)
    query = lax.broadcasted_iota(jnp.int32, shape, 3)
    qcol = (query >> 2) & 1
    for a in range(3):
        own_col = (token >> 2) & 1
        if a != 1:
            own_col = jnp.where(drow == a - 1, unit >> 1, own_col)
        kcol = jnp.where(unit < 4, own_col, 3 * qcol - 1)
        dcol = kcol - qcol
        acol = iw * 2 + kcol
        in_cols = (acol >= 0) & (acol < 2 * size_w)

        def of(n):
            return jnp.where(qcol == 0, reach[a, 0, n], reach[a, 1, n])

        arow = ia * 3 + a + drow
        ok = in_cols & (arow >= 0) & (arow < 3 * size_a)
        ok = ok & (drow >= -of(0)) & (drow <= of(1)) & (dcol >= -of(2)) & (dcol <= of(3))
        bias[a] = jnp.where(ok, 0.0, NEGATIVE).astype(F32).reshape(576, 128)

    def forward(h):
        receive(col_copy, h, sides, 0)
        receive(col_copy, h, sides, 1)
        send_rows(h, (0, 3))

    left_query = ((lax.broadcasted_iota(jnp.int32, (128, D), 0) >> 2) & 1) == 0
    none = jnp.zeros((128, D), BF16)

    def attend(h, a):
        def keys(kv, lo, hi):
            return kall[h, kv, lo:hi, a : a + 3].reshape((hi - lo) * 96, D)

        def halo(kv):
            return jnp.concatenate([keys(kv, 0, 2), keys(kv, 6, 8)], axis=1)

        def by_side(x):
            return jnp.concatenate([jnp.where(left_query, x, none), jnp.where(left_query, none, x)], axis=1)

        def own_side(x):
            return jnp.where(left_query, x[:, :D], x[:, D:])

        k_mid, v_mid, k_halo, v_halo = keys(0, 2, 6), keys(1, 2, 6), halo(0), halo(1)
        q = q_own[:, a, :, lanes(h)].reshape(128, D)
        g = g_own[:, a, :, lanes(h)].reshape(128, D)
        both = jnp.concatenate([jnp.concatenate([q, none], axis=1), jnp.concatenate([none, g], axis=1)], axis=0)
        q_side, g_side = by_side(q), by_side(g)
        mid = dot(jnp.concatenate([k_mid, v_mid], axis=1), both, 1, 1)
        s = jnp.concatenate([mid[:, :128], dot(k_halo, q_side, 1, 1)], axis=0)
        dp = jnp.concatenate([mid[:, 128:], dot(v_halo, g_side, 1, 1)], axis=0)
        s = s * (SCALE * LOG2E) + bias[a]
        p = jnp.exp2(s - jnp.max(s, axis=0, keepdims=True))
        p = p * (1.0 / jnp.sum(p, axis=0, keepdims=True))
        low = p.astype(BF16)
        t = p * dp
        ds = (t - p * jnp.sum(t, axis=0, keepdims=True)).astype(BF16)
        o = dot(low[:384], v_mid, 0, 0) + own_side(dot(low[384:], v_halo, 0, 0))
        dq = dot(ds[:384], k_mid, 0, 0) + own_side(dot(ds[384:], k_halo, 0, 0))
        o_out[:, a, :, lanes(h)] = o.astype(BF16).reshape(4, 32, D)
        dq_out[:, a, :, lanes(h)] = (dq * SCALE).astype(BF16).reshape(4, 32, D)
        mid = dot(jnp.concatenate([ds[:384], low[:384]], axis=1), both, 1, 0)
        sums = ((mid[:, :D], dot(ds[384:], q_side, 1, 0)), (mid[:, D:], dot(low[384:], g_side, 1, 0)))
        for kv, (own, beside) in enumerate(sums):
            own = own.reshape(4, 3, 32, D)
            two = (beside[:, :D].reshape(2, 3, 32, D), beside[:, D:].reshape(2, 3, 32, D))
            for i in range(3):
                row = a + i - 1
                if row in (-1, 3):
                    end = 0 if row < 0 else 1
                    g3s[h, end, 0, kv, 0:2] = two[0][:, i].astype(BF16)
                    g3s[h, end, 0, kv, 2:4] = own[0:2, i].astype(BF16)
                    g3s[h, end, 1, kv, 0:2] = own[2:4, i].astype(BF16)
                    g3s[h, end, 1, kv, 2:4] = two[1][:, i].astype(BF16)
                elif row > a or a == 0:
                    acc[h, kv, 0:2, row] = two[0][:, i]
                    acc[h, kv, 2:6, row] = own[:, i]
                    acc[h, kv, 6:8, row] = two[1][:, i]
                else:
                    acc[h, kv, 0:2, row] += two[0][:, i]
                    acc[h, kv, 2:6, row] += own[:, i]
                    acc[h, kv, 6:8, row] += two[1][:, i]

    def send_grad_rows(h, s):
        for_grad_rows(s, lambda half: lone_row_copy(h, s, half).start(), lambda half: grad_row_copy(h, s, half).start())

    def reduce_rows(h):
        for s in range(2):
            row = 2 * s

            def arrived(half, ref):
                remote(ref, ref, ss3.at[h, s, half], rs3.at[h, s, half], ends[s][1]).wait_recv()

            for_grad_rows(
                s,
                lambda half: arrived(half, part_of(g3r.at[h, s, half], half)),
                lambda half: arrived(half, g3r.at[h, s, half]),
            )
            for half, (there, _) in enumerate(sides):

                @pl.when(ends[s][0] & there)
                def _():
                    units = slice(6 * half, 6 * half + 2)
                    acc[h, :, units, row] += g3r[h, s, half, :, 2 * half : 2 * half + 2].astype(F32)

            @pl.when(ends[s][0])
            def _():
                x = [jnp.concatenate([g3r[h, s, 0, kv, 2:4], g3r[h, s, 1, kv, 0:2]]).reshape(128, D) for kv in range(2)]
                for kv, y in enumerate(permute(perm, x[0], x[1])):
                    acc[h, kv, 2:6, row] += y.reshape(4, 32, D)

        for s in range(2):
            g4s[h, s] = acc[h, :, 6 * s : 6 * s + 2].astype(BF16)
        send(grad_col_copy, grad_relay_in, relayed_grad, h)

    def finish(h):
        for s in range(2):
            receive(grad_col_copy, h, sides, s)
        for a in range(3):
            x = [g4r[h, :, kv, :, a].reshape(128, D) for kv in range(2)]
            y = permute(perm, x[0], x[1])
            dk = (y[0].reshape(4, 32, D) + acc[h, 0, 2:6, a]) * SCALE
            dv = y[1].reshape(4, 32, D) + acc[h, 1, 2:6, a]
            dk_out[:, a, :, lanes(h)] = dk.astype(BF16)
            dv_out[:, a, :, lanes(h)] = dv.astype(BF16)

    for h in range(RELAY_AHEAD):
        relay_col(h)
        if h < CORNERS_AHEAD:
            forward(h)
        if h + 4 < AHEAD:
            send_edges(h + 4)

    loads[2].wait()
    loads[3].wait()

    def step(h):
        @pl.when(h + CORNERS_AHEAD < HEADS)
        def _():
            forward(h + CORNERS_AHEAD)

        @pl.when(h + RELAY_AHEAD < HEADS)
        def _():
            relay_col(h + RELAY_AHEAD)

        @pl.when(h + AHEAD < HEADS)
        def _():
            send_edges(h + AHEAD)

        for a in range(3):
            if a != 1:
                for j in range(4):
                    receive_row(h, a // 2, j)
            attend(h, a)
            if a != 1:
                send_grad_rows(h, a // 2)

        @pl.when(h >= ROWS_BEHIND)
        def _():
            reduce_rows(h - ROWS_BEHIND)

        @pl.when(h >= RELAY_BEHIND)
        def _():
            relay_grad(h - RELAY_BEHIND)

        @pl.when(h >= BEHIND)
        def _():
            finish(h - BEHIND)

    loop(step)
    for h in range(HEADS - ROWS_BEHIND, HEADS):
        reduce_rows(h)

    for h in range(HEADS - RELAY_BEHIND, HEADS):
        relay_grad(h)
    for h in range(HEADS - BEHIND, HEADS):
        finish(h)

    def drain(h):
        @pl.when(relayed_col(h, carried))
        def _():
            col_relay_out(h).wait_send()

        @pl.when(relayed_grad(h, carried))
        def _():
            grad_relay_out(h).wait_send()

        for copy in (col_copy, grad_col_copy):
            for s, (there, dev) in enumerate(sides):

                @pl.when(there)
                def _():
                    copy(h, s, dev).wait_send()

        for s in range(2):
            for j in range(4):

                @pl.when(row_there(s, j))
                def _():
                    row_copy(h, s, j).wait_send()

            for_grad_rows(
                s, lambda half: lone_row_copy(h, s, half).wait_send(), lambda half: grad_row_copy(h, s, half).wait_send()
            )

    loop(drain)


def write_out(*refs):
    sources, outs, sem = refs[:4], refs[4:8], refs[8]
    copies = [pltpu.make_async_copy(x.at[f], y.at[f], sem.at[n, f]) for n, (x, y) in enumerate(zip(sources, outs)) for f in range(4)]
    for copy in copies:
        copy.start()
    for copy in copies:
        copy.wait()


def per_device(size_a, size_w, queries, key_heads, value_heads, out_grad, reach_tiles):
    shape = queries.shape
    ins = [x.reshape(4, 3, 32, HEADS * D) for x in (queries, key_heads, value_heads, out_grad)]
    ins = [pltpu.with_memory_space_constraint(x, pltpu.HBM) for x in ins]
    any_spec = pl.BlockSpec(memory_space=pl.ANY)
    pair = pltpu.SemaphoreType.DMA((HEADS, 2))
    results = pl.pallas_call(
        functools.partial(kernel, size_a, size_w),
        out_shape=[pltpu.VMEM((4, 3, 32, HEADS * D), BF16)] * 4,
        in_specs=[pl.BlockSpec(memory_space=pltpu.SMEM)] + [any_spec] * 4,
        out_specs=[pl.BlockSpec(memory_space=pltpu.VMEM)] * 4,
        scratch_shapes=[
            pltpu.VMEM((HEADS, 2, 8, 5, 32, D), BF16),
            pltpu.VMEM((4, 3, 32, HEADS * D), BF16),
            pltpu.VMEM((4, 3, 32, HEADS * D), BF16),
            pltpu.VMEM((4, 3, 32, HEADS * D), BF16),
            pltpu.VMEM((4, 3, 32, HEADS * D), BF16),
            pltpu.VMEM((HEADS, 2, 4, 3, 32, D), BF16),
            pltpu.VMEM((HEADS, 2, 8, 3, 32, D), F32),
            pltpu.VMEM((HEADS, 2, 2, 2, 4, 32, D), BF16),
            pltpu.VMEM((HEADS, 2, 2, 2, 4, 32, D), BF16),
            pltpu.VMEM((HEADS, 2, 2, 2, 3, 32, D), BF16),
            pltpu.VMEM((HEADS, 2, 2, 2, 3, 32, D), BF16),
            pltpu.VMEM((HEADS, 2, 2, 3, 32, D), BF16),
            pltpu.VMEM((HEADS, 2, 2, 3, 32, D), BF16),
            pltpu.VMEM((3, 576, 128), F32),
            pltpu.VMEM((128, 128), BF16),
            pltpu.VMEM((128, 128), BF16),
            pltpu.SemaphoreType.DMA((4,)),
        ]
        + [pair] * 2
        + [pltpu.SemaphoreType.DMA((HEADS, 2, 4))] * 2
        + [pltpu.SemaphoreType.DMA((HEADS, 2, 2))] * 2
        + [pair] * 2
        + [pltpu.SemaphoreType.DMA((HEADS,))] * 4,
        compiler_params=pltpu.CompilerParams(
            collective_id=0, has_side_effects=True, vmem_limit_bytes=56 * 1024 * 1024
        ),
    )(reach_tiles, *ins)
    outs = pl.pallas_call(
        write_out,
        out_shape=[jax.ShapeDtypeStruct((4, 3, 32, HEADS * D), BF16)] * 4,
        in_specs=[pl.BlockSpec(memory_space=pltpu.VMEM)] * 4,
        out_specs=[any_spec] * 4,
        scratch_shapes=[pltpu.SemaphoreType.DMA((4, 4))],
        compiler_params=pltpu.CompilerParams(vmem_limit_bytes=8 * 1024 * 1024),
    )(*(pltpu.with_memory_space_constraint(x, pltpu.VMEM) for x in results))
    return tuple(x.reshape(shape) for x in outs)


def solution(mesh):
    spec = P(None, "ha", "wa", None)
    return jax.shard_map(
        functools.partial(per_device, mesh.shape["ha"], mesh.shape["wa"]),
        mesh=mesh,
        in_specs=(spec, spec, spec, spec, P("ha", "wa", None)),
        out_specs=(spec, spec, spec, spec),
        check_vma=False,
    )
```

```python
import functools
import math

import jax
import jax.numpy as jnp
from jax import lax
from jax.experimental import pallas as pl
from jax.experimental.pallas import tpu as pltpu
from jax.sharding import PartitionSpec as P

HEADS = 12
TS = 4
D = 128
MESH = pl.DeviceIdType.MESH
AHEAD = 9
RELAY_AHEAD = 6
CORNERS_AHEAD = 3
ROWS_BEHIND = 4
RELAY_BEHIND = 7
BEHIND = 10
NEGATIVE = -1e30
SCALE = 1.0 / math.sqrt(D)
LOG2E = 1.4426950408889634

F32 = jnp.float32
BF16 = jnp.bfloat16


def dot(a, b, ca, cb):
    return lax.dot_general(a, b, (((ca,), (cb,)), ((), ())), preferred_element_type=F32)


def kernel(
    size_a, size_w, reach, q_in, k_in, v_in, g_in, o_out, dq_out, dk_out, dv_out,
    kall, k_own, v_own, q_own, g_own, pack, acc, g3s, g3r, g4s, g4r, r1, r4, bias, perm, perm_t,
    in_sem, ss1, rs1, ss2, rs2, ss3, rs3, ss4, rs4, ri1, ro1, ri4, ro4,
):
    half_a = size_a // 2
    ia = lax.axis_index("ha")
    iw = lax.axis_index("wa")
    has_u, has_d = ia > 0, ia < size_a - 1
    has_l, has_r = iw > 0, iw < size_w - 1
    up, down = (ia - 1, iw), (ia + 1, iw)
    left, right = (ia, iw - 1), (ia, iw + 1)
    sides = ((has_l, left), (has_r, right))
    ends = ((has_u, up), (has_d, down))
    crossed = (ia == half_a, ia == half_a - 1)

    parity, ring, rings = iw % 2, iw // 2, size_w // 2
    out = 2 * parity - 1
    shared = jnp.where(parity == 1, ring + 1, rings - ring)
    carried = jnp.where(parity == 1, ring, rings - 1 - ring)
    middle = (ia >= half_a - 2) & (ia < half_a + 2)

    def chosen(k, part, fewer):
        n = part * HEADS // rings - jnp.where(middle & (part > 0), fewer, 0)
        return (k * n) % HEADS >= HEADS - n

    def relayed_col(h, part):
        return chosen(h, part, jnp.where(part >= 2, 1, 0))

    def relayed_grad(h, part):
        return chosen(HEADS - 1 - h, part, jnp.where(part >= 3, 2, 1))

    def lanes(h):
        return pl.ds(pl.multiple_of(h * D, D), D)

    loads = [
        pltpu.make_async_copy(src, dst, in_sem.at[n])
        for n, (src, dst) in enumerate(((k_in, k_own), (v_in, v_own), (q_in, q_own), (g_in, g_own)))
    ]

    def remote(src, dst, ss, rs, dev):
        return pltpu.make_async_remote_copy(
            src_ref=src, dst_ref=dst, send_sem=ss, recv_sem=rs, device_id=dev, device_id_type=MESH
        )

    def col_copy(h, s, dev):
        lo = 6 - 6 * s
        return remote(
            pack.at[h, :, 2 * s : 2 * s + 2], kall.at[h, :, lo : lo + 2, 1:4], ss1.at[h, s], rs1.at[h, 1 - s], dev
        )

    def row_place(s, j):
        moved = crossed[s] & sides[j // 2][0]
        col = jnp.where(moved, iw + (2 * (j // 2) - 1), iw)
        return jnp.where(moved, (j + 2) % 4, j), (ia + (2 * s - 1), col)

    def row_there(s, j):
        return ends[s][0] if j in (1, 2) else ends[s][0] & sides[j // 2][0]

    def row_copy(h, s, j):
        slot, dev = row_place(s, j)
        src = pack.at[h, :, 2 * j - 2 : 2 * j, 2 * s] if j in (1, 2) else kall.at[h, :, 2 * j : 2 * j + 2, 1 + 2 * s]
        dst = kall.at[h, :, pl.ds(2 * slot, 2), 4 - 4 * s]
        return remote(src, dst, ss2.at[h, s, j], rs2.at[h, 1 - s, slot], dev)

    def send_rows(h, columns):
        for s in range(2):
            for j in columns:

                @pl.when(row_there(s, j))
                def _():
                    row_copy(h, s, j).start()

    def receive_row(h, s, j):
        @pl.when(row_there(s, j))
        def _():
            ref = kall.at[h, :, 2 * j : 2 * j + 2, 4 * s]
            remote(ref, ref, ss2.at[h, s, j], rs2.at[h, s, j], ends[s][1]).wait_recv()

    def alone(s, half):
        return crossed[s] & jnp.logical_not(sides[half][0])

    def part_of(ref, half):
        return ref.at[:, 2 - 2 * half : 4 - 2 * half]

    def lone_row_copy(h, s, half):
        return remote(
            part_of(g3s.at[h, s, half], half), part_of(g3r.at[h, 1 - s, half], half),
            ss3.at[h, s, half], rs3.at[h, 1 - s, half], ends[s][1],
        )

    def for_grad_rows(s, lone, full):
        for half in range(2):

            @pl.when(ends[s][0] & alone(s, half))
            def _():
                lone(half)

            @pl.when(ends[s][0] & jnp.logical_not(alone(s, half)))
            def _():
                full(half)

    def grad_row_copy(h, s, half):
        moved = crossed[s] & sides[half][0]
        col = jnp.where(moved, iw + (2 * half - 1), iw)
        to = jnp.where(moved, 1 - half, half)
        return remote(
            g3s.at[h, s, half], g3r.at[h, 1 - s, to], ss3.at[h, s, half], rs3.at[h, 1 - s, to], (ia + (2 * s - 1), col)
        )

    def col_relay_in(h, s):
        return remote(pack.at[h, :, 2 * s : 2 * s + 2], r1.at[h], ss1.at[h, s], ri1.at[h], (ia, iw + 2 * out))

    def col_relay_out(h):
        dst = kall.at[h, :, pl.ds(6 - 6 * parity, 2), 1:4]
        return remote(r1.at[h], dst, ro1.at[h], rs1.at[h, 1 - parity], (ia, iw - out))

    def grad_relay_in(h, s):
        return remote(g4s.at[h, s], r4.at[h], ss4.at[h, s], ri4.at[h], (ia, iw + 2 * out))

    def grad_relay_out(h):
        return remote(r4.at[h], g4r.at[h, 1 - parity], ro4.at[h], rs4.at[h, 1 - parity], (ia, iw - out))

    def grad_col_copy(h, s, dev):
        return remote(g4s.at[h, s], g4r.at[h, 1 - s], ss4.at[h, s], rs4.at[h, 1 - s], dev)

    def send(direct, by_relay, relayed, h):
        for s, (there, dev) in enumerate(sides):
            through = (parity == s) & relayed(h, shared)

            @pl.when(there & through)
            def _():
                by_relay(h, s).start()

            @pl.when(there & jnp.logical_not(through))
            def _():
                direct(h, s, dev).start()

    def relay_col(h):
        @pl.when(relayed_col(h, carried))
        def _():
            remote(r1.at[h], r1.at[h], ro1.at[h], ri1.at[h], (ia, iw - out)).wait_recv()
            col_relay_out(h).start()

    def relay_grad(h):
        @pl.when(relayed_grad(h, carried))
        def _():
            remote(r4.at[h], r4.at[h], ro4.at[h], ri4.at[h], (ia, iw - out)).wait_recv()
            grad_relay_out(h).start()

    def receive(copy, h, group, s):
        there, dev = group[s]

        @pl.when(there)
        def _():
            copy(h, 1 - s, dev).wait_recv()

    def loop(body):
        lax.fori_loop(0, HEADS, lambda h, c: (body(h), c)[1], 0)

    for load in loads:
        load.start()

    barrier = pltpu.get_barrier_semaphore()
    greeted = sides + ends
    for s, row in ((0, ia - 1), (1, ia + 1)):
        greeted += ((crossed[s] & has_l, (row, iw - 1)), (crossed[s] & has_r, (row, iw + 1)))
    greeted += ((iw >= 2, (ia, iw - 2)), (iw < size_w - 2, (ia, iw + 2)))
    for there, dev in greeted:

        @pl.when(there)
        def _():
            pl.semaphore_signal(barrier, inc=1, device_id=dev, device_id_type=MESH)

    def packed_of(i):
        return ((i >> 2) & 1) * 64 + (i >> 5) * 16 + ((i >> 3) & 3) * 4 + (i & 3)

    first = lax.broadcasted_iota(jnp.int32, (128, 128), 0)
    second = lax.broadcasted_iota(jnp.int32, (128, 128), 1)
    perm[...] = jnp.where(packed_of(first) == second, 1.0, 0.0).astype(BF16)
    perm_t[...] = jnp.where(packed_of(second) == first, 1.0, 0.0).astype(BF16)

    for s, (there, _) in enumerate(sides):

        @pl.when(jnp.logical_not(there))
        def _():
            def fill(h):
                kall[h, :, 6 * s : 6 * s + 2] = jnp.zeros((2, 2, 5, 32, D), BF16)
                g4r[h, s] = jnp.zeros((2, 2, 3, 32, D), BF16)

            loop(fill)

    for s, (there, _) in enumerate(ends):

        @pl.when(jnp.logical_not(there))
        def _():
            def fill(h):
                kall[h, :, :, 4 * s] = jnp.zeros((2, 8, 32, D), BF16)

            loop(fill)

    count = sum(there.astype(jnp.int32) for there, _ in greeted)
    pl.semaphore_wait(barrier, count)

    def permute(matrix, x, y):
        z = dot(matrix[...], jnp.concatenate([x, y], axis=1), 1, 0)
        return z[:, :D], z[:, D:]

    loads[0].wait()
    loads[1].wait()

    def send_edges(h):
        for a in range(3):
            x = [own[:, a, :, lanes(h)] for own in (k_own, v_own)]
            kall[h, 0, 2:6, a + 1] = x[0]
            kall[h, 1, 2:6, a + 1] = x[1]
            y = permute(perm_t, x[0].reshape(128, D), x[1].reshape(128, D))
            pack[h, 0, :, a] = y[0].astype(BF16).reshape(4, 32, D)
            pack[h, 1, :, a] = y[1].astype(BF16).reshape(4, 32, D)
        send_rows(h, (1, 2))
        send(col_copy, col_relay_in, relayed_col, h)

    for h in range(3):
        send_edges(h)

    shape = (6, 3, 32, 128)
    unit = lax.broadcasted_iota(jnp.int32, shape, 0)
    drow = lax.broadcasted_iota(jnp.int32, shape, 1) - 1
    token = lax.broadcasted_iota(jnp.int32, shape, 2)
    query = lax.broadcasted_iota(jnp.int32, shape, 3)
    qcol = (query >> 2) & 1
    for a in range(3):
        own_col = (token >> 2) & 1
        if a != 1:
            own_col = jnp.where(drow == a - 1, unit >> 1, own_col)
        kcol = jnp.where(unit < 4, own_col, 3 * qcol - 1)
        dcol = kcol - qcol
        acol = iw * 2 + kcol
        in_cols = (acol >= 0) & (acol < 2 * size_w)

        def of(n):
            return jnp.where(qcol == 0, reach[a, 0, n], reach[a, 1, n])

        arow = ia * 3 + a + drow
        ok = in_cols & (arow >= 0) & (arow < 3 * size_a)
        ok = ok & (drow >= -of(0)) & (drow <= of(1)) & (dcol >= -of(2)) & (dcol <= of(3))
        bias[a] = jnp.where(ok, 0.0, NEGATIVE).astype(F32).reshape(576, 128)

    def forward(h):
        receive(col_copy, h, sides, 0)
        receive(col_copy, h, sides, 1)
        send_rows(h, (0, 3))

    left_query = ((lax.broadcasted_iota(jnp.int32, (128, D), 0) >> 2) & 1) == 0
    none = jnp.zeros((128, D), BF16)

    def attend(h, a):
        def keys(kv, lo, hi):
            return kall[h, kv, lo:hi, a : a + 3].reshape((hi - lo) * 96, D)

        def halo(kv):
            return jnp.concatenate([keys(kv, 0, 2), keys(kv, 6, 8)], axis=1)

        def by_side(x):
            return jnp.concatenate([jnp.where(left_query, x, none), jnp.where(left_query, none, x)], axis=1)

        def own_side(x):
            return jnp.where(left_query, x[:, :D], x[:, D:])

        k_mid, v_mid, k_halo, v_halo = keys(0, 2, 6), keys(1, 2, 6), halo(0), halo(1)
        q = q_own[:, a, :, lanes(h)].reshape(128, D)
        g = g_own[:, a, :, lanes(h)].reshape(128, D)
        both = jnp.concatenate([jnp.concatenate([q, none], axis=1), jnp.concatenate([none, g], axis=1)], axis=0)
        q_side, g_side = by_side(q), by_side(g)
        mid = dot(jnp.concatenate([k_mid, v_mid], axis=1), both, 1, 1)
        s = jnp.concatenate([mid[:, :128], dot(k_halo, q_side, 1, 1)], axis=0)
        dp = jnp.concatenate([mid[:, 128:], dot(v_halo, g_side, 1, 1)], axis=0)
        s = s * (SCALE * LOG2E) + bias[a]
        p = jnp.exp2(s - jnp.max(s, axis=0, keepdims=True))
        p = p * (1.0 / jnp.sum(p, axis=0, keepdims=True))
        low = p.astype(BF16)
        t = p * dp
        ds = (t - p * jnp.sum(t, axis=0, keepdims=True)).astype(BF16)
        o = dot(low[:384], v_mid, 0, 0) + own_side(dot(low[384:], v_halo, 0, 0))
        dq = dot(ds[:384], k_mid, 0, 0) + own_side(dot(ds[384:], k_halo, 0, 0))
        o_out[:, a, :, lanes(h)] = o.astype(BF16).reshape(4, 32, D)
        dq_out[:, a, :, lanes(h)] = (dq * SCALE).astype(BF16).reshape(4, 32, D)
        mid = dot(jnp.concatenate([ds[:384], low[:384]], axis=1), both, 1, 0)
        sums = ((mid[:, :D], dot(ds[384:], q_side, 1, 0)), (mid[:, D:], dot(low[384:], g_side, 1, 0)))
        for kv, (own, beside) in enumerate(sums):
            own = own.reshape(4, 3, 32, D)
            two = (beside[:, :D].reshape(2, 3, 32, D), beside[:, D:].reshape(2, 3, 32, D))
            for i in range(3):
                row = a + i - 1
                if row in (-1, 3):
                    end = 0 if row < 0 else 1
                    g3s[h, end, 0, kv, 0:2] = two[0][:, i].astype(BF16)
                    g3s[h, end, 0, kv, 2:4] = own[0:2, i].astype(BF16)
                    g3s[h, end, 1, kv, 0:2] = own[2:4, i].astype(BF16)
                    g3s[h, end, 1, kv, 2:4] = two[1][:, i].astype(BF16)
                elif row > a or a == 0:
                    acc[h, kv, 0:2, row] = two[0][:, i]
                    acc[h, kv, 2:6, row] = own[:, i]
                    acc[h, kv, 6:8, row] = two[1][:, i]
                else:
                    acc[h, kv, 0:2, row] += two[0][:, i]
                    acc[h, kv, 2:6, row] += own[:, i]
                    acc[h, kv, 6:8, row] += two[1][:, i]

    def send_grad_rows(h, s):
        for_grad_rows(s, lambda half: lone_row_copy(h, s, half).start(), lambda half: grad_row_copy(h, s, half).start())

    def reduce_rows(h):
        for s in range(2):
            row = 2 * s

            def arrived(half, ref):
                remote(ref, ref, ss3.at[h, s, half], rs3.at[h, s, half], ends[s][1]).wait_recv()

            for_grad_rows(
                s,
                lambda half: arrived(half, part_of(g3r.at[h, s, half], half)),
                lambda half: arrived(half, g3r.at[h, s, half]),
            )
            for half, (there, _) in enumerate(sides):

                @pl.when(ends[s][0] & there)
                def _():
                    units = slice(6 * half, 6 * half + 2)
                    acc[h, :, units, row] += g3r[h, s, half, :, 2 * half : 2 * half + 2].astype(F32)

            @pl.when(ends[s][0])
            def _():
                x = [jnp.concatenate([g3r[h, s, 0, kv, 2:4], g3r[h, s, 1, kv, 0:2]]).reshape(128, D) for kv in range(2)]
                for kv, y in enumerate(permute(perm, x[0], x[1])):
                    acc[h, kv, 2:6, row] += y.reshape(4, 32, D)

        for s in range(2):
            g4s[h, s] = acc[h, :, 6 * s : 6 * s + 2].astype(BF16)
        send(grad_col_copy, grad_relay_in, relayed_grad, h)

    def finish(h):
        for s in range(2):
            receive(grad_col_copy, h, sides, s)
        for a in range(3):
            x = [g4r[h, :, kv, :, a].reshape(128, D) for kv in range(2)]
            y = permute(perm, x[0], x[1])
            dk = (y[0].reshape(4, 32, D) + acc[h, 0, 2:6, a]) * SCALE
            dv = y[1].reshape(4, 32, D) + acc[h, 1, 2:6, a]
            dk_out[:, a, :, lanes(h)] = dk.astype(BF16)
            dv_out[:, a, :, lanes(h)] = dv.astype(BF16)

    for h in range(RELAY_AHEAD):
        relay_col(h)
        if h < CORNERS_AHEAD:
            forward(h)
        if h + 3 < AHEAD:
            send_edges(h + 3)

    loads[2].wait()
    loads[3].wait()

    def step(h):
        @pl.when(h + CORNERS_AHEAD < HEADS)
        def _():
            forward(h + CORNERS_AHEAD)

        @pl.when(h + RELAY_AHEAD < HEADS)
        def _():
            relay_col(h + RELAY_AHEAD)

        @pl.when(h + AHEAD < HEADS)
        def _():
            send_edges(h + AHEAD)

        for a in range(3):
            if a != 1:
                for j in range(4):
                    receive_row(h, a // 2, j)
            attend(h, a)
            if a != 1:
                send_grad_rows(h, a // 2)

        @pl.when(h >= ROWS_BEHIND)
        def _():
            reduce_rows(h - ROWS_BEHIND)

        @pl.when(h >= RELAY_BEHIND)
        def _():
            relay_grad(h - RELAY_BEHIND)

        @pl.when(h >= BEHIND)
        def _():
            finish(h - BEHIND)

    loop(step)
    for h in range(HEADS - ROWS_BEHIND, HEADS):
        reduce_rows(h)

    for h in range(HEADS - RELAY_BEHIND, HEADS):
        relay_grad(h)
    for h in range(HEADS - BEHIND, HEADS):
        finish(h)

    def drain(h):
        @pl.when(relayed_col(h, carried))
        def _():
            col_relay_out(h).wait_send()

        @pl.when(relayed_grad(h, carried))
        def _():
            grad_relay_out(h).wait_send()

        for copy in (col_copy, grad_col_copy):
            for s, (there, dev) in enumerate(sides):

                @pl.when(there)
                def _():
                    copy(h, s, dev).wait_send()

        for s in range(2):
            for j in range(4):

                @pl.when(row_there(s, j))
                def _():
                    row_copy(h, s, j).wait_send()

            for_grad_rows(
                s, lambda half: lone_row_copy(h, s, half).wait_send(), lambda half: grad_row_copy(h, s, half).wait_send()
            )

    loop(drain)


def write_out(*refs):
    sources, outs, sem = refs[:4], refs[4:8], refs[8]
    copies = [pltpu.make_async_copy(x.at[f], y.at[f], sem.at[n, f]) for n, (x, y) in enumerate(zip(sources, outs)) for f in range(4)]
    for copy in copies:
        copy.start()
    for copy in copies:
        copy.wait()


def per_device(size_a, size_w, queries, key_heads, value_heads, out_grad, reach_tiles):
    shape = queries.shape
    ins = [x.reshape(4, 3, 32, HEADS * D) for x in (queries, key_heads, value_heads, out_grad)]
    ins = [pltpu.with_memory_space_constraint(x, pltpu.HBM) for x in ins]
    any_spec = pl.BlockSpec(memory_space=pl.ANY)
    pair = pltpu.SemaphoreType.DMA((HEADS, 2))
    results = pl.pallas_call(
        functools.partial(kernel, size_a, size_w),
        out_shape=[pltpu.VMEM((4, 3, 32, HEADS * D), BF16)] * 4,
        in_specs=[pl.BlockSpec(memory_space=pltpu.SMEM)] + [any_spec] * 4,
        out_specs=[pl.BlockSpec(memory_space=pltpu.VMEM)] * 4,
        scratch_shapes=[
            pltpu.VMEM((HEADS, 2, 8, 5, 32, D), BF16),
            pltpu.VMEM((4, 3, 32, HEADS * D), BF16),
            pltpu.VMEM((4, 3, 32, HEADS * D), BF16),
            pltpu.VMEM((4, 3, 32, HEADS * D), BF16),
            pltpu.VMEM((4, 3, 32, HEADS * D), BF16),
            pltpu.VMEM((HEADS, 2, 4, 3, 32, D), BF16),
            pltpu.VMEM((HEADS, 2, 8, 3, 32, D), F32),
            pltpu.VMEM((HEADS, 2, 2, 2, 4, 32, D), BF16),
            pltpu.VMEM((HEADS, 2, 2, 2, 4, 32, D), BF16),
            pltpu.VMEM((HEADS, 2, 2, 2, 3, 32, D), BF16),
            pltpu.VMEM((HEADS, 2, 2, 2, 3, 32, D), BF16),
            pltpu.VMEM((HEADS, 2, 2, 3, 32, D), BF16),
            pltpu.VMEM((HEADS, 2, 2, 3, 32, D), BF16),
            pltpu.VMEM((3, 576, 128), F32),
            pltpu.VMEM((128, 128), BF16),
            pltpu.VMEM((128, 128), BF16),
            pltpu.SemaphoreType.DMA((4,)),
        ]
        + [pair] * 2
        + [pltpu.SemaphoreType.DMA((HEADS, 2, 4))] * 2
        + [pltpu.SemaphoreType.DMA((HEADS, 2, 2))] * 2
        + [pair] * 2
        + [pltpu.SemaphoreType.DMA((HEADS,))] * 4,
        compiler_params=pltpu.CompilerParams(
            collective_id=0, has_side_effects=True, vmem_limit_bytes=56 * 1024 * 1024
        ),
    )(reach_tiles, *ins)
    outs = pl.pallas_call(
        write_out,
        out_shape=[jax.ShapeDtypeStruct((4, 3, 32, HEADS * D), BF16)] * 4,
        in_specs=[pl.BlockSpec(memory_space=pltpu.VMEM)] * 4,
        out_specs=[any_spec] * 4,
        scratch_shapes=[pltpu.SemaphoreType.DMA((4, 4))],
        compiler_params=pltpu.CompilerParams(vmem_limit_bytes=8 * 1024 * 1024),
    )(*(pltpu.with_memory_space_constraint(x, pltpu.VMEM) for x in results))
    return tuple(x.reshape(shape) for x in outs)


def solution(mesh):
    spec = P(None, "ha", "wa", None)
    return jax.shard_map(
        functools.partial(per_device, mesh.shape["ha"], mesh.shape["wa"]),
        mesh=mesh,
        in_specs=(spec, spec, spec, spec, P("ha", "wa", None)),
        out_specs=(spec, spec, spec, spec),
        check_vma=False,
    )
```

```python
import functools
import math

import jax
import jax.numpy as jnp
from jax import lax
from jax.experimental import pallas as pl
from jax.experimental.pallas import tpu as pltpu
from jax.sharding import PartitionSpec as P

HEADS = 12
TS = 4
D = 128
MESH = pl.DeviceIdType.MESH
AHEAD = 9
RELAY_AHEAD = 6
CORNERS_AHEAD = 3
ROWS_BEHIND = 3
RELAY_BEHIND = 6
BEHIND = 9
NEGATIVE = -1e30
SCALE = 1.0 / math.sqrt(D)
LOG2E = 1.4426950408889634

F32 = jnp.float32
BF16 = jnp.bfloat16


def dot(a, b, ca, cb):
    return lax.dot_general(a, b, (((ca,), (cb,)), ((), ())), preferred_element_type=F32)


def kernel(
    size_a, size_w, reach, q_in, k_in, v_in, g_in, o_out, dq_out, dk_out, dv_out,
    kall, k_own, v_own, q_own, g_own, pack, acc, g3s, g3r, g4s, g4r, r1, r4, bias, perm, perm_t,
    in_sem, ss1, rs1, ss2, rs2, ss3, rs3, ss4, rs4, ri1, ro1, ri4, ro4,
):
    half_a = size_a // 2
    ia = lax.axis_index("ha")
    iw = lax.axis_index("wa")
    has_u, has_d = ia > 0, ia < size_a - 1
    has_l, has_r = iw > 0, iw < size_w - 1
    up, down = (ia - 1, iw), (ia + 1, iw)
    left, right = (ia, iw - 1), (ia, iw + 1)
    sides = ((has_l, left), (has_r, right))
    ends = ((has_u, up), (has_d, down))
    crossed = (ia == half_a, ia == half_a - 1)

    parity, ring, rings = iw % 2, iw // 2, size_w // 2
    out = 2 * parity - 1
    shared = jnp.where(parity == 1, ring + 1, rings - ring)
    carried = jnp.where(parity == 1, ring, rings - 1 - ring)
    middle = (ia >= half_a - 2) & (ia < half_a + 2)

    def chosen(k, part, fewer):
        n = part * HEADS // rings - jnp.where(middle & (part > 0), fewer, 0)
        return (k * n) % HEADS >= HEADS - n

    def relayed_col(h, part):
        return chosen(h, part, jnp.where(part >= 2, 1, 0))

    def relayed_grad(h, part):
        return chosen(HEADS - 1 - h, part, jnp.where(part >= 3, 2, 1))

    def lanes(h):
        return pl.ds(pl.multiple_of(h * D, D), D)

    loads = [
        pltpu.make_async_copy(src, dst, in_sem.at[n])
        for n, (src, dst) in enumerate(((k_in, k_own), (v_in, v_own), (q_in, q_own), (g_in, g_own)))
    ]

    def remote(src, dst, ss, rs, dev):
        return pltpu.make_async_remote_copy(
            src_ref=src, dst_ref=dst, send_sem=ss, recv_sem=rs, device_id=dev, device_id_type=MESH
        )

    def col_copy(h, s, dev):
        lo = 6 - 6 * s
        return remote(
            pack.at[h, :, 2 * s : 2 * s + 2], kall.at[h, :, lo : lo + 2, 1:4], ss1.at[h, s], rs1.at[h, 1 - s], dev
        )

    def row_place(s, j):
        moved = crossed[s] & sides[j // 2][0]
        col = jnp.where(moved, iw + (2 * (j // 2) - 1), iw)
        return jnp.where(moved, (j + 2) % 4, j), (ia + (2 * s - 1), col)

    def row_there(s, j):
        return ends[s][0] if j in (1, 2) else ends[s][0] & sides[j // 2][0]

    def row_copy(h, s, j):
        slot, dev = row_place(s, j)
        src = pack.at[h, :, 2 * j - 2 : 2 * j, 2 * s] if j in (1, 2) else kall.at[h, :, 2 * j : 2 * j + 2, 1 + 2 * s]
        dst = kall.at[h, :, pl.ds(2 * slot, 2), 4 - 4 * s]
        return remote(src, dst, ss2.at[h, s, j], rs2.at[h, 1 - s, slot], dev)

    def send_rows(h, columns):
        for s in range(2):
            for j in columns:

                @pl.when(row_there(s, j))
                def _():
                    row_copy(h, s, j).start()

    def receive_row(h, s, j):
        @pl.when(row_there(s, j))
        def _():
            ref = kall.at[h, :, 2 * j : 2 * j + 2, 4 * s]
            remote(ref, ref, ss2.at[h, s, j], rs2.at[h, s, j], ends[s][1]).wait_recv()

    def alone(s, half):
        return crossed[s] & jnp.logical_not(sides[half][0])

    def part_of(ref, half):
        return ref.at[:, 2 - 2 * half : 4 - 2 * half]

    def lone_row_copy(h, s, half):
        return remote(
            part_of(g3s.at[h, s, half], half), part_of(g3r.at[h, 1 - s, half], half),
            ss3.at[h, s, half], rs3.at[h, 1 - s, half], ends[s][1],
        )

    def for_grad_rows(s, lone, full):
        for half in range(2):

            @pl.when(ends[s][0] & alone(s, half))
            def _():
                lone(half)

            @pl.when(ends[s][0] & jnp.logical_not(alone(s, half)))
            def _():
                full(half)

    def grad_row_copy(h, s, half):
        moved = crossed[s] & sides[half][0]
        col = jnp.where(moved, iw + (2 * half - 1), iw)
        to = jnp.where(moved, 1 - half, half)
        return remote(
            g3s.at[h, s, half], g3r.at[h, 1 - s, to], ss3.at[h, s, half], rs3.at[h, 1 - s, to], (ia + (2 * s - 1), col)
        )

    def col_relay_in(h, s):
        return remote(pack.at[h, :, 2 * s : 2 * s + 2], r1.at[h], ss1.at[h, s], ri1.at[h], (ia, iw + 2 * out))

    def col_relay_out(h):
        dst = kall.at[h, :, pl.ds(6 - 6 * parity, 2), 1:4]
        return remote(r1.at[h], dst, ro1.at[h], rs1.at[h, 1 - parity], (ia, iw - out))

    def grad_relay_in(h, s):
        return remote(g4s.at[h, s], r4.at[h], ss4.at[h, s], ri4.at[h], (ia, iw + 2 * out))

    def grad_relay_out(h):
        return remote(r4.at[h], g4r.at[h, 1 - parity], ro4.at[h], rs4.at[h, 1 - parity], (ia, iw - out))

    def grad_col_copy(h, s, dev):
        return remote(g4s.at[h, s], g4r.at[h, 1 - s], ss4.at[h, s], rs4.at[h, 1 - s], dev)

    def send(direct, by_relay, relayed, h):
        for s, (there, dev) in enumerate(sides):
            through = (parity == s) & relayed(h, shared)

            @pl.when(there & through)
            def _():
                by_relay(h, s).start()

            @pl.when(there & jnp.logical_not(through))
            def _():
                direct(h, s, dev).start()

    def relay_col(h):
        @pl.when(relayed_col(h, carried))
        def _():
            remote(r1.at[h], r1.at[h], ro1.at[h], ri1.at[h], (ia, iw - out)).wait_recv()
            col_relay_out(h).start()

    def relay_grad(h):
        @pl.when(relayed_grad(h, carried))
        def _():
            remote(r4.at[h], r4.at[h], ro4.at[h], ri4.at[h], (ia, iw - out)).wait_recv()
            grad_relay_out(h).start()

    def receive(copy, h, group, s):
        there, dev = group[s]

        @pl.when(there)
        def _():
            copy(h, 1 - s, dev).wait_recv()

    def loop(body):
        lax.fori_loop(0, HEADS, lambda h, c: (body(h), c)[1], 0)

    for load in loads:
        load.start()

    barrier = pltpu.get_barrier_semaphore()
    greeted = sides + ends
    for s, row in ((0, ia - 1), (1, ia + 1)):
        greeted += ((crossed[s] & has_l, (row, iw - 1)), (crossed[s] & has_r, (row, iw + 1)))
    greeted += ((iw >= 2, (ia, iw - 2)), (iw < size_w - 2, (ia, iw + 2)))
    for there, dev in greeted:

        @pl.when(there)
        def _():
            pl.semaphore_signal(barrier, inc=1, device_id=dev, device_id_type=MESH)

    def packed_of(i):
        return ((i >> 2) & 1) * 64 + (i >> 5) * 16 + ((i >> 3) & 3) * 4 + (i & 3)

    first = lax.broadcasted_iota(jnp.int32, (128, 128), 0)
    second = lax.broadcasted_iota(jnp.int32, (128, 128), 1)
    perm[...] = jnp.where(packed_of(first) == second, 1.0, 0.0).astype(BF16)
    perm_t[...] = jnp.where(packed_of(second) == first, 1.0, 0.0).astype(BF16)

    for s, (there, _) in enumerate(sides):

        @pl.when(jnp.logical_not(there))
        def _():
            def fill(h):
                kall[h, :, 6 * s : 6 * s + 2] = jnp.zeros((2, 2, 5, 32, D), BF16)
                g4r[h, s] = jnp.zeros((2, 2, 3, 32, D), BF16)

            loop(fill)

    for s, (there, _) in enumerate(ends):

        @pl.when(jnp.logical_not(there))
        def _():
            def fill(h):
                kall[h, :, :, 4 * s] = jnp.zeros((2, 8, 32, D), BF16)

            loop(fill)

    count = sum(there.astype(jnp.int32) for there, _ in greeted)
    pl.semaphore_wait(barrier, count)

    def permute(matrix, x, y):
        z = dot(matrix[...], jnp.concatenate([x, y], axis=1), 1, 0)
        return z[:, :D], z[:, D:]

    loads[0].wait()
    loads[1].wait()

    def send_edges(h):
        for a in range(3):
            x = [own[:, a, :, lanes(h)] for own in (k_own, v_own)]
            kall[h, 0, 2:6, a + 1] = x[0]
            kall[h, 1, 2:6, a + 1] = x[1]
            y = permute(perm_t, x[0].reshape(128, D), x[1].reshape(128, D))
            pack[h, 0, :, a] = y[0].astype(BF16).reshape(4, 32, D)
            pack[h, 1, :, a] = y[1].astype(BF16).reshape(4, 32, D)
        send_rows(h, (1, 2))
        send(col_copy, col_relay_in, relayed_col, h)

    for h in range(3):
        send_edges(h)

    shape = (6, 3, 32, 128)
    unit = lax.broadcasted_iota(jnp.int32, shape, 0)
    drow = lax.broadcasted_iota(jnp.int32, shape, 1) - 1
    token = lax.broadcasted_iota(jnp.int32, shape, 2)
    query = lax.broadcasted_iota(jnp.int32, shape, 3)
    qcol = (query >> 2) & 1
    for a in range(3):
        own_col = (token >> 2) & 1
        if a != 1:
            own_col = jnp.where(drow == a - 1, unit >> 1, own_col)
        kcol = jnp.where(unit < 4, own_col, 3 * qcol - 1)
        dcol = kcol - qcol
        acol = iw * 2 + kcol
        in_cols = (acol >= 0) & (acol < 2 * size_w)

        def of(n):
            return jnp.where(qcol == 0, reach[a, 0, n], reach[a, 1, n])

        arow = ia * 3 + a + drow
        ok = in_cols & (arow >= 0) & (arow < 3 * size_a)
        ok = ok & (drow >= -of(0)) & (drow <= of(1)) & (dcol >= -of(2)) & (dcol <= of(3))
        bias[a] = jnp.where(ok, 0.0, NEGATIVE).astype(F32).reshape(576, 128)

    def forward(h):
        receive(col_copy, h, sides, 0)
        receive(col_copy, h, sides, 1)
        send_rows(h, (0, 3))

    left_query = ((lax.broadcasted_iota(jnp.int32, (128, D), 0) >> 2) & 1) == 0
    none = jnp.zeros((128, D), BF16)

    def attend(h, a):
        def keys(kv, lo, hi):
            return kall[h, kv, lo:hi, a : a + 3].reshape((hi - lo) * 96, D)

        def halo(kv):
            return jnp.concatenate([keys(kv, 0, 2), keys(kv, 6, 8)], axis=1)

        def by_side(x):
            return jnp.concatenate([jnp.where(left_query, x, none), jnp.where(left_query, none, x)], axis=1)

        def own_side(x):
            return jnp.where(left_query, x[:, :D], x[:, D:])

        k_mid, v_mid, k_halo, v_halo = keys(0, 2, 6), keys(1, 2, 6), halo(0), halo(1)
        q = q_own[:, a, :, lanes(h)].reshape(128, D)
        g = g_own[:, a, :, lanes(h)].reshape(128, D)
        both = jnp.concatenate([jnp.concatenate([q, none], axis=1), jnp.concatenate([none, g], axis=1)], axis=0)
        q_side, g_side = by_side(q), by_side(g)
        mid = dot(jnp.concatenate([k_mid, v_mid], axis=1), both, 1, 1)
        s = jnp.concatenate([mid[:, :128], dot(k_halo, q_side, 1, 1)], axis=0)
        dp = jnp.concatenate([mid[:, 128:], dot(v_halo, g_side, 1, 1)], axis=0)
        s = s * (SCALE * LOG2E) + bias[a]
        p = jnp.exp2(s - jnp.max(s, axis=0, keepdims=True))
        p = p * (1.0 / jnp.sum(p, axis=0, keepdims=True))
        low = p.astype(BF16)
        t = p * dp
        ds = (t - p * jnp.sum(t, axis=0, keepdims=True)).astype(BF16)
        o = dot(low[:384], v_mid, 0, 0) + own_side(dot(low[384:], v_halo, 0, 0))
        dq = dot(ds[:384], k_mid, 0, 0) + own_side(dot(ds[384:], k_halo, 0, 0))
        o_out[:, a, :, lanes(h)] = o.astype(BF16).reshape(4, 32, D)
        dq_out[:, a, :, lanes(h)] = (dq * SCALE).astype(BF16).reshape(4, 32, D)
        mid = dot(jnp.concatenate([ds[:384], low[:384]], axis=1), both, 1, 0)
        sums = ((mid[:, :D], dot(ds[384:], q_side, 1, 0)), (mid[:, D:], dot(low[384:], g_side, 1, 0)))
        for kv, (own, beside) in enumerate(sums):
            own = own.reshape(4, 3, 32, D)
            two = (beside[:, :D].reshape(2, 3, 32, D), beside[:, D:].reshape(2, 3, 32, D))
            for i in range(3):
                row = a + i - 1
                if row in (-1, 3):
                    end = 0 if row < 0 else 1
                    g3s[h, end, 0, kv, 0:2] = two[0][:, i].astype(BF16)
                    g3s[h, end, 0, kv, 2:4] = own[0:2, i].astype(BF16)
                    g3s[h, end, 1, kv, 0:2] = own[2:4, i].astype(BF16)
                    g3s[h, end, 1, kv, 2:4] = two[1][:, i].astype(BF16)
                elif row > a or a == 0:
                    acc[h, kv, 0:2, row] = two[0][:, i]
                    acc[h, kv, 2:6, row] = own[:, i]
                    acc[h, kv, 6:8, row] = two[1][:, i]
                else:
                    acc[h, kv, 0:2, row] += two[0][:, i]
                    acc[h, kv, 2:6, row] += own[:, i]
                    acc[h, kv, 6:8, row] += two[1][:, i]

    def send_grad_rows(h, s):
        for_grad_rows(s, lambda half: lone_row_copy(h, s, half).start(), lambda half: grad_row_copy(h, s, half).start())

    def reduce_rows(h):
        for s in range(2):
            row = 2 * s

            def arrived(half, ref):
                remote(ref, ref, ss3.at[h, s, half], rs3.at[h, s, half], ends[s][1]).wait_recv()

            for_grad_rows(
                s,
                lambda half: arrived(half, part_of(g3r.at[h, s, half], half)),
                lambda half: arrived(half, g3r.at[h, s, half]),
            )
            for half, (there, _) in enumerate(sides):

                @pl.when(ends[s][0] & there)
                def _():
                    units = slice(6 * half, 6 * half + 2)
                    acc[h, :, units, row] += g3r[h, s, half, :, 2 * half : 2 * half + 2].astype(F32)

            @pl.when(ends[s][0])
            def _():
                x = [jnp.concatenate([g3r[h, s, 0, kv, 2:4], g3r[h, s, 1, kv, 0:2]]).reshape(128, D) for kv in range(2)]
                for kv, y in enumerate(permute(perm, x[0], x[1])):
                    acc[h, kv, 2:6, row] += y.reshape(4, 32, D)

        for s in range(2):
            g4s[h, s] = acc[h, :, 6 * s : 6 * s + 2].astype(BF16)
        send(grad_col_copy, grad_relay_in, relayed_grad, h)

    def finish(h):
        for s in range(2):
            receive(grad_col_copy, h, sides, s)
        for a in range(3):
            x = [g4r[h, :, kv, :, a].reshape(128, D) for kv in range(2)]
            y = permute(perm, x[0], x[1])
            dk = (y[0].reshape(4, 32, D) + acc[h, 0, 2:6, a]) * SCALE
            dv = y[1].reshape(4, 32, D) + acc[h, 1, 2:6, a]
            dk_out[:, a, :, lanes(h)] = dk.astype(BF16)
            dv_out[:, a, :, lanes(h)] = dv.astype(BF16)

    for h in range(RELAY_AHEAD):
        relay_col(h)
        if h < CORNERS_AHEAD:
            forward(h)
        if h + 3 < AHEAD:
            send_edges(h + 3)

    loads[2].wait()
    loads[3].wait()

    def step(h):
        @pl.when(h + CORNERS_AHEAD < HEADS)
        def _():
            forward(h + CORNERS_AHEAD)

        @pl.when(h + RELAY_AHEAD < HEADS)
        def _():
            relay_col(h + RELAY_AHEAD)

        @pl.when(h + AHEAD < HEADS)
        def _():
            send_edges(h + AHEAD)

        for a in range(3):
            if a != 1:
                for j in range(4):
                    receive_row(h, a // 2, j)
            attend(h, a)
            if a != 1:
                send_grad_rows(h, a // 2)

        @pl.when(h >= ROWS_BEHIND)
        def _():
            reduce_rows(h - ROWS_BEHIND)

        @pl.when(h >= RELAY_BEHIND)
        def _():
            relay_grad(h - RELAY_BEHIND)

        @pl.when(h >= BEHIND)
        def _():
            finish(h - BEHIND)

    loop(step)
    for h in range(HEADS - ROWS_BEHIND, HEADS):
        reduce_rows(h)

    for h in range(HEADS - RELAY_BEHIND, HEADS):
        relay_grad(h)
    for h in range(HEADS - BEHIND, HEADS):
        finish(h)

    def drain(h):
        @pl.when(relayed_col(h, carried))
        def _():
            col_relay_out(h).wait_send()

        @pl.when(relayed_grad(h, carried))
        def _():
            grad_relay_out(h).wait_send()

        for copy in (col_copy, grad_col_copy):
            for s, (there, dev) in enumerate(sides):

                @pl.when(there)
                def _():
                    copy(h, s, dev).wait_send()

        for s in range(2):
            for j in range(4):

                @pl.when(row_there(s, j))
                def _():
                    row_copy(h, s, j).wait_send()

            for_grad_rows(
                s, lambda half: lone_row_copy(h, s, half).wait_send(), lambda half: grad_row_copy(h, s, half).wait_send()
            )

    loop(drain)


def write_out(*refs):
    sources, outs, sem = refs[:4], refs[4:8], refs[8]
    copies = [pltpu.make_async_copy(x, y, sem.at[n]) for n, (x, y) in enumerate(zip(sources, outs))]
    for copy in copies:
        copy.start()
    for copy in copies:
        copy.wait()


def per_device(size_a, size_w, queries, key_heads, value_heads, out_grad, reach_tiles):
    shape = queries.shape
    ins = [x.reshape(4, 3, 32, HEADS * D) for x in (queries, key_heads, value_heads, out_grad)]
    ins = [pltpu.with_memory_space_constraint(x, pltpu.HBM) for x in ins]
    any_spec = pl.BlockSpec(memory_space=pl.ANY)
    pair = pltpu.SemaphoreType.DMA((HEADS, 2))
    results = pl.pallas_call(
        functools.partial(kernel, size_a, size_w),
        out_shape=[pltpu.VMEM((4, 3, 32, HEADS * D), BF16)] * 4,
        in_specs=[pl.BlockSpec(memory_space=pltpu.SMEM)] + [any_spec] * 4,
        out_specs=[pl.BlockSpec(memory_space=pltpu.VMEM)] * 4,
        scratch_shapes=[
            pltpu.VMEM((HEADS, 2, 8, 5, 32, D), BF16),
            pltpu.VMEM((4, 3, 32, HEADS * D), BF16),
            pltpu.VMEM((4, 3, 32, HEADS * D), BF16),
            pltpu.VMEM((4, 3, 32, HEADS * D), BF16),
            pltpu.VMEM((4, 3, 32, HEADS * D), BF16),
            pltpu.VMEM((HEADS, 2, 4, 3, 32, D), BF16),
            pltpu.VMEM((HEADS, 2, 8, 3, 32, D), F32),
            pltpu.VMEM((HEADS, 2, 2, 2, 4, 32, D), BF16),
            pltpu.VMEM((HEADS, 2, 2, 2, 4, 32, D), BF16),
            pltpu.VMEM((HEADS, 2, 2, 2, 3, 32, D), BF16),
            pltpu.VMEM((HEADS, 2, 2, 2, 3, 32, D), BF16),
            pltpu.VMEM((HEADS, 2, 2, 3, 32, D), BF16),
            pltpu.VMEM((HEADS, 2, 2, 3, 32, D), BF16),
            pltpu.VMEM((3, 576, 128), F32),
            pltpu.VMEM((128, 128), BF16),
            pltpu.VMEM((128, 128), BF16),
            pltpu.SemaphoreType.DMA((4,)),
        ]
        + [pair] * 2
        + [pltpu.SemaphoreType.DMA((HEADS, 2, 4))] * 2
        + [pltpu.SemaphoreType.DMA((HEADS, 2, 2))] * 2
        + [pair] * 2
        + [pltpu.SemaphoreType.DMA((HEADS,))] * 4,
        compiler_params=pltpu.CompilerParams(
            collective_id=0, has_side_effects=True, vmem_limit_bytes=56 * 1024 * 1024
        ),
    )(reach_tiles, *ins)
    outs = pl.pallas_call(
        write_out,
        out_shape=[jax.ShapeDtypeStruct((4, 3, 32, HEADS * D), BF16)] * 4,
        in_specs=[pl.BlockSpec(memory_space=pltpu.VMEM)] * 4,
        out_specs=[any_spec] * 4,
        scratch_shapes=[pltpu.SemaphoreType.DMA((4,))],
        compiler_params=pltpu.CompilerParams(vmem_limit_bytes=8 * 1024 * 1024),
    )(*(pltpu.with_memory_space_constraint(x, pltpu.VMEM) for x in results))
    return tuple(x.reshape(shape) for x in outs)


def solution(mesh):
    spec = P(None, "ha", "wa", None)
    return jax.shard_map(
        functools.partial(per_device, mesh.shape["ha"], mesh.shape["wa"]),
        mesh=mesh,
        in_specs=(spec, spec, spec, spec, P("ha", "wa", None)),
        out_specs=(spec, spec, spec, spec),
        check_vma=False,
    )
```
